32 devices in a mesh: row: 4 (over x, core), col: 4 (over z), mom: 2 (over y).
Axes of the slice: x: 2, y: 2, z: 4, core: 2. Of those that a mesh axis runs over, the one named last changes fastest.
Arguments:
- lesser: bfloat16 [4, 2, 1536, 1536], P('mom', None, 'row', 'col'), may hold values from -8 to 8
- greater: bfloat16 [4, 2, 1536, 1536], P('mom', None, 'col', 'row'), may hold values from -8 to 8
- triples: int32 [4, 8, 3], replicated, may hold values from 0 to 3
- diag_inverse: bfloat16 [4, 2, 1536, 384], P('mom', None, 'row'), may hold values from -0.21875 to 0.21875
- right_side: bfloat16 [4, 1536, 2, 1536], P('mom', 'row', None, 'col'), may hold values from -6 to 6
Outputs:
- sigma: bfloat16 [4, 2, 1536, 1536], P('mom', None, 'row', 'col')
- solution: bfloat16 [4, 1536, 2, 1536], P('mom', 'row', None, 'col')
The draws below stay inside these ranges and needn't reach their ends.
Inputs may be any that keep to these rules, and one draw needn't show every extreme that they name: `triples`: each entry names a momentum point.
All inputs are finite; a program needn't handle non-finite values.
Results may differ from the reference program's by a relative error of at most 0.017.
Values may be sent and summed in bfloat16 or wider, within the bound.
No kernel may reach another device: no remote copies, remote signals or barrier semaphores. Data moves between devices by JAX's collectives and lax.ppermute only.
A program may use at most 128 MiB of HBM per device.

```python
import math
import jax
import jax.numpy as jnp
from jax import lax

PAIRS = 8
K = 4
BO = 384
N = 1536
N_ROW = 4


def place_ends(result, rng, least, top_value):
    shape = result.shape
    index_at = [jax.random.randint(jax.random.fold_in(rng, axis), (), 0, shape[axis]) for axis in range(len(shape))]
    result = result.at[tuple(index_at)].set(least)
    longest = shape.index(max(shape))
    index_at[longest] = (index_at[longest] + 1) % shape[longest]
    return result.at[tuple(index_at)].set(top_value)


def level_of(own_key, extent, cuts, low, high):
    factor_of = 1.0
    for position, parts in cuts:
        draws = jax.random.uniform(jax.random.fold_in(jax.random.fold_in(own_key, 6), position), (parts,), jnp.float32, low / len(cuts), high / len(cuts))
        factor_of = factor_of * jnp.repeat(jnp.exp(draws), extent[position] // parts).reshape((-1,) + (1,) * (len(extent) - 1 - position))
    return factor_of


def gaussian(own_key, extent, spread, bound, pieces=(), held_as=jnp.bfloat16):
    result = spread * jax.random.normal(own_key, extent, jnp.float32)
    if pieces:
        result = result * level_of(own_key, extent, pieces, -0.22, 0.18)
    return jnp.clip(result, -bound, bound).astype(held_as)


def setup_inputs(seed: int = 0) -> dict:
    seeds = jax.random.split(jax.random.key(seed), 6)
    return {
        "lesser": gaussian(seeds[0], (K, 2, N, N), 1.32, 8.0, ((0, 2), (2, 4), (3, 4))),
        "greater": gaussian(seeds[1], (K, 2, N, N), 1.32, 8.0, ((0, 2), (2, 4), (3, 4))),
        "triples": place_ends(jax.random.randint(seeds[2], (K, PAIRS, 3), 0, K), jax.random.fold_in(seeds[2], 1), 0, K - 1).astype(jnp.int32),
        "diag_inverse": gaussian(seeds[3], (K, 2, N, BO), (2 * BO) ** -0.5, 0.21875, ((0, 2), (2, 4))),
        "right_side": gaussian(seeds[4], (K, N, 2, N), 1.0, 6.0, ((0, 2), (1, 4), (3, 4))),
    }


def complex_mul(left_real, left_imag, right_real, right_imag):
    return (left_real * right_real - left_imag * right_imag, left_real * right_imag + left_imag * right_real)

def self_energy(lesser, partner, table_rows):

    def add_term(pair_index, carry):
        sum_real, sum_imag = carry
        first_tile = lax.dynamic_index_in_dim(lesser, table_rows[pair_index, 0], 0, keepdims=False).astype(jnp.float32)
        second_tile = lax.dynamic_index_in_dim(lesser, table_rows[pair_index, 1], 0, keepdims=False).astype(jnp.float32)
        third_tile = lax.dynamic_index_in_dim(partner, table_rows[pair_index, 2], 0, keepdims=False).astype(jnp.float32)
        prod_real, prod_imag = complex_mul(first_tile[0], first_tile[1], second_tile[0], second_tile[1])
        full_real, full_imag = complex_mul(prod_real, prod_imag, third_tile[0], third_tile[1])
        return (sum_real + full_real, sum_imag + full_imag)
    zero_tile = jnp.zeros((N, N), jnp.float32)
    sum_real, sum_imag = lax.fori_loop(0, PAIRS, add_term, (zero_tile, zero_tile))
    return (jnp.stack([sum_real, sum_imag]) * (1.0 / PAIRS)).astype(jnp.bfloat16)

def complex_rows(left_tiles, right_rows):
    left_real = left_tiles[0]
    left_imag = left_tiles[1]
    right_real = right_rows[:, 0, :]
    right_imag = right_rows[:, 1, :]
    out_real = jnp.dot(left_real, right_real, preferred_element_type=jnp.float32) - jnp.dot(left_imag, right_imag, preferred_element_type=jnp.float32)
    out_imag = jnp.dot(left_real, right_imag, preferred_element_type=jnp.float32) + jnp.dot(left_imag, right_real, preferred_element_type=jnp.float32)
    return jnp.stack([out_real, out_imag], axis=1)

def solve_momentum(kernel, inverse, right):
    weight = 1.0 / math.sqrt(N)
    finished = []
    for block in range(N_ROW):
        row_start = block * BO
        row_stop = row_start + BO
        pending = right[row_start:row_stop].astype(jnp.float32)
        if block > 0:
            earlier = jnp.concatenate(finished, axis=0)
            pending = pending + weight * complex_rows(kernel[:, row_start:row_stop, :row_start], earlier)
        rounded = pending.astype(jnp.bfloat16)
        finished.append(complex_rows(inverse[:, row_start:row_stop, :], rounded).astype(jnp.bfloat16))
    return jnp.concatenate(finished, axis=0)

def reference(lesser, greater, triples, diag_inverse, right_side):
    partner = jnp.swapaxes(greater, 2, 3)
    sigma_list = []
    solved_list = []
    for momentum in range(K):
        sigma_one = self_energy(lesser, partner, triples[momentum])
        sigma_list.append(sigma_one)
        solved_list.append(solve_momentum(sigma_one, diag_inverse[momentum], right_side[momentum]))
    return (jnp.stack(sigma_list), jnp.stack(solved_list))
```

```python
import functools
import itertools
import math

import jax
import jax.numpy as jnp
from jax import lax
from jax.experimental import pallas as pl
from jax.experimental.pallas import tpu as pltpu
from jax.sharding import PartitionSpec as P

AXES = ("row", "col", "mom")
VMEM_BYTES = 56 * 1024 * 1024


class Plan:
    def __init__(self, mesh, moments, side):
        self.rows = mesh.shape["row"]
        self.cols = mesh.shape["col"]
        self.moms = mesh.shape["mom"]
        self.moments = moments
        self.side = side
        self.groups = self.rows // moments
        self.half = side // self.moms
        self.part = 2 * self.half // self.groups
        self.dpart = 2 * side // self.groups
        self.width = side // self.groups
        self.tiles = self.rows * (self.rows - 1) // 2

    def tile(self, row, col):
        return row * (row - 1) // 2 + col

    def send(self, value, target):
        pairs = []
        index = lambda r, c, m: (r * self.cols + c) * self.moms + m
        for place in itertools.product(range(self.rows), range(self.cols), range(self.moms)):
            goal = target(*place)
            if goal is not None:
                pairs.append((index(*place), index(*goal)))
        return lax.ppermute(value, AXES, pairs)


def hbm(count):
    return [pl.BlockSpec(memory_space=pl.ANY)] * count


def smem():
    return pl.BlockSpec(memory_space=pltpu.SMEM)


def run_copies(copies):
    for copy in copies:
        copy.start()
    for copy in copies:
        copy.wait()


def sigma_kernel(plan, pair_count, place, triples, *refs):
    moms, moments, groups = plan.moms, plan.moments, plan.groups
    half, part, side = plan.half, plan.part, plan.side
    lesser_in, partner_in = refs[:moms], refs[moms : 2 * moms]
    outs = refs[2 * moms : 2 * moms + moms * plan.rows]
    lesser, partner, result, sems = refs[2 * moms + moms * plan.rows :]
    r, y = place[0], place[2]
    copies = []
    for which, (sources, target) in enumerate(((lesser_in, lesser), (partner_in, partner))):
        for q in range(moms):
            owner = y ^ q
            source = sources[q]
            if q == 0:
                source = source.at[:, :, pl.ds(pl.multiple_of(y * half, half), half), :]
            copies.append(
                pltpu.make_async_copy(
                    source, target.at[pl.ds(owner * moments, moments)], sems.at[which * moms + q]
                )
            )
    run_copies(copies)
    scale = 1.0 / pair_count
    lanes = 128 if side % 128 == 0 else side
    for q in reversed(range(moms)):
        for base in range(0, plan.rows, groups):
            moment = (y ^ q) * moments + (r ^ base) // groups
            table = [[triples[moment, m, n] for n in range(3)] for m in range(pair_count)]

            def block(index, _, table=table):
                row = pl.multiple_of(index * 16, 16)
                for lane in range(0, side, lanes):
                    at = (pl.ds(row, 16), pl.ds(lane, lanes))
                    total_re = total_im = None
                    for a, b, c in table:
                        a_re = lesser[(a, 0) + at].astype(jnp.float32)
                        a_im = lesser[(a, 1) + at].astype(jnp.float32)
                        b_re = lesser[(b, 0) + at].astype(jnp.float32)
                        b_im = lesser[(b, 1) + at].astype(jnp.float32)
                        c_re = partner[(c, 0) + at].astype(jnp.float32)
                        c_im = partner[(c, 1) + at].astype(jnp.float32)
                        p_re = a_re * b_re - a_im * b_im
                        p_im = a_re * b_im + a_im * b_re
                        f_re = p_re * c_re - p_im * c_im
                        f_im = p_re * c_im + p_im * c_re
                        total_re = f_re if total_re is None else total_re + f_re
                        total_im = f_im if total_im is None else total_im + f_im
                    result[(0,) + at] = (total_re * scale).astype(jnp.bfloat16)
                    result[(1,) + at] = (total_im * scale).astype(jnp.bfloat16)
                return 0

            lax.fori_loop(0, half // 16, block, 0)
            for t in range(groups):
                g = (r % groups) ^ t
                start = pl.multiple_of(lax.rem(g * part, half), 16)
                outs[q * plan.rows + base + t][...] = result[g * part // half, pl.ds(start, part), :]


def gather_kernel(plan, sources, place, *refs):
    ins, out, sems = refs[:-2], refs[-2], refs[-1]
    for col in range(plan.cols):

        @pl.when(place[1] == col)
        def _(col=col):
            run_copies(
                [
                    pltpu.make_async_copy(ins[sources[col][t]], out.at[t], sems.at[t])
                    for t in range(plan.tiles)
                ]
            )


def place_kernel(plan, place, *refs):
    ins, out, sems = refs[:-2], refs[-2], refs[-1]
    r, y = place[0], place[2]
    copies = []
    for q in range(plan.moms):
        for s in range(plan.rows):
            g = (r ^ s) % plan.groups
            row = (y ^ q) * plan.half + lax.rem(g * plan.part, plan.half)
            index = q * plan.rows + s
            copies.append(
                pltpu.make_async_copy(
                    ins[index],
                    out.at[
                        (r ^ s) // plan.groups,
                        g * plan.part // plan.half,
                        pl.ds(pl.multiple_of(row, 16), plan.part),
                        :,
                    ],
                    sems.at[index],
                )
            )
    run_copies(copies)


def solve_kernel(plan, place, *refs):
    rows, moms, groups, side = plan.rows, plan.moms, plan.groups, plan.side
    refs = list(refs)
    take = lambda count: [refs.pop(0) for _ in range(count)]
    sig_in, diag_in, right_in, outs = take(moms * groups), take(groups), take(rows), take(rows)
    sig, diag, right, solved, turned, sems = refs
    r, y = place[0], place[2]
    copies = []

    def copy(source, target):
        copies.append(pltpu.make_async_copy(source, target, sems.at[len(copies)]))

    for t in range(groups):
        g = (r % groups) ^ t
        for s in range(rows):
            row = pl.multiple_of(lax.rem(g * plan.dpart, side), 16)
            copy(
                diag_in[t].at[s],
                diag.at[r ^ t ^ s, g * plan.dpart // side, pl.ds(row, plan.dpart), :],
            )
        for q in range(moms):
            row = (y ^ q) * plan.half + lax.rem(g * plan.part, plan.half)
            copy(
                sig_in[q * groups + t],
                sig.at[:, g * plan.part // plan.half, pl.ds(pl.multiple_of(row, 16), plan.part), :],
            )
    for s in range(rows):
        copy(right_in[s], right.at[r ^ s])
    run_copies(copies)

    weight = 1.0 / math.sqrt(side * rows)
    width = plan.width

    def turn(value):
        return jnp.concatenate([-value[:, width:], value[:, :width]], axis=1)

    def dot(left, value):
        return jnp.dot(left, value, preferred_element_type=jnp.float32)

    for row in range(rows):
        pending = right[row].astype(jnp.float32)
        if row > 0:
            update = None
            for col in range(row):
                t = plan.tile(row, col)
                term = dot(sig[t, 0], solved[col]) + dot(sig[t, 1], turned[col])
                update = term if update is None else update + term
            pending = pending + weight * update
        value = dot(diag[row, 0], pending.astype(jnp.bfloat16)) + dot(
            diag[row, 1], turn(pending).astype(jnp.bfloat16)
        )
        solved[row] = value.astype(jnp.bfloat16)
        turned[row] = turn(value).astype(jnp.bfloat16)
    copies = [
        pltpu.make_async_copy(solved.at[r ^ s], outs[s], sems.at[s]) for s in range(rows)
    ]
    run_copies(copies)


def on_device(mesh, lesser, greater, triples, diag_inverse, right_side):
    moments, _, side, _ = lesser.shape
    plan = Plan(mesh, moments, side)
    rows, cols, moms, groups = plan.rows, plan.cols, plan.moms, plan.groups
    half, part, width = plan.half, plan.part, plan.width
    pair_count = triples.shape[1]
    r, z, y = (lax.axis_index(axis) for axis in AXES)
    place = jnp.stack([r, z, y]).astype(jnp.int32)
    bf16 = jnp.bfloat16
    params = pltpu.CompilerParams(vmem_limit_bytes=VMEM_BYTES)
    dma = lambda count: pltpu.SemaphoreType.DMA((count,))

    def exchange_mom(value, q):
        return plan.send(value, lambda a, b, c: (a, b, c ^ q))

    def exchange_row(value, s):
        return plan.send(value, lambda a, b, c: (a ^ s, b, c))

    def half_of(value, q):
        return lax.dynamic_slice_in_dim(value, (y ^ q) * half, half, 2)

    lesser_all = [lesser] + [exchange_mom(half_of(lesser, q), q) for q in range(1, moms)]
    partner = jnp.swapaxes(greater, 2, 3)
    partner_all = [partner] + [exchange_mom(half_of(partner, q), q) for q in range(1, moms)]

    flat_diag = diag_inverse.reshape(moments * 2 * side, side)
    diag_parts = [
        lax.dynamic_slice_in_dim(flat_diag, (r ^ s) * plan.dpart, plan.dpart, 0) for s in range(rows)
    ]
    diag_parts = [diag_parts[0]] + [exchange_row(diag_parts[s], s) for s in range(1, rows)]
    diag_own = jnp.stack(diag_parts)
    diag_all = [diag_own] + [exchange_row(diag_own, t) for t in range(1, groups)]

    right = right_side.reshape(moments, side, 2, groups, width).transpose(0, 3, 1, 2, 4)
    right = right.reshape(rows, side, 2 * width)
    right_parts = [lax.dynamic_index_in_dim(right, r ^ s, 0, keepdims=False) for s in range(rows)]
    right_all = [right_parts[0]] + [exchange_row(right_parts[s], s) for s in range(1, rows)]

    slots = pl.pallas_call(
        functools.partial(sigma_kernel, plan, pair_count),
        out_shape=[jax.ShapeDtypeStruct((part, side), bf16)] * (moms * rows),
        in_specs=[smem(), smem()] + hbm(2 * moms),
        scratch_shapes=[
            pltpu.VMEM((moms * moments, 2, half, side), bf16),
            pltpu.VMEM((moms * moments, 2, half, side), bf16),
            pltpu.VMEM((2, half, side), bf16),
            dma(2 * moms),
        ],
        compiler_params=params,
        name="self_energy",
    )(place, triples, *lesser_all, *partner_all)

    chunks = [slots[:rows]]
    for q in range(1, moms):
        chunks.append([exchange_mom(slot, q) for slot in slots[q * rows : (q + 1) * rows]])

    sigma = pl.pallas_call(
        functools.partial(place_kernel, plan),
        out_shape=jax.ShapeDtypeStruct(lesser.shape, bf16),
        in_specs=[smem()] + hbm(moms * rows),
        out_specs=pl.BlockSpec(memory_space=pl.ANY),
        scratch_shapes=[dma(moms * rows)],
        compiler_params=params,
        name="place_sigma",
    )(place, *[slot for chunk in chunks for slot in chunk])

    def spread(chunk):
        came = [chunk[0]] + [
            plan.send(chunk[s], lambda a, b, c: (a ^ s, b, c) if a > b else None)
            for s in range(1, rows)
        ]
        own = {}
        for i in range(1, rows):
            own[i] = lax.select_n(r ^ jnp.minimum(z + i, rows - 1), *came)
        buffers, found = [], {}

        def keep(value, pairs):
            for key in pairs:
                found[key] = len(buffers)
            buffers.append(value)

        for i in range(1, rows):
            keep(own[i], [(j, i, j) for j in range(cols) if j + i < rows])
        last = cols - 1
        relay = []
        for step in range(1, cols):
            for i in range(1, rows):
                up = [
                    j
                    for j in range(cols)
                    if j + i < rows and j + step < cols and (j + step < last or step == 1)
                ]
                if up:
                    value = plan.send(own[i], lambda a, b, c: (a, b + step, c) if b in up else None)
                    keep(value, [(j, i, j + step) for j in up])
                    if last - 1 - step in up:
                        relay.append((last - 1 - step, i, value))
        for j, i, value in relay:
            value = plan.send(value, lambda a, b, c: (a, last, c) if b == last - 1 else None)
            keep(value, [(j, i, last)])
        for step in range(1, cols):
            for i in range(1, rows):
                down = [j for j in range(cols) if j + i < rows and j - step >= 0]
                if down:
                    value = plan.send(own[i], lambda a, b, c: (a, b - step, c) if b in down else None)
                    keep(value, [(j, i, j - step) for j in down])
        sources = [
            [found[(j, i - j, c)] for i in range(rows) for j in range(i)] for c in range(cols)
        ]
        lower = pl.pallas_call(
            functools.partial(gather_kernel, plan, sources),
            out_shape=jax.ShapeDtypeStruct((plan.tiles, part, side), bf16),
            in_specs=[smem()] + hbm(len(buffers)),
            out_specs=pl.BlockSpec(memory_space=pl.ANY),
            scratch_shapes=[dma(plan.tiles)],
            compiler_params=params,
            name="collect_lower",
        )(place, *buffers)
        return [lower] + [exchange_row(lower, t) for t in range(1, groups)]

    sigma_all = [part_of for chunk in chunks for part_of in spread(chunk)]

    solved = pl.pallas_call(
        functools.partial(solve_kernel, plan),
        out_shape=[jax.ShapeDtypeStruct((side, 2 * width), bf16)] * rows,
        in_specs=[smem()] + hbm(moms * groups + groups + rows),
        out_specs=hbm(rows),
        scratch_shapes=[
            pltpu.VMEM((plan.tiles, 2, side, side), bf16),
            pltpu.VMEM((rows, 2, side, side), bf16),
            pltpu.VMEM((rows, side, 2 * width), bf16),
            pltpu.VMEM((rows, side, 2 * width), bf16),
            pltpu.VMEM((rows, side, 2 * width), bf16),
            dma(groups * (rows + moms) + rows),
        ],
        compiler_params=params,
        name="substitution",
    )(place, *sigma_all, *diag_all, *right_all)

    back = [solved[0]] + [exchange_row(solved[s], s) for s in range(1, rows)]
    pieces = jnp.stack([lax.select_n(r ^ s, *back) for s in range(rows)])
    pieces = pieces.reshape(moments, groups, side, 2, width).transpose(0, 2, 3, 1, 4)
    return sigma, pieces.reshape(moments, side, 2, side)


def solution(mesh):
    placed = (
        P("mom", None, "row", "col"),
        P("mom", None, "col", "row"),
        P(),
        P("mom", None, "row", None),
        P("mom", "row", None, "col"),
    )
    return jax.shard_map(
        functools.partial(on_device, mesh),
        mesh=mesh,
        in_specs=placed,
        out_specs=(P("mom", None, "row", "col"), P("mom", "row", None, "col")),
        check_vma=False,
    )
```

```python
import functools
import itertools
import math

import jax
import jax.numpy as jnp
from jax import lax
from jax.experimental import pallas as pl
from jax.experimental.pallas import tpu as pltpu
from jax.sharding import PartitionSpec as P

AXES = ("row", "col", "mom")
VMEM_BYTES = 56 * 1024 * 1024


class Plan:
    def __init__(self, mesh, moments, side):
        self.rows = mesh.shape["row"]
        self.cols = mesh.shape["col"]
        self.moms = mesh.shape["mom"]
        self.moments = moments
        self.side = side
        self.groups = self.rows // moments
        self.half = side // self.moms
        self.width = side // self.groups
        self.keys = [
            (b, j)
            for b in reversed(range(moments))
            for j in range(self.cols - 1)
            if (b + 1) * self.groups - 1 > j
        ]

    def send(self, value, target):
        pairs = []
        index = lambda r, c, m: (r * self.cols + c) * self.moms + m
        for place in itertools.product(range(self.rows), range(self.cols), range(self.moms)):
            goal = target(*place)
            if goal is not None:
                pairs.append((index(*place), index(*goal)))
        return lax.ppermute(value, AXES, pairs)

    def direct(self):
        last = self.cols - 1
        wanted = [
            (key, key[1], to)
            for key in self.keys
            for to in range(self.cols)
            if to != key[1] and (to < last or key[1] == last - 1)
        ]
        first = lambda send: (send[0][0] < self.moments - 1, send[2] != last - 1, abs(send[1] - send[2]))
        steps = []
        for key, source, to in sorted(wanted, key=first):
            for step in steps:
                if source not in step and to not in [goal for _, goal in step.values()]:
                    break
            else:
                step = {}
                steps.append(step)
            step[source] = (key, to)
        return steps


def hbm(count):
    return [pl.BlockSpec(memory_space=pl.ANY)] * count


def smem():
    return pl.BlockSpec(memory_space=pltpu.SMEM)


def run_copies(copies):
    for copy in copies:
        copy.start()
    for copy in copies:
        copy.wait()


def sigma_kernel(plan, pair_count, extra, place, triples, *refs):
    moms, moments, groups = plan.moms, plan.moments, plan.groups
    half, side = plan.half, plan.side
    lesser_in, partner_in = refs[:moms], refs[moms : 2 * moms]
    outs = refs[2 * moms + extra : 2 * moms + extra + moms * moments]
    lesser, partner, sems = refs[2 * moms + extra + moms * moments :]
    x, y = place[0] // groups, place[2]
    copies = []
    for which, (sources, target) in enumerate(((lesser_in, lesser), (partner_in, partner))):
        for q in range(moms):
            source = sources[q]
            if q == 0:
                source = source.at[:, :, pl.ds(pl.multiple_of(y * half, half), half), :]
            copies.append(
                pltpu.make_async_copy(
                    source, target.at[pl.ds((y ^ q) * moments, moments)], sems.at[which * moms + q]
                )
            )
    run_copies(copies)
    scale = 1.0 / pair_count
    lanes = 128 if side % 128 == 0 else side
    for q in reversed(range(moms)):
        for b in range(moments):
            moment = (y ^ q) * moments + (x ^ b)
            table = [[triples[moment, m, n] for n in range(3)] for m in range(pair_count)]
            out = outs[q * moments + b]

            def block(index, _, table=table, out=out):
                row = pl.multiple_of(index * 16, 16)
                for lane in range(0, side, lanes):
                    at = (pl.ds(row, 16), pl.ds(lane, lanes))
                    total_re = total_im = None
                    for a, b, c in table:
                        a_re, a_im = lesser[(a, 0) + at], lesser[(a, 1) + at]
                        b_re, b_im = lesser[(b, 0) + at], lesser[(b, 1) + at]
                        c_re, c_im = partner[(c, 0) + at], partner[(c, 1) + at]
                        p_re = a_re * b_re - a_im * b_im
                        p_im = a_re * b_im + a_im * b_re
                        f_re = (p_re * c_re - p_im * c_im).astype(jnp.float32)
                        f_im = (p_re * c_im + p_im * c_re).astype(jnp.float32)
                        total_re = f_re if total_re is None else total_re + f_re
                        total_im = f_im if total_im is None else total_im + f_im
                    out[(0,) + at] = (total_re * scale).astype(jnp.bfloat16)
                    out[(1,) + at] = (total_im * scale).astype(jnp.bfloat16)
                return 0

            lax.fori_loop(0, half // 16, block, 0)


def gather_kernel(plan, sources, place, *refs):
    ins, out, sems = refs[:-2], refs[-2], refs[-1]
    for col in range(plan.cols):

        @pl.when(place[1] == col)
        def _(col=col):
            run_copies(
                [
                    pltpu.make_async_copy(ins[index], out.at[k], sems.at[k])
                    for k, index in enumerate(sources[col])
                ]
            )


def place_kernel(plan, place, *refs):
    ins, out, sems = refs[:-2], refs[-2], refs[-1]
    x, y = place[0] // plan.groups, place[2]
    copies = []
    for q in range(plan.moms):
        rows = pl.ds(pl.multiple_of((y ^ q) * plan.half, plan.half), plan.half)
        for b in range(plan.moments):
            index = q * plan.moments + b
            copies.append(pltpu.make_async_copy(ins[index], out.at[x ^ b, :, rows, :], sems.at[index]))
    run_copies(copies)


def solve_kernel(plan, place, *refs):
    rows, moms, groups, side = plan.rows, plan.moms, plan.groups, plan.side
    moments, half, width = plan.moments, plan.half, plan.width
    refs = list(refs)
    take = lambda count: [refs.pop(0) for _ in range(count)]
    sig_in, diag_in, right_in = take(moms * groups), take(moments * groups), take(rows)
    outs = take(rows)
    sig, diag, right, solved, sems = refs
    r, y = place[0], place[2]
    count = [0]

    def copy(source, target):
        made = pltpu.make_async_copy(source, target, sems.at[count[0]])
        count[0] += 1
        made.start()
        return made

    stages = [[] for _ in range(moments)]
    for s in range(rows):
        stages[0].append(copy(right_in[s], right.at[r ^ s]))
    for b in range(moments):
        for t in range(groups):
            for p in range(2):
                stages[0].append(
                    copy(
                        diag_in[b * groups + t].at[p],
                        diag.at[r ^ (b * groups) ^ t, :, pl.ds(p * side, side)],
                    )
                )
    for k, (b, j) in reversed(list(enumerate(plan.keys))):
        for t in range(groups):
            tile_row = b * groups + ((r % groups) ^ t)
            for q in range(moms):
                at = pl.ds(pl.multiple_of((y ^ q) * half, half), half)
                for p in range(2):
                    stages[b].append(
                        copy(
                            sig_in[q * groups + t].at[k, p],
                            sig.at[tile_row, at, pl.ds((2 * j + p) * side, side)],
                        )
                    )

    weight = 1.0 / math.sqrt(side * rows)

    def turn(value):
        return jnp.concatenate([-value[:, width:], value[:, :width]], axis=1)

    for row in range(rows):
        if row % groups == 0:
            for made in stages[row // groups]:
                made.wait()
        pending = right[row].astype(jnp.float32)
        if row > 0:
            depth = 2 * side * row
            pending = pending + weight * jnp.dot(
                sig[row, :, :depth], solved[:depth, :], preferred_element_type=jnp.float32
            )
        both = jnp.concatenate([pending, turn(pending)], axis=0).astype(jnp.bfloat16)
        value = jnp.dot(diag[row], both, preferred_element_type=jnp.float32)
        solved[pl.ds(2 * row * side, side), :] = value.astype(jnp.bfloat16)
        solved[pl.ds((2 * row + 1) * side, side), :] = turn(value).astype(jnp.bfloat16)
    copies = []
    for s in range(rows):
        at = pl.ds(pl.multiple_of(2 * (r ^ s) * side, side), side)
        copies.append(pltpu.make_async_copy(solved.at[at, :], outs[s], sems.at[s]))
    run_copies(copies)


def on_device(mesh, lesser, greater, triples, diag_inverse, right_side):
    moments, _, side, _ = lesser.shape
    plan = Plan(mesh, moments, side)
    rows, cols, moms, groups = plan.rows, plan.cols, plan.moms, plan.groups
    half, width = plan.half, plan.width
    pair_count = triples.shape[1]
    r, z, y = (lax.axis_index(axis) for axis in AXES)
    x = r // groups
    place = jnp.stack([r, z, y]).astype(jnp.int32)
    bf16 = jnp.bfloat16
    params = pltpu.CompilerParams(vmem_limit_bytes=VMEM_BYTES)
    dma = lambda count: pltpu.SemaphoreType.DMA((count,))

    def exchange_mom(value, q):
        return plan.send(value, lambda a, b, c: (a, b, c ^ q))

    def exchange_row(value, s):
        return plan.send(value, lambda a, b, c: (a ^ s, b, c))

    def half_of(value, q):
        return lax.dynamic_slice_in_dim(value, (y ^ q) * half, half, 2)

    lesser_all = [lesser] + [exchange_mom(half_of(lesser, q), q) for q in range(1, moms)]
    partner = jnp.swapaxes(greater, 2, 3)
    partner_all = [partner] + [exchange_mom(half_of(partner, q), q) for q in range(1, moms)]

    diag_all = [lax.dynamic_index_in_dim(diag_inverse, x ^ b, 0, keepdims=False) for b in range(moments)]
    diag_all = diag_all[:1] + [exchange_row(diag_all[b], b * groups) for b in range(1, moments)]

    right = right_side.reshape(moments, side, 2, groups, width).transpose(0, 3, 1, 2, 4)
    right = right.reshape(rows, side, 2 * width)
    right_all = [lax.dynamic_index_in_dim(right, r ^ s, 0, keepdims=False) for s in range(rows)]
    right_all = right_all[:1] + [exchange_row(right_all[s], s) for s in range(1, rows)]

    early = diag_all + right_all
    slots = pl.pallas_call(
        functools.partial(sigma_kernel, plan, pair_count, len(early)),
        out_shape=[jax.ShapeDtypeStruct((2, half, side), bf16)] * (moms * moments),
        in_specs=[smem(), smem()] + hbm(2 * moms + len(early)),
        scratch_shapes=[
            pltpu.VMEM((moms * moments, 2, half, side), bf16),
            pltpu.VMEM((moms * moments, 2, half, side), bf16),
            dma(2 * moms),
        ],
        compiler_params=params,
        name="self_energy",
    )(place, triples, *lesser_all, *partner_all, *early)

    diag_all = [
        value if t == 0 else exchange_row(value, t) for value in diag_all for t in range(groups)
    ]
    chunks = [slots[:moments]]
    for q in range(1, moms):
        chunks.append([exchange_mom(slot, q) for slot in slots[q * moments : (q + 1) * moments]])

    sigma = pl.pallas_call(
        functools.partial(place_kernel, plan),
        out_shape=jax.ShapeDtypeStruct(lesser.shape, bf16),
        in_specs=[smem()] + hbm(moms * moments),
        scratch_shapes=[dma(moms * moments)],
        compiler_params=params,
        name="place_sigma",
    )(place, *[slot for chunk in chunks for slot in chunk])

    def spread(chunk):
        came = [chunk[0]] + [
            plan.send(chunk[b], lambda a, c, m: (a ^ (b * groups), c, m) if a > c else None)
            for b in range(1, moments)
        ]
        own = [lax.select_n(x ^ b, *came) for b in range(moments)]
        buffers, found = list(own), {}
        for b, j in plan.keys:
            found[(b, j, j)] = b
        last = cols - 1

        def valid(key, a):
            return key[0] * groups + a % groups > key[1]

        for step in plan.direct():
            blocks = sorted({key[0] for key, _ in step.values()})
            value = own[blocks[0]]
            for b in blocks[1:]:
                for source, (key, _) in step.items():
                    if key[0] == b:
                        value = jnp.where(z == source, own[b], value)
            goal = lambda a, c, m: (
                (a, step[c][1], m) if c in step and valid(step[c][0], a) else None
            )
            for key, to in step.values():
                found[key + (to,)] = len(buffers)
            buffers.append(plan.send(value, goal))
        for key in sorted(plan.keys, key=lambda key: found.get(key + (last - 1,), 0)):
            if key[1] < last - 1:
                value = buffers[found[key + (last - 1,)]]
                goal = lambda a, c, m: (a, last, m) if c == last - 1 and valid(key, a) else None
                found[key + (last,)] = len(buffers)
                buffers.append(plan.send(value, goal))
        sources = [[found[key + (c,)] for key in plan.keys] for c in range(cols)]
        lower = pl.pallas_call(
            functools.partial(gather_kernel, plan, sources),
            out_shape=jax.ShapeDtypeStruct((len(plan.keys), 2, half, side), bf16),
            in_specs=[smem()] + hbm(len(buffers)),
            scratch_shapes=[dma(len(plan.keys))],
            compiler_params=params,
            name="collect_lower",
        )(place, *buffers)
        return [lower] + [exchange_row(lower, t) for t in range(1, groups)]

    sigma_all = [part_of for chunk in chunks for part_of in spread(chunk)]

    solved = pl.pallas_call(
        functools.partial(solve_kernel, plan),
        out_shape=[jax.ShapeDtypeStruct((side, 2 * width), bf16)] * rows,
        in_specs=[smem()] + hbm(moms * groups + rows + rows),
        out_specs=hbm(rows),
        scratch_shapes=[
            pltpu.VMEM((rows, side, 2 * side * (cols - 1)), bf16),
            pltpu.VMEM((rows, side, 2 * side), bf16),
            pltpu.VMEM((rows, side, 2 * width), bf16),
            pltpu.VMEM((rows * 2 * side, 2 * width), bf16),
            dma(rows + 2 * rows + len(plan.keys) * groups * moms * 2),
        ],
        compiler_params=params,
        name="substitution",
    )(place, *sigma_all, *diag_all, *right_all)

    back = [solved[0]] + [exchange_row(solved[s], s) for s in range(1, rows)]
    pieces = jnp.stack([lax.select_n(r ^ s, *back) for s in range(rows)])
    pieces = pieces.reshape(moments, groups, side, 2, width).transpose(0, 2, 3, 1, 4)
    return sigma, pieces.reshape(moments, side, 2, side)


def solution(mesh):
    placed = (
        P("mom", None, "row", "col"),
        P("mom", None, "col", "row"),
        P(),
        P("mom", None, "row", None),
        P("mom", "row", None, "col"),
    )
    return jax.shard_map(
        functools.partial(on_device, mesh),
        mesh=mesh,
        in_specs=placed,
        out_specs=(P("mom", None, "row", "col"), P("mom", "row", None, "col")),
        check_vma=False,
    )
```

```python
import functools
import itertools
import math

import jax
import jax.numpy as jnp
from jax import lax
from jax.experimental import pallas as pl
from jax.experimental.pallas import tpu as pltpu
from jax.sharding import PartitionSpec as P

AXES = ("row", "col", "mom")
VMEM_BYTES = 56 * 1024 * 1024


class Plan:
    def __init__(self, mesh, moments, side):
        self.rows = mesh.shape["row"]
        self.cols = mesh.shape["col"]
        self.moms = mesh.shape["mom"]
        self.moments = moments
        self.side = side
        self.groups = self.rows // moments
        self.half = side // self.moms
        self.width = side // self.groups
        self.keys = [
            (b, j)
            for b in range(moments)
            for j in range(self.cols - 1)
            if (b + 1) * self.groups - 1 > j
        ]

    def send(self, value, target):
        pairs = []
        index = lambda r, c, m: (r * self.cols + c) * self.moms + m
        for place in itertools.product(range(self.rows), range(self.cols), range(self.moms)):
            goal = target(*place)
            if goal is not None:
                pairs.append((index(*place), index(*goal)))
        return lax.ppermute(value, AXES, pairs)

    def direct(self, wanted):
        hub = self.cols - 2
        steps = []
        for key, source, to in sorted(wanted, key=lambda s: (s[2] != hub, abs(s[1] - s[2]))):
            for step in steps:
                if source not in step and to not in [goal for _, goal in step.values()]:
                    break
            else:
                step = {}
                steps.append(step)
            step[source] = (key, to)
        return steps


def hbm(count):
    return [pl.BlockSpec(memory_space=pl.ANY)] * count


def smem():
    return pl.BlockSpec(memory_space=pltpu.SMEM)


def run_copies(copies):
    for copy in copies:
        copy.start()
    for copy in copies:
        copy.wait()


def sigma_kernel(plan, pair_count, place, triples, *refs):
    moms, moments, groups = plan.moms, plan.moments, plan.groups
    half, side = plan.half, plan.side
    lesser_in, partner_in = refs[:moms], refs[moms : 2 * moms]
    outs = refs[2 * moms : 2 * moms + moms * moments]
    lesser, partner, sems = refs[2 * moms + moms * moments :]
    x, y = place[0] // groups, place[2]
    copies = []
    for which, (sources, target) in enumerate(((lesser_in, lesser), (partner_in, partner))):
        for q in range(moms):
            source = sources[q]
            if q == 0:
                source = source.at[:, :, pl.ds(pl.multiple_of(y * half, half), half), :]
            copies.append(
                pltpu.make_async_copy(
                    source, target.at[pl.ds((y ^ q) * moments, moments)], sems.at[which * moms + q]
                )
            )
    run_copies(copies)
    scale = 1.0 / pair_count
    lanes = 128 if side % 128 == 0 else side
    for q in reversed(range(moms)):
        for b in range(moments):
            moment = (y ^ q) * moments + (x ^ b)
            table = [[triples[moment, m, n] for n in range(3)] for m in range(pair_count)]
            out = outs[q * moments + b]

            def block(index, _, table=table, out=out):
                row = pl.multiple_of(index * 16, 16)
                for lane in range(0, side, lanes):
                    at = (pl.ds(row, 16), pl.ds(lane, lanes))
                    total_re = total_im = None
                    for a, b, c in table:
                        a_re, a_im = lesser[(a, 0) + at], lesser[(a, 1) + at]
                        b_re, b_im = lesser[(b, 0) + at], lesser[(b, 1) + at]
                        c_re, c_im = partner[(c, 0) + at], partner[(c, 1) + at]
                        p_re = a_re * b_re - a_im * b_im
                        p_im = a_re * b_im + a_im * b_re
                        f_re = (p_re * c_re - p_im * c_im).astype(jnp.float32)
                        f_im = (p_re * c_im + p_im * c_re).astype(jnp.float32)
                        total_re = f_re if total_re is None else total_re + f_re
                        total_im = f_im if total_im is None else total_im + f_im
                    out[(0,) + at] = (total_re * scale).astype(jnp.bfloat16)
                    out[(1,) + at] = (total_im * scale).astype(jnp.bfloat16)
                return 0

            lax.fori_loop(0, half // 16, block, 0)


def place_kernel(plan, place, *refs):
    ins, out, sems = refs[:-2], refs[-2], refs[-1]
    x, y = place[0] // plan.groups, place[2]
    copies = []
    for q in range(plan.moms):
        rows = pl.ds(pl.multiple_of((y ^ q) * plan.half, plan.half), plan.half)
        for b in range(plan.moments):
            index = q * plan.moments + b
            copies.append(pltpu.make_async_copy(ins[index], out.at[x ^ b, :, rows, :], sems.at[index]))
    run_copies(copies)


def solve_kernel(plan, block, place, *refs):
    rows, moms, groups, side = plan.rows, plan.moms, plan.groups, plan.side
    half, width = plan.half, plan.width
    keys = [j for b, j in plan.keys if b == block]
    final = block == plan.moments - 1
    refs = list(refs)
    take = lambda count: [refs.pop(0) for _ in range(count)]
    sig_in, diag_in, right_in = take(moms * groups * len(keys)), take(groups), take(rows)
    before = take(1 if block else 0)
    outs = take(rows if final else 1)
    sig, diag, right, solved, sems = refs
    r, y = place[0], place[2]
    copies = []

    def copy(source, target):
        copies.append(pltpu.make_async_copy(source, target, sems.at[len(copies)]))
        copies[-1].start()

    base = block * groups
    done = 2 * side * base
    for t in range(groups):
        local = (r % groups) ^ t
        for k, j in enumerate(keys):
            for q in range(moms):
                at = pl.ds(pl.multiple_of((y ^ q) * half, half), half)
                for p in range(2):
                    copy(
                        sig_in[(q * groups + t) * len(keys) + k].at[p],
                        sig.at[local, at, pl.ds((2 * j + p) * side, side)],
                    )
        for p in range(2):
            copy(diag_in[t].at[p], diag.at[local, :, pl.ds(p * side, side)])
    for s in range(rows):
        copy(right_in[s], right.at[r ^ s])
    if block:
        copy(before[0], solved.at[pl.ds(0, done), :])
    for made in copies:
        made.wait()

    weight = 1.0 / math.sqrt(side * rows)

    def turn(value):
        return jnp.concatenate([-value[:, width:], value[:, :width]], axis=1)

    for row in range(base, base + groups):
        pending = right[row].astype(jnp.float32)
        if row > 0:
            depth = 2 * side * row
            pending = pending + weight * jnp.dot(
                sig[row - base, :, :depth], solved[:depth, :], preferred_element_type=jnp.float32
            )
        both = jnp.concatenate([pending, turn(pending)], axis=0).astype(jnp.bfloat16)
        value = jnp.dot(diag[row - base], both, preferred_element_type=jnp.float32)
        solved[pl.ds(2 * row * side, side), :] = value.astype(jnp.bfloat16)
        solved[pl.ds((2 * row + 1) * side, side), :] = turn(value).astype(jnp.bfloat16)
    if final:
        copies = []
        for s in range(rows):
            at = pl.ds(pl.multiple_of(2 * (r ^ s) * side, side), side)
            copies.append(pltpu.make_async_copy(solved.at[at, :], outs[s], sems.at[s]))
        run_copies(copies)
    else:
        run_copies([pltpu.make_async_copy(solved, outs[0], sems.at[0])])


def on_device(mesh, lesser, greater, triples, diag_inverse, right_side):
    moments, _, side, _ = lesser.shape
    plan = Plan(mesh, moments, side)
    rows, cols, moms, groups = plan.rows, plan.cols, plan.moms, plan.groups
    half, width = plan.half, plan.width
    pair_count = triples.shape[1]
    r, z, y = (lax.axis_index(axis) for axis in AXES)
    x = r // groups
    place = jnp.stack([r, z, y]).astype(jnp.int32)
    bf16 = jnp.bfloat16
    params = pltpu.CompilerParams(vmem_limit_bytes=VMEM_BYTES)
    dma = lambda count: pltpu.SemaphoreType.DMA((count,))

    def exchange_mom(value, q):
        return plan.send(value, lambda a, b, c: (a, b, c ^ q))

    def exchange_row(value, s):
        return plan.send(value, lambda a, b, c: (a ^ s, b, c))

    def half_of(value, q):
        return lax.dynamic_slice_in_dim(value, (y ^ q) * half, half, 2)

    halves = [half_of(lesser, q) for q in range(1, moms)]
    halves, diag_inverse = lax.optimization_barrier((halves, diag_inverse))
    lesser_all = [lesser] + [exchange_mom(halves[q - 1], q) for q in range(1, moms)]
    partner = jnp.swapaxes(greater, 2, 3)
    partner_all = [partner] + [exchange_mom(half_of(partner, q), q) for q in range(1, moms)]

    came = [lax.dynamic_index_in_dim(diag_inverse, x ^ b, 0, keepdims=False) for b in range(moments)]
    came = came[:1] + [exchange_row(came[b], b * groups) for b in range(1, moments)]
    diag = [lax.select_n(x ^ b, *came) for b in range(moments)]

    right = right_side.reshape(moments, side, 2, groups, width).transpose(0, 3, 1, 2, 4)
    right = right.reshape(rows, side, 2 * width)
    right_all = [lax.dynamic_index_in_dim(right, r ^ s, 0, keepdims=False) for s in range(rows)]
    lesser_all, partner_all, right_all, diag = lax.optimization_barrier(
        (lesser_all, partner_all, right_all, diag)
    )

    slots = pl.pallas_call(
        functools.partial(sigma_kernel, plan, pair_count),
        out_shape=[jax.ShapeDtypeStruct((2, half, side), bf16)] * (moms * moments),
        in_specs=[smem(), smem()] + hbm(2 * moms),
        scratch_shapes=[
            pltpu.VMEM((moms * moments, 2, half, side), bf16),
            pltpu.VMEM((moms * moments, 2, half, side), bf16),
            dma(2 * moms),
        ],
        compiler_params=params,
        name="self_energy",
    )(place, triples, *lesser_all, *partner_all)

    own, whole = [], list(slots[:moments])
    for q in range(moms):
        mine = slots[q * moments : (q + 1) * moments]
        came = [mine[0] if q == 0 else exchange_mom(mine[0], q)]
        for b in range(1, moments):
            came.append(
                plan.send(mine[b], lambda a, c, m: (a ^ (b * groups), c, m ^ q) if a > c else None)
            )
        own.append([lax.select_n(x ^ b, *came) for b in range(moments)])
        if q > 0:
            whole += came[:1] + [exchange_mom(mine[b], q) for b in range(1, moments)]

    sigma = pl.pallas_call(
        functools.partial(place_kernel, plan),
        out_shape=jax.ShapeDtypeStruct(lesser.shape, bf16),
        in_specs=[smem()] + hbm(moms * moments),
        scratch_shapes=[dma(moms * moments)],
        compiler_params=params,
        name="place_sigma",
    )(place, *whole)

    last, top = cols - 1, moments - 1
    found = {}

    def valid(key, a):
        return key[0] * groups + a % groups > key[1]

    def spread(step, values):
        chosen = None
        for source, (key, _) in step.items():
            value = values[key[0]]
            if chosen is None:
                chosen, used = value, value
            elif value is not used:
                chosen = jnp.where(z == source, value, chosen)
        goal = lambda a, c, m: ((a, step[c][1], m) if c in step and valid(step[c][0], a) else None)
        return plan.send(chosen, goal)

    def relay(value, key):
        goal = lambda a, c, m: (a, last, m) if c == last - 1 and valid(key, a) else None
        return plan.send(value, goal)

    sends = [
        (key, key[1], to)
        for key in plan.keys
        for to in range(cols)
        if to != key[1] and (to < last or key[1] == last - 1)
    ]
    split = [send for send in sends if send[0][0] == top and send[2] >= send[1] - 1]
    joint = [send for send in sends if send not in split]
    for key in plan.keys:
        found[key, key[1]] = [own[q][key[0]] for q in range(moms)]
    previous = None
    for q in range(moms):
        values = own[q]
        if previous is not None:
            values, _, right_all = lax.optimization_barrier((values, previous, right_all))
        previous = []
        for step in plan.direct(split):
            value = spread(step, values)
            previous.append(value)
            for key, to in step.values():
                found.setdefault((key, to), []).append(value)
        for key in plan.keys:
            if key[0] == top and key[1] < last - 1:
                value = found[key, last - 1][q]
                if q > 0:
                    value, _ = lax.optimization_barrier((value, found[key, last][q - 1]))
                found.setdefault((key, last), []).append(relay(value, key))
    values = [jnp.stack([own[q][b] for q in range(moms)]) for b in range(moments)]
    for step in plan.direct(joint):
        value = spread(step, values)
        for key, to in step.values():
            found[key, to] = [value[q] for q in range(moms)]
            if key[0] < top and to == last - 1 and key[1] < last - 1:
                value_last = relay(value, key)
                found[key, last] = [value_last[q] for q in range(moms)]

    right_all = right_all[:1] + [exchange_row(right_all[s], s) for s in range(1, rows)]
    before = []
    for block in range(moments):
        keys = [key for key in plan.keys if key[0] == block]
        tiles = [
            [lax.select_n(z, *[found[key, c][q] for c in range(cols)]) for key in keys]
            for q in range(moms)
        ]
        sig_all = [
            value if t == 0 else exchange_row(value, t)
            for q in range(moms)
            for t in range(groups)
            for value in tiles[q]
        ]
        diag_all = [diag[block] if t == 0 else exchange_row(diag[block], t) for t in range(groups)]
        final = block == top
        shape = (side, 2 * width) if final else ((block + 1) * groups * 2 * side, 2 * width)
        count = rows if final else 1
        depth = max(j for _, j in keys) + 1
        before = pl.pallas_call(
            functools.partial(solve_kernel, plan, block),
            out_shape=[jax.ShapeDtypeStruct(shape, bf16)] * count,
            in_specs=[smem()] + hbm(len(sig_all) + groups + rows + (1 if block else 0)),
            out_specs=hbm(count),
            scratch_shapes=[
                pltpu.VMEM((groups, side, 2 * side * depth), bf16),
                pltpu.VMEM((groups, side, 2 * side), bf16),
                pltpu.VMEM((rows, side, 2 * width), bf16),
                pltpu.VMEM(((block + 1) * groups * 2 * side, 2 * width), bf16),
                dma(2 * len(sig_all) + 2 * groups + rows + 1),
            ],
            compiler_params=params,
            name="substitution",
        )(place, *sig_all, *diag_all, *right_all, *before)

    back = [before[0]] + [exchange_row(before[s], s) for s in range(1, rows)]
    pieces = jnp.stack([lax.select_n(r ^ s, *back) for s in range(rows)])
    pieces = pieces.reshape(moments, groups, side, 2, width).transpose(0, 2, 3, 1, 4)
    return sigma, pieces.reshape(moments, side, 2, side)


def solution(mesh):
    placed = (
        P("mom", None, "row", "col"),
        P("mom", None, "col", "row"),
        P(),
        P("mom", None, "row", None),
        P("mom", "row", None, "col"),
    )
    return jax.shard_map(
        functools.partial(on_device, mesh),
        mesh=mesh,
        in_specs=placed,
        out_specs=(P("mom", None, "row", "col"), P("mom", "row", None, "col")),
        check_vma=False,
    )
```

```python
import functools
import itertools
import math

import jax
import jax.numpy as jnp
from jax import lax
from jax.experimental import pallas as pl
from jax.experimental.pallas import tpu as pltpu
from jax.sharding import PartitionSpec as P

AXES = ("row", "col", "mom")
VMEM_BYTES = 56 * 1024 * 1024


class Plan:
    def __init__(self, mesh, moments, side):
        self.rows = mesh.shape["row"]
        self.cols = mesh.shape["col"]
        self.moms = mesh.shape["mom"]
        self.moments = moments
        self.side = side
        self.groups = self.rows // moments
        self.half = side // self.moms
        self.width = side // self.groups
        self.keys = [
            (b, j)
            for b in range(moments)
            for j in range(self.cols - 1)
            if (b + 1) * self.groups - 1 > j
        ]

    def send(self, value, target):
        pairs = []
        index = lambda r, c, m: (r * self.cols + c) * self.moms + m
        for place in itertools.product(range(self.rows), range(self.cols), range(self.moms)):
            goal = target(*place)
            if goal is not None:
                pairs.append((index(*place), index(*goal)))
        return lax.ppermute(value, AXES, pairs)

    def direct(self, wanted):
        hub = self.cols - 2
        steps = []
        for key, source, to in sorted(wanted, key=lambda s: (s[2] != hub, abs(s[1] - s[2]))):
            for step in steps:
                if source not in step and to not in [goal for _, goal in step.values()]:
                    break
            else:
                step = {}
                steps.append(step)
            step[source] = (key, to)
        return steps


def hbm(count):
    return [pl.BlockSpec(memory_space=pl.ANY)] * count


def smem():
    return pl.BlockSpec(memory_space=pltpu.SMEM)


def run_copies(copies):
    for copy in copies:
        copy.start()
    for copy in copies:
        copy.wait()


def sigma_kernel(plan, pair_count, chunks, place, quads, thirds, *refs):
    moms, moments, groups = plan.moms, plan.moments, plan.groups
    half, side, count = plan.half, plan.side, plan.moms * plan.moments
    lesser_in, partner_in = refs[:moms], refs[moms : 2 * moms]
    outs = refs[2 * moms : 2 * moms + count]
    lesser, partner, pairs, third, held, in_sems, out_sems = refs[2 * moms + count :]
    x, y = place[0] // groups, place[2]
    height = half // chunks
    copies = [[] for _ in range(chunks)]
    for chunk in range(chunks):
        rows = pl.ds(chunk * height, height)
        for which, (sources, target) in enumerate(((lesser_in, lesser), (partner_in, partner))):
            for q in range(moms):
                source = sources[q].at[:, :, rows, :]
                if q == 0:
                    start = pl.multiple_of(y * half + chunk * height, 16)
                    source = sources[q].at[:, :, pl.ds(start, height), :]
                copy = pltpu.make_async_copy(
                    source,
                    target.at[pl.ds((y ^ q) * moments, moments), :, rows, :],
                    in_sems.at[(chunk * 2 + which) * moms + q],
                )
                copy.start()
                copies[chunk].append(copy)
    scale = 1.0 / pair_count
    lanes = 128 if side % 128 == 0 else side
    order = [(q, b) for q in reversed(range(moms)) for b in range(moments)]
    sent = []
    for chunk in range(chunks):
        for copy in copies[chunk]:
            copy.wait()

        def block(index, _, chunk=chunk):
            rows = pl.ds(pl.multiple_of(chunk * height + index * 16, 16), 16)
            for c in range(count):
                for p in range(2):
                    third[c, p] = partner[c, p, rows, :].astype(jnp.float32)
            n = 0
            for a in range(count):
                for b in range(a + 1):
                    for lane in range(0, side, lanes):
                        cols = pl.ds(lane, lanes)
                        a_re = lesser[a, 0, rows, cols].astype(jnp.float32)
                        a_im = lesser[a, 1, rows, cols].astype(jnp.float32)
                        b_re = lesser[b, 0, rows, cols].astype(jnp.float32)
                        b_im = lesser[b, 1, rows, cols].astype(jnp.float32)
                        pairs[n, 0, :, cols] = a_re * b_re - a_im * b_im
                        pairs[n, 1, :, cols] = a_re * b_im + a_im * b_re
                    n += 1
            for q, b in order:
                moment = (y ^ q) * moments + (x ^ b)
                for lane in range(0, side, lanes):
                    cols = pl.ds(lane, lanes)
                    total_re = total_im = None
                    for m in range(pair_count):
                        quad, c = quads[moment, m], thirds[moment, m]
                        p_re, p_im = pairs[quad, 0, :, cols], pairs[quad, 1, :, cols]
                        c_re, c_im = third[c, 0, :, cols], third[c, 1, :, cols]
                        f_re = p_re * c_re - p_im * c_im
                        f_im = p_re * c_im + p_im * c_re
                        total_re = f_re if total_re is None else total_re + f_re
                        total_im = f_im if total_im is None else total_im + f_im
                    held[q * moments + b, 0, rows, cols] = (total_re * scale).astype(jnp.bfloat16)
                    held[q * moments + b, 1, rows, cols] = (total_im * scale).astype(jnp.bfloat16)
            return 0

        lax.fori_loop(0, height // 16, block, 0)
        rows = pl.ds(chunk * height, height)
        for index in range(count):
            copy = pltpu.make_async_copy(
                held.at[index, :, rows, :], outs[index].at[:, rows, :], out_sems.at[chunk * count + index]
            )
            copy.start()
            sent.append(copy)
    for copy in sent:
        copy.wait()


def place_kernel(plan, place, *refs):
    ins, out, sems = refs[:-2], refs[-2], refs[-1]
    x, y = place[0] // plan.groups, place[2]
    copies = []
    for q in range(plan.moms):
        rows = pl.ds(pl.multiple_of((y ^ q) * plan.half, plan.half), plan.half)
        for b in range(plan.moments):
            index = q * plan.moments + b
            copies.append(pltpu.make_async_copy(ins[index], out.at[x ^ b, :, rows, :], sems.at[index]))
    run_copies(copies)


def solve_kernel(plan, place, *refs):
    rows, moms, groups, side = plan.rows, plan.moms, plan.groups, plan.side
    moments, half, width, keys = plan.moments, plan.half, plan.width, plan.keys
    top = moments - 1
    refs = list(refs)
    take = lambda count: [refs.pop(0) for _ in range(count)]
    sig_in = {}
    for key in keys:
        for t in range(groups):
            if key[0] == top:
                sig_in[key, t] = take(moms)
            else:
                (ref,) = take(1)
                sig_in[key, t] = [ref.at[q] for q in range(moms)]
    diag_in = {(b, t): take(1)[0] for b in range(moments) for t in range(groups)}
    right_in, outs = take(rows), take(rows)
    sig, diag, right, solved, right_sems, sems, out_sems = refs
    r, y = place[0], place[2]
    g = r % groups

    def tile_copies(row, t):
        made = []
        b = row // groups
        add = lambda source, target: made.append(
            pltpu.make_async_copy(source, target, sems.at[row, len(made)])
        )
        for p in range(2):
            add(diag_in[b, t].at[p], diag.at[row, :, pl.ds(p * side, side)])
        for key in keys:
            if key[0] == b and row > key[1]:
                for q in range(moms):
                    at = pl.ds(pl.multiple_of((y ^ q) * half, half), half)
                    for p in range(2):
                        lane = pl.ds((2 * key[1] + p) * side, side)
                        add(sig_in[key, t][q].at[p], sig.at[row, at, lane])
        return made

    for s in range(rows):
        pltpu.make_async_copy(right_in[s], right.at[r ^ s], right_sems.at[s]).start()
    for me in range(groups):

        @pl.when(g == me)
        def _(me=me):
            for row in range(rows):
                for copy in tile_copies(row, me ^ (row % groups)):
                    copy.start()

    for s in range(rows):
        pltpu.make_async_copy(right_in[s], right.at[r ^ s], right_sems.at[s]).wait()

    weight = 1.0 / math.sqrt(side * rows)

    def turn(value):
        return jnp.concatenate([-value[:, width:], value[:, :width]], axis=1)

    for row in range(rows):
        for copy in tile_copies(row, 0):
            copy.wait()
        pending = right[row].astype(jnp.float32)
        if row > 0:
            depth = 2 * side * row
            pending = pending + weight * jnp.dot(
                sig[row, :, :depth], solved[:depth, :], preferred_element_type=jnp.float32
            )
        both = jnp.concatenate([pending, turn(pending)], axis=0).astype(jnp.bfloat16)
        value = jnp.dot(diag[row], both, preferred_element_type=jnp.float32)
        solved[pl.ds(2 * row * side, side), :] = value.astype(jnp.bfloat16)
        solved[pl.ds((2 * row + 1) * side, side), :] = turn(value).astype(jnp.bfloat16)
        for s in range(rows):

            @pl.when((r ^ s) == row)
            def _(s=s, row=row):
                at = pl.ds(2 * row * side, side)
                pltpu.make_async_copy(solved.at[at, :], outs[s], out_sems.at[s]).start()

    for s in range(rows):
        pltpu.make_async_copy(solved.at[pl.ds(0, side), :], outs[s], out_sems.at[s]).wait()


def after(value, *others):
    return lax.optimization_barrier((value, others))[0]


def on_device(mesh, lesser, greater, triples, diag_inverse, right_side):
    moments, _, side, _ = lesser.shape
    plan = Plan(mesh, moments, side)
    rows, cols, moms, groups = plan.rows, plan.cols, plan.moms, plan.groups
    half, width = plan.half, plan.width
    pair_count = triples.shape[1]
    count = moms * moments
    r, z, y = (lax.axis_index(axis) for axis in AXES)
    x = r // groups
    place = jnp.stack([r, z, y]).astype(jnp.int32)
    bf16, f32 = jnp.bfloat16, jnp.float32
    params = pltpu.CompilerParams(vmem_limit_bytes=VMEM_BYTES)
    dma = lambda *shape: pltpu.SemaphoreType.DMA(shape)

    def exchange_mom(value, q):
        return plan.send(value, lambda a, b, c: (a, b, c ^ q))

    def exchange_row(value, s):
        return plan.send(value, lambda a, b, c: (a ^ s, b, c))

    def half_of(value, q):
        return lax.dynamic_slice_in_dim(value, (y ^ q) * half, half, 2)

    halves = [half_of(lesser, q) for q in range(1, moms)]
    greater, diag_inverse, right_side = after((greater, diag_inverse, right_side), halves)
    lesser_all = [lesser] + [exchange_mom(halves[q - 1], q) for q in range(1, moms)]
    partner = jnp.swapaxes(greater, 2, 3)
    halves = [half_of(partner, q) for q in range(1, moms)]
    diag_inverse, right_side = after((diag_inverse, right_side), halves)
    partner_all = [partner] + [exchange_mom(halves[q - 1], q) for q in range(1, moms)]

    came = [lax.dynamic_index_in_dim(diag_inverse, x ^ b, 0, keepdims=False) for b in range(moments)]
    came = came[:1] + [exchange_row(came[b], b * groups) for b in range(1, moments)]
    diag = [lax.select_n(x ^ b, *came) for b in range(moments)]

    right = right_side.reshape(moments, side, 2, groups, width).transpose(0, 3, 1, 2, 4)
    right = right.reshape(rows, side, 2 * width)
    right_all = [lax.dynamic_index_in_dim(right, r ^ s, 0, keepdims=False) for s in range(rows)]
    lesser_all, partner_all, right_all, diag = lax.optimization_barrier(
        (lesser_all, partner_all, right_all, diag)
    )

    high = jnp.maximum(triples[..., 0], triples[..., 1])
    low = jnp.minimum(triples[..., 0], triples[..., 1])
    quads, thirds = high * (high + 1) // 2 + low, triples[..., 2]
    chunks = 4 if half % 64 == 0 else 1
    slots = pl.pallas_call(
        functools.partial(sigma_kernel, plan, pair_count, chunks),
        out_shape=[jax.ShapeDtypeStruct((2, half, side), bf16)] * count,
        in_specs=[smem()] * 3 + hbm(2 * moms),
        out_specs=hbm(count),
        scratch_shapes=[
            pltpu.VMEM((count, 2, half, side), bf16),
            pltpu.VMEM((count, 2, half, side), bf16),
            pltpu.VMEM((count * (count + 1) // 2, 2, 16, side), f32),
            pltpu.VMEM((count, 2, 16, side), f32),
            pltpu.VMEM((count, 2, half, side), bf16),
            dma(chunks * 2 * moms),
            dma(chunks * count),
        ],
        compiler_params=params,
        name="self_energy",
    )(place, quads, thirds, *lesser_all, *partner_all)

    def own_tiles(q):
        mine = slots[q * moments : (q + 1) * moments]
        came = []
        for b in range(1, moments):
            came.append(
                plan.send(mine[b], lambda a, c, m: (a ^ (b * groups), c, m ^ q) if a > c else None)
            )
        return [mine[0] if q == 0 else exchange_mom(mine[0], q)] + came

    def by_block(came):
        return [lax.select_n(x ^ b, *came) for b in range(moments)]

    came = [own_tiles(q) for q in range(moms)]
    last, top = cols - 1, moments - 1

    def valid(key, a):
        return key[0] * groups + a % groups > key[1]

    def spread(step, values):
        chosen = used = None
        for source, (key, _) in step.items():
            value = values[key[0]]
            if chosen is None:
                chosen = used = value
            elif value is not used:
                chosen = jnp.where(z == source, value, chosen)
        goal = lambda a, c, m: ((a, step[c][1], m) if c in step and valid(step[c][0], a) else None)
        return plan.send(chosen, goal)

    def relay(value, key):
        goal = lambda a, c, m: (a, last, m) if c == last - 1 and valid(key, a) else None
        return plan.send(value, goal)

    sends = [
        (key, key[1], to)
        for key in plan.keys
        for to in range(cols)
        if to != key[1] and (to < last or key[1] == last - 1)
    ]
    split = [send for send in sends if send[0][0] == top and send[2] >= send[1] - 1]
    joint = [send for send in sends if send not in split]
    found = {}
    own, whole = [], None
    log = []

    def issue(make, value):
        if len(log) > 2:
            value = after(value, log[-3])
        log.append(make(value))
        return log[-1]

    extra = []

    def fill():
        if extra:
            extra.pop(0)()

    right_came = [right_all[0]] + [None] * (rows - 1)

    def right_step(s):
        def run():
            right_came[s] = issue(lambda v: exchange_row(v, s), right_all[s])

        return run

    diag_came = {}

    def diag_step(b, t):
        def run():
            diag_came[b, t] = issue(lambda v: exchange_row(v, t), diag[b])

        return run

    extra += [right_step(s) for s in reversed(range(1, rows))]
    extra += [diag_step(b, t) for b in range(moments) for t in range(1, groups)]

    for q in range(moms):
        own.append(by_block(came[q]))
        for key in plan.keys:
            if key[0] == top:
                found.setdefault((key, key[1]), []).append(own[q][top])
    joint_values = [jnp.stack([own[k][b] for k in range(moms)]) for b in range(moments)]
    for key in plan.keys:
        if key[0] < top:
            found[key, key[1]] = joint_values[key[0]]

    def split_step(q, step):
        def run():
            value = issue(lambda v: spread(step, v), own[q])
            for key, to in step.values():
                found.setdefault((key, to), []).append(value)

        return run

    def split_relay(q, key):
        def run():
            value = found[key, last - 1][q]
            if q + 1 < moms:
                value = after(value, came[q + 1])
            value = issue(lambda v: relay(v, key), value)
            found.setdefault((key, last), []).append(value)
            fill()

        return run

    def joint_step(step):
        def run():
            value = issue(lambda v: spread(step, v), joint_values)
            for key, to in step.values():
                found[key, to] = [value[k] for k in range(moms)] if key[0] == top else value

        return run

    def joint_relay(key):
        def run():
            found[key, last] = issue(lambda v: relay(v, key), found[key, last - 1])

        return run

    relays = sorted([key for key in plan.keys if key[1] < last - 1], key=lambda key: -key[1])
    schedule, waiting = [], []
    for q in range(moms):
        for n, step in enumerate(plan.direct(split)):
            if waiting:
                schedule.append(waiting.pop(0))
            schedule.append(split_step(q, step))
        schedule += waiting
        waiting = [split_relay(q, key) for key in relays if key[0] == top]
    steps = [joint_step(step) for step in plan.direct(joint)]
    schedule = schedule[:-1] + steps[:1] + schedule[-1:]
    low_relays = [joint_relay(key) for key in relays if key[0] < top]
    schedule += waiting[:1] + (steps[1:] + low_relays if cols > 4 else low_relays)
    schedule += waiting[1:] + (steps[1:] if cols <= 4 else [])
    for run in schedule:
        run()
    while extra:
        fill()

    whole = [slots[b] for b in range(moments)]
    for q in range(1, moms):
        whole.append(came[q][0])
        for b in range(1, moments):
            whole.append(exchange_mom(after(slots[q * moments + b], log[-1]), q))
    sigma = pl.pallas_call(
        functools.partial(place_kernel, plan),
        out_shape=jax.ShapeDtypeStruct(lesser.shape, bf16),
        in_specs=[smem()] + hbm(count),
        scratch_shapes=[dma(count)],
        compiler_params=params,
        name="place_sigma",
    )(place, *whole)

    sig_all = []
    for key in plan.keys:
        if key[0] == top:
            mine = [lax.select_n(z, *[found[key, c][q] for c in range(cols)]) for q in range(moms)]
        else:
            mine = [lax.select_n(z, *[found[key, c] for c in range(cols)])]
        for t in range(groups):
            sig_all += mine if t == 0 else [exchange_row(value, t) for value in mine]
    diag_all = [
        diag[b] if t == 0 else diag_came[b, t] for b in range(moments) for t in range(groups)
    ]
    most = 2 + 4 * moms * (cols - 1)
    solved = pl.pallas_call(
        functools.partial(solve_kernel, plan),
        out_shape=[jax.ShapeDtypeStruct((side, 2 * width), bf16)] * rows,
        in_specs=[smem()] + hbm(len(sig_all) + len(diag_all) + rows),
        out_specs=hbm(rows),
        scratch_shapes=[
            pltpu.VMEM((rows, side, 2 * side * (cols - 1)), bf16),
            pltpu.VMEM((rows, side, 2 * side), bf16),
            pltpu.VMEM((rows, side, 2 * width), bf16),
            pltpu.VMEM((rows * 2 * side, 2 * width), bf16),
            dma(rows),
            dma(rows, most),
            dma(rows),
        ],
        compiler_params=params,
        name="substitution",
    )(place, *sig_all, *diag_all, *right_came)

    back = [solved[0]] + [exchange_row(solved[s], s) for s in range(1, rows)]
    pieces = jnp.stack([lax.select_n(r ^ s, *back) for s in range(rows)])
    pieces = pieces.reshape(moments, groups, side, 2, width).transpose(0, 2, 3, 1, 4)
    return sigma, pieces.reshape(moments, side, 2, side)


def solution(mesh):
    placed = (
        P("mom", None, "row", "col"),
        P("mom", None, "col", "row"),
        P(),
        P("mom", None, "row", None),
        P("mom", "row", None, "col"),
    )
    return jax.shard_map(
        functools.partial(on_device, mesh),
        mesh=mesh,
        in_specs=placed,
        out_specs=(P("mom", None, "row", "col"), P("mom", "row", None, "col")),
        check_vma=False,
    )
```

```python
import functools
import itertools
import math

import jax
import jax.numpy as jnp
from jax import lax
from jax.experimental import pallas as pl
from jax.experimental.pallas import tpu as pltpu
from jax.sharding import PartitionSpec as P

AXES = ("row", "col", "mom")
VMEM_BYTES = 56 * 1024 * 1024


class Plan:
    def __init__(self, mesh, moments, side):
        self.rows = mesh.shape["row"]
        self.cols = mesh.shape["col"]
        self.moms = mesh.shape["mom"]
        self.moments = moments
        self.side = side
        self.groups = self.rows // moments
        self.half = side // self.moms
        self.width = side // self.groups
        self.keys = [
            (b, j)
            for b in range(moments)
            for j in range(self.cols - 1)
            if (b + 1) * self.groups - 1 > j
        ]

    def send(self, value, target):
        pairs = []
        index = lambda r, c, m: (r * self.cols + c) * self.moms + m
        for place in itertools.product(range(self.rows), range(self.cols), range(self.moms)):
            goal = target(*place)
            if goal is not None:
                pairs.append((index(*place), index(*goal)))
        return lax.ppermute(value, AXES, pairs)

    def direct(self, wanted):
        hub = self.cols - 2
        steps = []
        for key, source, to in sorted(wanted, key=lambda s: (s[2] != hub, abs(s[1] - s[2]))):
            for step in steps:
                if source not in step and to not in [goal for _, goal in step.values()]:
                    break
            else:
                step = {}
                steps.append(step)
            step[source] = (key, to)
        return steps


def hbm(count):
    return [pl.BlockSpec(memory_space=pl.ANY)] * count


def smem():
    return pl.BlockSpec(memory_space=pltpu.SMEM)


def run_copies(copies):
    for copy in copies:
        copy.start()
    for copy in copies:
        copy.wait()


def sigma_kernel(plan, pair_count, chunks, place, quads, thirds, *refs):
    moms, moments, groups = plan.moms, plan.moments, plan.groups
    half, side, count = plan.half, plan.side, plan.moms * plan.moments
    lesser_in, partner_in = refs[:moms], refs[moms : 2 * moms]
    outs = refs[2 * moms : 2 * moms + count]
    lesser, partner, pairs, third, held, in_sems, out_sems = refs[2 * moms + count :]
    x, y = place[0] // groups, place[2]
    height = half // chunks
    copies = [[] for _ in range(chunks)]
    for chunk in range(chunks):
        rows = pl.ds(chunk * height, height)
        for which, (sources, target) in enumerate(((lesser_in, lesser), (partner_in, partner))):
            for q in range(moms):
                source = sources[q].at[:, :, rows, :]
                if q == 0:
                    start = pl.multiple_of(y * half + chunk * height, 16)
                    source = sources[q].at[:, :, pl.ds(start, height), :]
                copy = pltpu.make_async_copy(
                    source,
                    target.at[pl.ds((y ^ q) * moments, moments), :, rows, :],
                    in_sems.at[(chunk * 2 + which) * moms + q],
                )
                copy.start()
                copies[chunk].append(copy)
    scale = 1.0 / pair_count
    lanes = 128 if side % 128 == 0 else side
    order = [(q, b) for q in reversed(range(moms)) for b in range(moments)]
    sent = []
    for chunk in range(chunks):
        for copy in copies[chunk]:
            copy.wait()

        def block(index, _, chunk=chunk):
            rows = pl.ds(pl.multiple_of(chunk * height + index * 16, 16), 16)
            for c in range(count):
                for p in range(2):
                    third[c, p] = partner[c, p, rows, :].astype(jnp.float32)
            n = 0
            for a in range(count):
                for b in range(a + 1):
                    for lane in range(0, side, lanes):
                        cols = pl.ds(lane, lanes)
                        a_re = lesser[a, 0, rows, cols].astype(jnp.float32)
                        a_im = lesser[a, 1, rows, cols].astype(jnp.float32)
                        b_re = lesser[b, 0, rows, cols].astype(jnp.float32)
                        b_im = lesser[b, 1, rows, cols].astype(jnp.float32)
                        pairs[n, 0, :, cols] = a_re * b_re - a_im * b_im
                        pairs[n, 1, :, cols] = a_re * b_im + a_im * b_re
                    n += 1
            for q, b in order:
                moment = (y ^ q) * moments + (x ^ b)
                for lane in range(0, side, lanes):
                    cols = pl.ds(lane, lanes)
                    total_re = total_im = None
                    for m in range(pair_count):
                        quad, c = quads[moment, m], thirds[moment, m]
                        p_re, p_im = pairs[quad, 0, :, cols], pairs[quad, 1, :, cols]
                        c_re, c_im = third[c, 0, :, cols], third[c, 1, :, cols]
                        f_re = p_re * c_re - p_im * c_im
                        f_im = p_re * c_im + p_im * c_re
                        total_re = f_re if total_re is None else total_re + f_re
                        total_im = f_im if total_im is None else total_im + f_im
                    held[q * moments + b, 0, rows, cols] = (total_re * scale).astype(jnp.bfloat16)
                    held[q * moments + b, 1, rows, cols] = (total_im * scale).astype(jnp.bfloat16)
            return 0

        lax.fori_loop(0, height // 16, block, 0)
        rows = pl.ds(chunk * height, height)
        for index in range(count):
            copy = pltpu.make_async_copy(
                held.at[index, :, rows, :], outs[index].at[:, rows, :], out_sems.at[chunk * count + index]
            )
            copy.start()
            sent.append(copy)
    for copy in sent:
        copy.wait()


def place_kernel(plan, place, *refs):
    ins, out, sems = refs[:-2], refs[-2], refs[-1]
    x, y = place[0] // plan.groups, place[2]
    copies = []
    for q in range(plan.moms):
        rows = pl.ds(pl.multiple_of((y ^ q) * plan.half, plan.half), plan.half)
        for b in range(plan.moments):
            index = q * plan.moments + b
            copies.append(pltpu.make_async_copy(ins[index], out.at[x ^ b, :, rows, :], sems.at[index]))
    run_copies(copies)


def solve_kernel(plan, place, *refs):
    rows, moms, groups, side = plan.rows, plan.moms, plan.groups, plan.side
    moments, half, width, keys = plan.moments, plan.half, plan.width, plan.keys
    top = moments - 1
    refs = list(refs)
    take = lambda count: [refs.pop(0) for _ in range(count)]
    sig_in = {}
    for key in keys:
        for t in range(groups):
            if key[0] == top:
                sig_in[key, t] = take(1)
            else:
                (ref,) = take(1)
                sig_in[key, t] = [ref.at[q] for q in range(moms)]
    gathered = [None] + take(moms - 1)
    diag_in = {(b, t): take(1)[0] for b in range(moments) for t in range(groups)}
    right_in, outs = take(rows), take(rows)
    sig, diag, right, solved, right_sems, sems, out_sems = refs
    r, y = place[0], place[2]
    g = r % groups

    def tile_copies(row, t):
        made = []
        b = row // groups
        add = lambda source, target: made.append(
            pltpu.make_async_copy(source, target, sems.at[row, len(made)])
        )
        for p in range(2):
            add(diag_in[b, t].at[p], diag.at[row, :, pl.ds(p * side, side)])
        for key in keys:
            if key[0] == b and row > key[1]:
                for q in range(moms):
                    at = pl.ds(pl.multiple_of((y ^ q) * half, half), half)
                    if b == top and q > 0:
                        source = gathered[q].at[(row % groups) * plan.cols + key[1]]
                    else:
                        source = sig_in[key, t][q]
                    for p in range(2):
                        lane = pl.ds((2 * key[1] + p) * side, side)
                        add(source.at[p], sig.at[row, at, lane])
        return made

    for s in range(rows):
        pltpu.make_async_copy(right_in[s], right.at[r ^ s], right_sems.at[s]).start()
    for me in range(groups):

        @pl.when(g == me)
        def _(me=me):
            for row in range(rows):
                for copy in tile_copies(row, me ^ (row % groups)):
                    copy.start()

    for s in range(rows):
        pltpu.make_async_copy(right_in[s], right.at[r ^ s], right_sems.at[s]).wait()

    weight = 1.0 / math.sqrt(side * rows)

    def turn(value):
        return jnp.concatenate([-value[:, width:], value[:, :width]], axis=1)

    for row in range(rows):
        for copy in tile_copies(row, 0):
            copy.wait()
        pending = right[row].astype(jnp.float32)
        if row > 0:
            depth = 2 * side * row
            pending = pending + weight * jnp.dot(
                sig[row, :, :depth], solved[:depth, :], preferred_element_type=jnp.float32
            )
        both = jnp.concatenate([pending, turn(pending)], axis=0).astype(jnp.bfloat16)
        value = jnp.dot(diag[row], both, preferred_element_type=jnp.float32)
        solved[pl.ds(2 * row * side, side), :] = value.astype(jnp.bfloat16)
        solved[pl.ds((2 * row + 1) * side, side), :] = turn(value).astype(jnp.bfloat16)
        for s in range(rows):

            @pl.when((r ^ s) == row)
            def _(s=s, row=row):
                at = pl.ds(2 * row * side, side)
                pltpu.make_async_copy(solved.at[at, :], outs[s], out_sems.at[s]).start()

    for s in range(rows):
        pltpu.make_async_copy(solved.at[pl.ds(0, side), :], outs[s], out_sems.at[s]).wait()


def after(value, *others):
    return lax.optimization_barrier((value, others))[0]


def on_device(mesh, lesser, greater, triples, diag_inverse, right_side):
    moments, _, side, _ = lesser.shape
    plan = Plan(mesh, moments, side)
    rows, cols, moms, groups = plan.rows, plan.cols, plan.moms, plan.groups
    half, width = plan.half, plan.width
    pair_count = triples.shape[1]
    count = moms * moments
    r, z, y = (lax.axis_index(axis) for axis in AXES)
    x = r // groups
    place = jnp.stack([r, z, y]).astype(jnp.int32)
    bf16, f32 = jnp.bfloat16, jnp.float32
    params = pltpu.CompilerParams(vmem_limit_bytes=VMEM_BYTES)
    dma = lambda *shape: pltpu.SemaphoreType.DMA(shape)

    def exchange_mom(value, q):
        return plan.send(value, lambda a, b, c: (a, b, c ^ q))

    def exchange_row(value, s):
        return plan.send(value, lambda a, b, c: (a ^ s, b, c))

    def half_of(value, q):
        return lax.dynamic_slice_in_dim(value, (y ^ q) * half, half, 2)

    halves = [half_of(lesser, q) for q in range(1, moms)]
    greater, diag_inverse, right_side = after((greater, diag_inverse, right_side), halves)
    lesser_all = [lesser] + [exchange_mom(halves[q - 1], q) for q in range(1, moms)]
    partner = jnp.swapaxes(greater, 2, 3)
    halves = [half_of(partner, q) for q in range(1, moms)]
    diag_inverse, right_side = after((diag_inverse, right_side), halves)
    partner_all = [partner] + [exchange_mom(halves[q - 1], q) for q in range(1, moms)]

    came = [lax.dynamic_index_in_dim(diag_inverse, x ^ b, 0, keepdims=False) for b in range(moments)]
    came = came[:1] + [exchange_row(came[b], b * groups) for b in range(1, moments)]
    diag = [lax.select_n(x ^ b, *came) for b in range(moments)]

    right = right_side.reshape(moments, side, 2, groups, width).transpose(0, 3, 1, 2, 4)
    right = right.reshape(rows, side, 2 * width)
    right_all = [lax.dynamic_index_in_dim(right, r ^ s, 0, keepdims=False) for s in range(rows)]
    right_all = after(right_all, lesser_all[1:])
    right_came = right_all[:1] + [exchange_row(right_all[s], s) for s in range(1, rows)]
    diag_all = [
        diag[b] if t == 0 else exchange_row(diag[b], t) for b in range(moments) for t in range(groups)
    ]
    lesser_all, partner_all, right_came, diag_all = lax.optimization_barrier(
        (lesser_all, partner_all, right_came, diag_all)
    )

    high = jnp.maximum(triples[..., 0], triples[..., 1])
    low = jnp.minimum(triples[..., 0], triples[..., 1])
    quads, thirds = high * (high + 1) // 2 + low, triples[..., 2]
    chunks = 4 if half % 64 == 0 else 1
    slots = pl.pallas_call(
        functools.partial(sigma_kernel, plan, pair_count, chunks),
        out_shape=[jax.ShapeDtypeStruct((2, half, side), bf16)] * count,
        in_specs=[smem()] * 3 + hbm(2 * moms),
        out_specs=hbm(count),
        scratch_shapes=[
            pltpu.VMEM((count, 2, half, side), bf16),
            pltpu.VMEM((count, 2, half, side), bf16),
            pltpu.VMEM((count * (count + 1) // 2, 2, 16, side), f32),
            pltpu.VMEM((count, 2, 16, side), f32),
            pltpu.VMEM((count, 2, half, side), bf16),
            dma(chunks * 2 * moms),
            dma(chunks * count),
        ],
        compiler_params=params,
        name="self_energy",
    )(place, quads, thirds, *lesser_all, *partner_all)

    def own_tiles(q):
        mine = slots[q * moments : (q + 1) * moments]
        came = []
        for b in range(1, moments):
            came.append(
                plan.send(mine[b], lambda a, c, m: (a ^ (b * groups), c, m ^ q) if a > c else None)
            )
        return [mine[0] if q == 0 else exchange_mom(mine[0], q)] + came

    def by_block(came):
        return [lax.select_n(x ^ b, *came) for b in range(moments)]

    came = [own_tiles(q) for q in range(moms)]
    last, top = cols - 1, moments - 1

    def valid(key, a):
        return key[0] * groups + a % groups > key[1]

    def spread(step, values):
        chosen = used = None
        for source, (key, _) in step.items():
            value = values[key[0]]
            if chosen is None:
                chosen = used = value
            elif value is not used:
                chosen = jnp.where(z == source, value, chosen)
        goal = lambda a, c, m: ((a, step[c][1], m) if c in step and valid(step[c][0], a) else None)
        return plan.send(chosen, goal)

    def relay(value, key):
        goal = lambda a, c, m: (a, last, m) if c == last - 1 and valid(key, a) else None
        return plan.send(value, goal)

    sends = [
        (key, key[1], to)
        for key in plan.keys
        for to in range(cols)
        if to != key[1] and (to < last or key[1] == last - 1)
    ]
    split = [send for send in sends if send[0][0] == top and send[2] >= send[1] - 1]
    joint = [send for send in sends if send not in split]
    found = {}
    own, whole = [], None
    log = []

    def issue(make, value):
        if len(log) > 2:
            value = after(value, log[-3])
        log.append(make(value))
        return log[-1]

    for q in range(moms):
        own.append(by_block(came[q]))
    members = [
        [(b * groups + g) * cols + c for g in range(groups) for c in range(cols)]
        for b in range(moments)
    ]
    gathered = [
        lax.all_gather(own[q][top], AXES[:2], axis_index_groups=members) for q in range(1, moms)
    ]
    for key in plan.keys:
        if key[0] == top:
            found[key, key[1]] = own[0][top]
    joint_values = [jnp.stack([own[k][b] for k in range(moms)]) for b in range(moments)]
    for key in plan.keys:
        if key[0] < top:
            found[key, key[1]] = joint_values[key[0]]

    def split_step(step):
        def run():
            value = issue(lambda v: spread(step, v), own[0])
            for key, to in step.values():
                found[key, to] = value

        return run

    def split_relay(key):
        def run():
            value = after(found[key, last - 1], came[1:])
            found[key, last] = issue(lambda v: relay(v, key), value)

        return run

    def joint_step(step):
        def run():
            value = issue(lambda v: spread(step, v), joint_values)
            for key, to in step.values():
                found[key, to] = value[0] if key[0] == top else value

        return run

    def joint_relay(key):
        def run():
            found[key, last] = issue(lambda v: relay(v, key), found[key, last - 1])

        return run

    relays = sorted([key for key in plan.keys if key[1] < last - 1], key=lambda key: -key[1])
    schedule = [split_step(step) for step in plan.direct(split)]
    schedule += [split_relay(key) for key in relays if key[0] == top]
    schedule += [joint_step(step) for step in plan.direct(joint)]
    schedule += [joint_relay(key) for key in relays if key[0] < top]
    for run in schedule:
        run()

    whole = [slots[b] for b in range(moments)]
    for q in range(1, moms):
        whole.append(came[q][0])
        for b in range(1, moments):
            whole.append(exchange_mom(after(slots[q * moments + b], log[-1]), q))
    sigma = pl.pallas_call(
        functools.partial(place_kernel, plan),
        out_shape=jax.ShapeDtypeStruct(lesser.shape, bf16),
        in_specs=[smem()] + hbm(count),
        scratch_shapes=[dma(count)],
        compiler_params=params,
        name="place_sigma",
    )(place, *whole)

    sig_all = []
    for key in plan.keys:
        mine = lax.select_n(z, *[found[key, c] for c in range(cols)])
        for t in range(groups):
            sig_all.append(mine if t == 0 else exchange_row(mine, t))
    sig_all += gathered
    most = 2 + 4 * moms * (cols - 1)
    solved = pl.pallas_call(
        functools.partial(solve_kernel, plan),
        out_shape=[jax.ShapeDtypeStruct((side, 2 * width), bf16)] * rows,
        in_specs=[smem()] + hbm(len(sig_all) + len(diag_all) + rows),
        out_specs=hbm(rows),
        scratch_shapes=[
            pltpu.VMEM((rows, side, 2 * side * (cols - 1)), bf16),
            pltpu.VMEM((rows, side, 2 * side), bf16),
            pltpu.VMEM((rows, side, 2 * width), bf16),
            pltpu.VMEM((rows * 2 * side, 2 * width), bf16),
            dma(rows),
            dma(rows, most),
            dma(rows),
        ],
        compiler_params=params,
        name="substitution",
    )(place, *sig_all, *diag_all, *right_came)

    back = [solved[0]] + [exchange_row(solved[s], s) for s in range(1, rows)]
    pieces = jnp.stack([lax.select_n(r ^ s, *back) for s in range(rows)])
    pieces = pieces.reshape(moments, groups, side, 2, width).transpose(0, 2, 3, 1, 4)
    return sigma, pieces.reshape(moments, side, 2, side)


def solution(mesh):
    placed = (
        P("mom", None, "row", "col"),
        P("mom", None, "col", "row"),
        P(),
        P("mom", None, "row", None),
        P("mom", "row", None, "col"),
    )
    return jax.shard_map(
        functools.partial(on_device, mesh),
        mesh=mesh,
        in_specs=placed,
        out_specs=(P("mom", None, "row", "col"), P("mom", "row", None, "col")),
        check_vma=False,
    )
```

```python
import functools
import itertools
import math

import jax
import jax.numpy as jnp
from jax import lax
from jax.experimental import pallas as pl
from jax.experimental.pallas import tpu as pltpu
from jax.sharding import PartitionSpec as P

AXES = ("row", "col", "mom")
VMEM_BYTES = 56 * 1024 * 1024


class Plan:
    def __init__(self, mesh, moments, side):
        self.rows = mesh.shape["row"]
        self.cols = mesh.shape["col"]
        self.moms = mesh.shape["mom"]
        self.moments = moments
        self.side = side
        self.groups = self.rows // moments
        self.half = side // self.moms
        self.width = side // self.groups
        self.keys = [
            (b, j)
            for b in range(moments)
            for j in range(self.cols - 1)
            if (b + 1) * self.groups - 1 > j
        ]

    def send(self, value, target):
        pairs = []
        index = lambda r, c, m: (r * self.cols + c) * self.moms + m
        for place in itertools.product(range(self.rows), range(self.cols), range(self.moms)):
            goal = target(*place)
            if goal is not None:
                pairs.append((index(*place), index(*goal)))
        return lax.ppermute(value, AXES, pairs)

    def direct(self, wanted):
        hub = self.cols - 2
        steps = []
        for key, source, to in sorted(wanted, key=lambda s: (s[2] != hub, abs(s[1] - s[2]))):
            for step in steps:
                if source not in step and to not in [goal for _, goal in step.values()]:
                    break
            else:
                step = {}
                steps.append(step)
            step[source] = (key, to)
        return steps


def hbm(count):
    return [pl.BlockSpec(memory_space=pl.ANY)] * count


def smem():
    return pl.BlockSpec(memory_space=pltpu.SMEM)


def run_copies(copies):
    for copy in copies:
        copy.start()
    for copy in copies:
        copy.wait()


def sigma_kernel(plan, pair_count, chunks, place, quads, thirds, *refs):
    moms, moments, groups = plan.moms, plan.moments, plan.groups
    half, side, count = plan.half, plan.side, plan.moms * plan.moments
    lesser_in, partner_in = refs[:moms], refs[moms : 2 * moms]
    outs = refs[2 * moms : 2 * moms + count]
    lesser, partner, pairs, third, held, in_sems, out_sems = refs[2 * moms + count :]
    x, y = place[0] // groups, place[2]
    height = half // chunks
    copies = [[] for _ in range(chunks)]
    for chunk in range(chunks):
        rows = pl.ds(chunk * height, height)
        for which, (sources, target) in enumerate(((lesser_in, lesser), (partner_in, partner))):
            for q in range(moms):
                source = sources[q].at[:, :, rows, :]
                if q == 0:
                    start = pl.multiple_of(y * half + chunk * height, 16)
                    source = sources[q].at[:, :, pl.ds(start, height), :]
                copy = pltpu.make_async_copy(
                    source,
                    target.at[pl.ds((y ^ q) * moments, moments), :, rows, :],
                    in_sems.at[(chunk * 2 + which) * moms + q],
                )
                copy.start()
                copies[chunk].append(copy)
    scale = 1.0 / pair_count
    lanes = 128 if side % 128 == 0 else side
    order = [(q, b) for q in reversed(range(moms)) for b in range(moments)]
    sent = []
    for chunk in range(chunks):
        for copy in copies[chunk]:
            copy.wait()

        def block(index, _, chunk=chunk):
            rows = pl.ds(pl.multiple_of(chunk * height + index * 16, 16), 16)
            for c in range(count):
                for p in range(2):
                    third[c, p] = partner[c, p, rows, :].astype(jnp.float32)
            n = 0
            for a in range(count):
                for b in range(a + 1):
                    for lane in range(0, side, lanes):
                        cols = pl.ds(lane, lanes)
                        a_re = lesser[a, 0, rows, cols].astype(jnp.float32)
                        a_im = lesser[a, 1, rows, cols].astype(jnp.float32)
                        b_re = lesser[b, 0, rows, cols].astype(jnp.float32)
                        b_im = lesser[b, 1, rows, cols].astype(jnp.float32)
                        pairs[n, 0, :, cols] = a_re * b_re - a_im * b_im
                        pairs[n, 1, :, cols] = a_re * b_im + a_im * b_re
                    n += 1
            for q, b in order:
                moment = (y ^ q) * moments + (x ^ b)
                for lane in range(0, side, lanes):
                    cols = pl.ds(lane, lanes)
                    total_re = total_im = None
                    for m in range(pair_count):
                        quad, c = quads[moment, m], thirds[moment, m]
                        p_re, p_im = pairs[quad, 0, :, cols], pairs[quad, 1, :, cols]
                        c_re, c_im = third[c, 0, :, cols], third[c, 1, :, cols]
                        f_re = p_re * c_re - p_im * c_im
                        f_im = p_re * c_im + p_im * c_re
                        total_re = f_re if total_re is None else total_re + f_re
                        total_im = f_im if total_im is None else total_im + f_im
                    held[q * moments + b, 0, rows, cols] = (total_re * scale).astype(jnp.bfloat16)
                    held[q * moments + b, 1, rows, cols] = (total_im * scale).astype(jnp.bfloat16)
            return 0

        lax.fori_loop(0, height // 16, block, 0)
        rows = pl.ds(chunk * height, height)
        for index in range(count):
            copy = pltpu.make_async_copy(
                held.at[index, :, rows, :], outs[index].at[:, rows, :], out_sems.at[chunk * count + index]
            )
            copy.start()
            sent.append(copy)
    for copy in sent:
        copy.wait()


def place_kernel(plan, place, *refs):
    ins, out, sems = refs[:-2], refs[-2], refs[-1]
    x, y = place[0] // plan.groups, place[2]
    copies = []
    for q in range(plan.moms):
        rows = pl.ds(pl.multiple_of((y ^ q) * plan.half, plan.half), plan.half)
        for b in range(plan.moments):
            index = q * plan.moments + b
            copies.append(pltpu.make_async_copy(ins[index], out.at[x ^ b, :, rows, :], sems.at[index]))
    run_copies(copies)


def solve_kernel(plan, sources, place, diag, right, *refs):
    rows, moms, groups, side = plan.rows, plan.moms, plan.groups, plan.side
    moments, half, width, keys = plan.moments, plan.half, plan.width, plan.keys
    top = moments - 1
    sig_in, outs = refs[: -rows - 4], refs[-rows - 4 : -4]
    sig, solved, sems, out_sems = refs[-4:]
    r, y = place[0], place[2]
    g = r % groups
    for key in sorted(keys, key=lambda key: key[0]):
        for col in range(plan.cols):

            @pl.when(place[1] == col)
            def _(key=key, col=col):
                for t in range(groups):
                    row = key[0] * groups + (g ^ t)
                    for q in range(moms):
                        index, part = sources[key, col, q, t]
                        ref = sig_in[index] if part is None else sig_in[index].at[part]
                        at = pl.ds(pl.multiple_of((y ^ q) * half, half), half)
                        for p in range(2):
                            lane = pl.ds((2 * key[1] + p) * side, side)
                            pltpu.make_async_copy(
                                ref.at[p], sig.at[row, at, lane], sems.at[key[0]]
                            ).start()

    weight = 1.0 / math.sqrt(side * rows)

    def turn(value):
        return jnp.concatenate([-value[:, width:], value[:, :width]], axis=1)

    for row in range(rows):
        if row == max(1, row // groups * groups):
            for key in keys:
                if key[0] == row // groups:
                    for t in range(groups * moms * 2):
                        pltpu.make_async_copy(
                            sig.at[0, pl.ds(0, half), pl.ds(0, side)],
                            sig.at[0, pl.ds(0, half), pl.ds(0, side)],
                            sems.at[key[0]],
                        ).wait()
        pending = right[r ^ row].astype(jnp.float32)
        if row > 0:
            depth = 2 * side * row
            pending = pending + weight * jnp.dot(
                sig[row, :, :depth], solved[:depth, :], preferred_element_type=jnp.float32
            )
        both = jnp.concatenate([pending, turn(pending)], axis=0).astype(jnp.bfloat16)
        value = jnp.dot(
            diag[(row // groups) * groups + (g ^ (row % groups))],
            both,
            preferred_element_type=jnp.float32,
        )
        solved[pl.ds(2 * row * side, side), :] = value.astype(jnp.bfloat16)
        solved[pl.ds((2 * row + 1) * side, side), :] = turn(value).astype(jnp.bfloat16)
        for s in range(rows):

            @pl.when((r ^ s) == row)
            def _(s=s, row=row):
                at = pl.ds(2 * row * side, side)
                pltpu.make_async_copy(solved.at[at, :], outs[s], out_sems.at[s]).start()

    for s in range(rows):
        pltpu.make_async_copy(solved.at[pl.ds(0, side), :], outs[s], out_sems.at[s]).wait()


def after(value, *others):
    return lax.optimization_barrier((value, others))[0]


def on_device(mesh, lesser, greater, triples, diag_inverse, right_side):
    moments, _, side, _ = lesser.shape
    plan = Plan(mesh, moments, side)
    rows, cols, moms, groups = plan.rows, plan.cols, plan.moms, plan.groups
    half, width = plan.half, plan.width
    pair_count = triples.shape[1]
    count = moms * moments
    r, z, y = (lax.axis_index(axis) for axis in AXES)
    x = r // groups
    place = jnp.stack([r, z, y]).astype(jnp.int32)
    bf16, f32 = jnp.bfloat16, jnp.float32
    params = pltpu.CompilerParams(vmem_limit_bytes=VMEM_BYTES)
    dma = lambda *shape: pltpu.SemaphoreType.DMA(shape)

    def exchange_mom(value, q):
        return plan.send(value, lambda a, b, c: (a, b, c ^ q))

    def exchange_row(value, s):
        return plan.send(value, lambda a, b, c: (a ^ s, b, c))

    def half_of(value, q):
        return lax.dynamic_slice_in_dim(value, (y ^ q) * half, half, 2)

    halves = [half_of(lesser, q) for q in range(1, moms)]
    greater, diag_inverse, right_side = after((greater, diag_inverse, right_side), halves)
    lesser_all = [lesser] + [exchange_mom(halves[q - 1], q) for q in range(1, moms)]
    partner = jnp.swapaxes(greater, 2, 3)
    halves = [half_of(partner, q) for q in range(1, moms)]
    diag_inverse, right_side = after((diag_inverse, right_side), halves)
    partner_all = [partner] + [exchange_mom(halves[q - 1], q) for q in range(1, moms)]

    came = [lax.dynamic_index_in_dim(diag_inverse, x ^ b, 0, keepdims=False) for b in range(moments)]
    came = came[:1] + [exchange_row(came[b], b * groups) for b in range(1, moments)]
    diag = [lax.select_n(x ^ b, *came) for b in range(moments)]

    right = right_side.reshape(moments, side, 2, groups, width).transpose(0, 3, 1, 2, 4)
    right = right.reshape(rows, side, 2 * width)
    right_all = [lax.dynamic_index_in_dim(right, r ^ s, 0, keepdims=False) for s in range(rows)]
    right_all = after(right_all, lesser_all[1:])
    right_came = jnp.stack(right_all[:1] + [exchange_row(right_all[s], s) for s in range(1, rows)])
    diag = [jnp.concatenate([value[0], value[1]], axis=1) for value in diag]
    diag_came = jnp.stack(
        [diag[b] if t == 0 else exchange_row(diag[b], t) for b in range(moments) for t in range(groups)]
    )
    lesser_all, partner_all, right_came, diag_came = lax.optimization_barrier(
        (lesser_all, partner_all, right_came, diag_came)
    )

    high = jnp.maximum(triples[..., 0], triples[..., 1])
    low = jnp.minimum(triples[..., 0], triples[..., 1])
    quads, thirds = high * (high + 1) // 2 + low, triples[..., 2]
    chunks = 4 if half % 64 == 0 else 1
    slots = pl.pallas_call(
        functools.partial(sigma_kernel, plan, pair_count, chunks),
        out_shape=[jax.ShapeDtypeStruct((2, half, side), bf16)] * count,
        in_specs=[smem()] * 3 + hbm(2 * moms),
        out_specs=hbm(count),
        scratch_shapes=[
            pltpu.VMEM((count, 2, half, side), bf16),
            pltpu.VMEM((count, 2, half, side), bf16),
            pltpu.VMEM((count * (count + 1) // 2, 2, 16, side), f32),
            pltpu.VMEM((count, 2, 16, side), f32),
            pltpu.VMEM((count, 2, half, side), bf16),
            dma(chunks * 2 * moms),
            dma(chunks * count),
        ],
        compiler_params=params,
        name="self_energy",
    )(place, quads, thirds, *lesser_all, *partner_all)

    def own_tiles(q):
        mine = slots[q * moments : (q + 1) * moments]
        came = []
        for b in range(1, moments):
            came.append(
                plan.send(mine[b], lambda a, c, m: (a ^ (b * groups), c, m ^ q) if a > c else None)
            )
        return [mine[0] if q == 0 else exchange_mom(mine[0], q)] + came

    def by_block(came):
        return [lax.select_n(x ^ b, *came) for b in range(moments)]

    came = [own_tiles(q) for q in range(moms)]
    last, top = cols - 1, moments - 1

    def valid(key, a):
        return key[0] * groups + a % groups > key[1]

    def spread(step, values):
        chosen = used = None
        for source, (key, _) in step.items():
            value = values[key[0]]
            if chosen is None:
                chosen = used = value
            elif value is not used:
                chosen = jnp.where(z == source, value, chosen)
        goal = lambda a, c, m: ((a, step[c][1], m) if c in step and valid(step[c][0], a) else None)
        return plan.send(chosen, goal)

    def relay(value, key):
        goal = lambda a, c, m: (a, last, m) if c == last - 1 and valid(key, a) else None
        return plan.send(value, goal)

    sends = [
        (key, key[1], to)
        for key in plan.keys
        for to in range(cols)
        if to != key[1] and (to < last or key[1] == last - 1)
    ]
    split = [send for send in sends if send[0][0] == top and send[2] >= send[1] - 1]
    joint = [send for send in sends if send not in split]
    found = {}
    own, whole = [], None
    buffers = []

    def number(value):
        for index, held in enumerate(buffers):
            if held is value:
                return index
        buffers.append(value)
        return len(buffers) - 1

    for q in range(moms):
        own.append(by_block(came[q]))
        for key in plan.keys:
            if key[0] == top:
                found[key, key[1], q] = (own[q][top], None)
    joint_values = [jnp.stack([own[k][b] for k in range(moms)]) for b in range(moments)]
    for key in plan.keys:
        if key[0] < top:
            for q in range(moms):
                found[key, key[1], q] = (joint_values[key[0]], q)

    steps = plan.direct(split)
    sent, relayed = {}, [[] for _ in range(moms)]

    def split_step(q, n):
        value = own[q]
        if q > 0:
            value = after(value, sent[q - 1, n], relayed[q - 1][:n])
        sent[q, n] = value = spread(steps[n], value)
        for key, to in steps[n].values():
            found[key, to, q] = (value, None)

    def split_relay(q, key):
        value = found[key, last - 1, q][0]
        if q + 1 < moms:
            value = after(value, came[q + 1])
        if q > 0:
            value = after(value, found[key, last, q - 1][0])
        value = relay(value, key)
        found[key, last, q] = (value, None)
        relayed[q].append(value)

    relays = sorted([key for key in plan.keys if key[1] < last - 1], key=lambda key: -key[1])
    for q in range(moms):
        for n in range(len(steps)):
            split_step(q, n)
        for key in relays:
            if key[0] == top:
                split_relay(q, key)
    for n, step in enumerate(plan.direct(joint)):
        behind = sent[moms - 1, min(n, len(steps) - 1)]
        value = spread(step, after(joint_values, behind, relayed[0]))
        for key, to in step.values():
            for q in range(moms):
                found[key, to, q] = (value, q)
    for key in relays:
        if key[0] < top:
            value = relay(found[key, last - 1, 0][0], key)
            for q in range(moms):
                found[key, last, q] = (value, q)

    sources = {}
    for (key, col, q), (value, part) in found.items():
        sources[key, col, q, 0] = (number(value), part)
    swapped = {}
    for (key, col, q), (value, part) in found.items():
        for t in range(1, groups):
            index = number(value)
            if (index, t) not in swapped:
                swapped[index, t] = exchange_row(value, t)
            sources[key, col, q, t] = ((index, t), part)
    place_of = {name: len(buffers) + n for n, name in enumerate(swapped)}
    for name, (index, part) in sources.items():
        if name[3] > 0:
            sources[name] = (place_of[index], part)
    sig_all = buffers + list(swapped.values())

    solved = pl.pallas_call(
        functools.partial(solve_kernel, plan, sources),
        out_shape=[jax.ShapeDtypeStruct((side, 2 * width), bf16)] * rows,
        in_specs=[smem()] + [pl.BlockSpec(memory_space=pltpu.VMEM)] * 2 + hbm(len(sig_all)),
        out_specs=hbm(rows),
        scratch_shapes=[
            pltpu.VMEM((rows, side, 2 * side * (cols - 1)), bf16),
            pltpu.VMEM((rows * 2 * side, 2 * width), bf16),
            dma(moments),
            dma(rows),
        ],
        compiler_params=params,
        name="substitution",
    )(place, diag_came, right_came, *sig_all)

    whole = [slots[b] for b in range(moments)]
    for q in range(1, moms):
        whole.append(came[q][0])
        for b in range(1, moments):
            whole.append(exchange_mom(after(slots[q * moments + b], solved), q))
    sigma = pl.pallas_call(
        functools.partial(place_kernel, plan),
        out_shape=jax.ShapeDtypeStruct(lesser.shape, bf16),
        in_specs=[smem()] + hbm(count),
        scratch_shapes=[dma(count)],
        compiler_params=params,
        name="place_sigma",
    )(place, *whole)

    back = [solved[0]] + [exchange_row(solved[s], s) for s in range(1, rows)]
    back = after(back, sigma)
    pieces = jnp.stack([lax.select_n(r ^ s, *back) for s in range(rows)])
    pieces = pieces.reshape(moments, groups, side, 2, width).transpose(0, 2, 3, 1, 4)
    return sigma, pieces.reshape(moments, side, 2, side)


def solution(mesh):
    placed = (
        P("mom", None, "row", "col"),
        P("mom", None, "col", "row"),
        P(),
        P("mom", None, "row", None),
        P("mom", "row", None, "col"),
    )
    return jax.shard_map(
        functools.partial(on_device, mesh),
        mesh=mesh,
        in_specs=placed,
        out_specs=(P("mom", None, "row", "col"), P("mom", "row", None, "col")),
        check_vma=False,
    )
```

```python
import functools
import itertools
import math

import jax
import jax.numpy as jnp
from jax import lax
from jax.experimental import pallas as pl
from jax.experimental.pallas import tpu as pltpu
from jax.sharding import PartitionSpec as P

AXES = ("row", "col", "mom")
VMEM_BYTES = 56 * 1024 * 1024


class Plan:
    def __init__(self, mesh, moments, side):
        self.rows = mesh.shape["row"]
        self.cols = mesh.shape["col"]
        self.moms = mesh.shape["mom"]
        self.moments = moments
        self.side = side
        self.groups = self.rows // moments
        self.half = side // self.moms
        self.width = side // self.groups
        self.keys = [
            (b, j)
            for b in range(moments)
            for j in range(self.cols - 1)
            if (b + 1) * self.groups - 1 > j
        ]

    def send(self, value, target):
        pairs = []
        index = lambda r, c, m: (r * self.cols + c) * self.moms + m
        for place in itertools.product(range(self.rows), range(self.cols), range(self.moms)):
            goal = target(*place)
            if goal is not None:
                pairs.append((index(*place), index(*goal)))
        return lax.ppermute(value, AXES, pairs)

    def ring(self, step):
        own = {
            col: [key for key in reversed(self.keys) if key[1] == col] for col in range(self.cols)
        }
        sends = {}
        order = range(self.cols) if step > 0 else reversed(range(self.cols))
        queue = []
        for col in order:
            queue = [(key, None) for key in own[col]] + [(key, n) for n, (key, _) in enumerate(queue)]
            if 0 <= col + step < self.cols:
                for n, item in enumerate(queue):
                    sends[col, n] = item
        return sends


def hbm(count):
    return [pl.BlockSpec(memory_space=pl.ANY)] * count


def smem():
    return pl.BlockSpec(memory_space=pltpu.SMEM)


def run_copies(copies):
    for copy in copies:
        copy.start()
    for copy in copies:
        copy.wait()


def sigma_kernel(plan, pair_count, chunks, place, quads, thirds, *refs):
    moms, moments, groups = plan.moms, plan.moments, plan.groups
    half, side, count = plan.half, plan.side, plan.moms * plan.moments
    lesser_in, partner_in = refs[:moms], refs[moms : 2 * moms]
    outs = refs[2 * moms : 2 * moms + count]
    lesser, partner, pairs, third, held, in_sems, out_sems = refs[2 * moms + count :]
    x, y = place[0] // groups, place[2]
    height = half // chunks
    copies = [[] for _ in range(chunks)]
    for chunk in range(chunks):
        rows = pl.ds(chunk * height, height)
        for which, (sources, target) in enumerate(((lesser_in, lesser), (partner_in, partner))):
            for q in range(moms):
                source = sources[q].at[:, :, rows, :]
                if q == 0:
                    start = pl.multiple_of(y * half + chunk * height, 16)
                    source = sources[q].at[:, :, pl.ds(start, height), :]
                copy = pltpu.make_async_copy(
                    source,
                    target.at[pl.ds((y ^ q) * moments, moments), :, rows, :],
                    in_sems.at[(chunk * 2 + which) * moms + q],
                )
                copy.start()
                copies[chunk].append(copy)
    scale = 1.0 / pair_count
    lanes = 128 if side % 128 == 0 else side
    order = [(q, b) for q in reversed(range(moms)) for b in range(moments)]
    sent = []
    for chunk in range(chunks):
        for copy in copies[chunk]:
            copy.wait()

        def block(index, _, chunk=chunk):
            rows = pl.ds(pl.multiple_of(chunk * height + index * 16, 16), 16)
            for c in range(count):
                for p in range(2):
                    third[c, p] = partner[c, p, rows, :].astype(jnp.float32)
            n = 0
            for a in range(count):
                for b in range(a + 1):
                    for lane in range(0, side, lanes):
                        cols = pl.ds(lane, lanes)
                        a_re = lesser[a, 0, rows, cols].astype(jnp.float32)
                        a_im = lesser[a, 1, rows, cols].astype(jnp.float32)
                        b_re = lesser[b, 0, rows, cols].astype(jnp.float32)
                        b_im = lesser[b, 1, rows, cols].astype(jnp.float32)
                        pairs[n, 0, :, cols] = a_re * b_re - a_im * b_im
                        pairs[n, 1, :, cols] = a_re * b_im + a_im * b_re
                    n += 1
            for q, b in order:
                moment = (y ^ q) * moments + (x ^ b)
                for lane in range(0, side, lanes):
                    cols = pl.ds(lane, lanes)
                    total_re = total_im = None
                    for m in range(pair_count):
                        quad, c = quads[moment, m], thirds[moment, m]
                        p_re, p_im = pairs[quad, 0, :, cols], pairs[quad, 1, :, cols]
                        c_re, c_im = third[c, 0, :, cols], third[c, 1, :, cols]
                        f_re = p_re * c_re - p_im * c_im
                        f_im = p_re * c_im + p_im * c_re
                        total_re = f_re if total_re is None else total_re + f_re
                        total_im = f_im if total_im is None else total_im + f_im
                    held[q * moments + b, 0, rows, cols] = (total_re * scale).astype(jnp.bfloat16)
                    held[q * moments + b, 1, rows, cols] = (total_im * scale).astype(jnp.bfloat16)
            return 0

        lax.fori_loop(0, height // 16, block, 0)
        rows = pl.ds(chunk * height, height)
        for index in range(count):
            copy = pltpu.make_async_copy(
                held.at[index, :, rows, :], outs[index].at[:, rows, :], out_sems.at[chunk * count + index]
            )
            copy.start()
            sent.append(copy)
    for copy in sent:
        copy.wait()


def place_kernel(plan, place, *refs):
    ins, out, sems = refs[:-2], refs[-2], refs[-1]
    x, y = place[0] // plan.groups, place[2]
    copies = []
    for q in range(plan.moms):
        rows = pl.ds(pl.multiple_of((y ^ q) * plan.half, plan.half), plan.half)
        for b in range(plan.moments):
            index = q * plan.moments + b
            copies.append(pltpu.make_async_copy(ins[index], out.at[x ^ b, :, rows, :], sems.at[index]))
    run_copies(copies)


def solve_kernel(plan, sources, place, diag, right, *refs):
    rows, moms, groups, side = plan.rows, plan.moms, plan.groups, plan.side
    moments, half, width, keys = plan.moments, plan.half, plan.width, plan.keys
    top = moments - 1
    sig_in, outs = refs[: -rows - 4], refs[-rows - 4 : -4]
    sig, solved, sems, out_sems = refs[-4:]
    r, y = place[0], place[2]
    g = r % groups
    for key in sorted(keys, key=lambda key: key[0]):
        for col in range(plan.cols):

            @pl.when(place[1] == col)
            def _(key=key, col=col):
                for t in range(groups):
                    row = key[0] * groups + (g ^ t)
                    for q in range(moms):
                        ref = sig_in[sources[key, col, q, t]]
                        at = pl.ds(pl.multiple_of((y ^ q) * half, half), half)
                        for p in range(2):
                            lane = pl.ds((2 * key[1] + p) * side, side)
                            pltpu.make_async_copy(
                                ref.at[p], sig.at[row, at, lane], sems.at[key[0]]
                            ).start()

    weight = 1.0 / math.sqrt(side * rows)

    def turn(value):
        return jnp.concatenate([-value[:, width:], value[:, :width]], axis=1)

    for row in range(rows):
        if row == max(1, row // groups * groups):
            for key in keys:
                if key[0] == row // groups:
                    for t in range(groups * moms * 2):
                        pltpu.make_async_copy(
                            sig.at[0, pl.ds(0, half), pl.ds(0, side)],
                            sig.at[0, pl.ds(0, half), pl.ds(0, side)],
                            sems.at[key[0]],
                        ).wait()
        pending = right[r ^ row].astype(jnp.float32)
        if row > 0:
            depth = 2 * side * row
            pending = pending + weight * jnp.dot(
                sig[row, :, :depth], solved[:depth, :], preferred_element_type=jnp.float32
            )
        both = jnp.concatenate([pending, turn(pending)], axis=0).astype(jnp.bfloat16)
        value = jnp.dot(
            diag[(row // groups) * groups + (g ^ (row % groups))],
            both,
            preferred_element_type=jnp.float32,
        )
        solved[pl.ds(2 * row * side, side), :] = value.astype(jnp.bfloat16)
        solved[pl.ds((2 * row + 1) * side, side), :] = turn(value).astype(jnp.bfloat16)
        for s in range(rows):

            @pl.when((r ^ s) == row)
            def _(s=s, row=row):
                at = pl.ds(2 * row * side, side)
                pltpu.make_async_copy(solved.at[at, :], outs[s], out_sems.at[s]).start()

    for s in range(rows):
        pltpu.make_async_copy(solved.at[pl.ds(0, side), :], outs[s], out_sems.at[s]).wait()


def after(value, *others):
    return lax.optimization_barrier((value, others))[0]


def on_device(mesh, lesser, greater, triples, diag_inverse, right_side):
    moments, _, side, _ = lesser.shape
    plan = Plan(mesh, moments, side)
    rows, cols, moms, groups = plan.rows, plan.cols, plan.moms, plan.groups
    half, width = plan.half, plan.width
    pair_count = triples.shape[1]
    count = moms * moments
    r, z, y = (lax.axis_index(axis) for axis in AXES)
    x = r // groups
    place = jnp.stack([r, z, y]).astype(jnp.int32)
    bf16, f32 = jnp.bfloat16, jnp.float32
    params = pltpu.CompilerParams(vmem_limit_bytes=VMEM_BYTES)
    dma = lambda *shape: pltpu.SemaphoreType.DMA(shape)

    def exchange_mom(value, q):
        return plan.send(value, lambda a, b, c: (a, b, c ^ q))

    def exchange_row(value, s):
        return plan.send(value, lambda a, b, c: (a ^ s, b, c))

    def half_of(value, q):
        return lax.dynamic_slice_in_dim(value, (y ^ q) * half, half, 2)

    halves = [half_of(lesser, q) for q in range(1, moms)]
    greater, diag_inverse, right_side = after((greater, diag_inverse, right_side), halves)
    lesser_all = [lesser] + [exchange_mom(halves[q - 1], q) for q in range(1, moms)]
    partner = jnp.swapaxes(greater, 2, 3)
    halves = [half_of(partner, q) for q in range(1, moms)]
    diag_inverse, right_side = after((diag_inverse, right_side), halves)
    partner_all = [partner] + [exchange_mom(halves[q - 1], q) for q in range(1, moms)]

    came = [lax.dynamic_index_in_dim(diag_inverse, x ^ b, 0, keepdims=False) for b in range(moments)]
    came = came[:1] + [exchange_row(came[b], b * groups) for b in range(1, moments)]
    diag = [lax.select_n(x ^ b, *came) for b in range(moments)]

    right = right_side.reshape(moments, side, 2, groups, width).transpose(0, 3, 1, 2, 4)
    right = right.reshape(rows, side, 2 * width)
    right_all = [lax.dynamic_index_in_dim(right, r ^ s, 0, keepdims=False) for s in range(rows)]
    diag = [jnp.concatenate([value[0], value[1]], axis=1) for value in diag]
    diag_all = [
        diag[b] if t == 0 else exchange_row(diag[b], t) for b in range(moments) for t in range(groups)
    ]
    lesser_all, partner_all, right_all, diag_all = lax.optimization_barrier(
        (lesser_all, partner_all, right_all, diag_all)
    )
    diag_came = jnp.stack(diag_all)

    high = jnp.maximum(triples[..., 0], triples[..., 1])
    low = jnp.minimum(triples[..., 0], triples[..., 1])
    quads, thirds = high * (high + 1) // 2 + low, triples[..., 2]
    chunks = 4 if half % 64 == 0 else 1
    slots = pl.pallas_call(
        functools.partial(sigma_kernel, plan, pair_count, chunks),
        out_shape=[jax.ShapeDtypeStruct((2, half, side), bf16)] * count,
        in_specs=[smem()] * 3 + hbm(2 * moms),
        out_specs=hbm(count),
        scratch_shapes=[
            pltpu.VMEM((count, 2, half, side), bf16),
            pltpu.VMEM((count, 2, half, side), bf16),
            pltpu.VMEM((count * (count + 1) // 2, 2, 16, side), f32),
            pltpu.VMEM((count, 2, 16, side), f32),
            pltpu.VMEM((count, 2, half, side), bf16),
            dma(chunks * 2 * moms),
            dma(chunks * count),
        ],
        compiler_params=params,
        name="self_energy",
    )(place, quads, thirds, *lesser_all, *partner_all)

    came = []

    def own_tiles(q):
        mine = slots[q * moments : (q + 1) * moments]
        if came:
            mine = mine[:1] + after(mine[1:], came[-1][1:])
        got = []
        for b in range(1, moments):
            got.append(
                plan.send(mine[b], lambda a, c, m: (a ^ (b * groups), c, m ^ q) if a > c else None)
            )
        came.append([mine[0] if q == 0 else exchange_mom(mine[0], q)] + got)

    def by_block(came):
        return [lax.select_n(x ^ b, *came) for b in range(moments)]

    for q in range(moms):
        own_tiles(q)
    right_all = after(right_all, came[-1])
    right_all = right_all[:1] + [exchange_row(right_all[s], s) for s in range(1, rows)]
    right_came = jnp.stack(right_all)

    def valid(key, a):
        return key[0] * groups + a % groups > key[1]

    found = {}
    own = []
    for q in range(moms):
        own.append(by_block(came[q]))
        for key in plan.keys:
            found[key, key[1], q] = own[q][key[0]]

    def shift(q, direction, number, got, *behind):
        sends = {col: item for (col, n), item in plan.ring(direction).items() if n == number}
        chosen = used = None
        for col, (key, step) in sends.items():
            value = own[q][key[0]] if step is None else got[step]
            if chosen is None:
                chosen = used = value
            elif value is not used:
                chosen = jnp.where(z == col, value, chosen)
        goal = lambda a, c, m: (
            (a, c + direction, m) if c in sends and valid(sends[c][0], a) else None
        )
        value = plan.send(after(chosen, behind), goal)
        got.append(value)
        for col, (key, _) in sends.items():
            found[key, col + direction, q] = value

    right_got, left_got = [[] for _ in range(moms)], [[] for _ in range(moms)]
    right_steps = max(n for _, n in plan.ring(1)) + 1
    left_steps = max(n for _, n in plan.ring(-1)) + 1
    for number in range(right_steps):
        for q in range(moms):
            behind = []
            if q > 0:
                behind.append(right_got[q - 1][number])
            if number == 1 and q + 1 < moms:
                behind.append(came[q + 1])
            if number + 1 == right_steps and q + 1 == moms:
                behind += [right_came, diag_came]
            shift(q, 1, number, right_got[q], *behind)
    for number in range(left_steps):
        for q in range(moms):
            shift(q, -1, number, left_got[q], right_got[q][min(number, right_steps - 1)])

    buffers = []

    def number_of(value):
        for index, held in enumerate(buffers):
            if held is value:
                return index
        buffers.append(value)
        return len(buffers) - 1

    sources = {name + (0,): number_of(value) for name, value in found.items()}
    sig_all = list(buffers)
    for t in range(1, groups):
        for name, value in found.items():
            sources[name + (t,)] = len(sig_all) + number_of(value)
        sig_all += [exchange_row(value, t) for value in buffers]

    solved = pl.pallas_call(
        functools.partial(solve_kernel, plan, sources),
        out_shape=[jax.ShapeDtypeStruct((side, 2 * width), bf16)] * rows,
        in_specs=[smem()] + [pl.BlockSpec(memory_space=pltpu.VMEM)] * 2 + hbm(len(sig_all)),
        out_specs=hbm(rows),
        scratch_shapes=[
            pltpu.VMEM((rows, side, 2 * side * (cols - 1)), bf16),
            pltpu.VMEM((rows * 2 * side, 2 * width), bf16),
            dma(moments),
            dma(rows),
        ],
        compiler_params=params,
        name="substitution",
    )(place, diag_came, right_came, *sig_all)

    whole = [slots[b] for b in range(moments)]
    for q in range(1, moms):
        whole.append(came[q][0])
        for b in range(1, moments):
            whole.append(exchange_mom(after(slots[q * moments + b], solved), q))
    sigma = pl.pallas_call(
        functools.partial(place_kernel, plan),
        out_shape=jax.ShapeDtypeStruct(lesser.shape, bf16),
        in_specs=[smem()] + hbm(count),
        scratch_shapes=[dma(count)],
        compiler_params=params,
        name="place_sigma",
    )(place, *whole)

    back = [solved[0]] + [exchange_row(solved[s], s) for s in range(1, rows)]
    back = after(back, sigma)
    pieces = jnp.stack([lax.select_n(r ^ s, *back) for s in range(rows)])
    pieces = pieces.reshape(moments, groups, side, 2, width).transpose(0, 2, 3, 1, 4)
    return sigma, pieces.reshape(moments, side, 2, side)


def solution(mesh):
    placed = (
        P("mom", None, "row", "col"),
        P("mom", None, "col", "row"),
        P(),
        P("mom", None, "row", None),
        P("mom", "row", None, "col"),
    )
    return jax.shard_map(
        functools.partial(on_device, mesh),
        mesh=mesh,
        in_specs=placed,
        out_specs=(P("mom", None, "row", "col"), P("mom", "row", None, "col")),
        check_vma=False,
    )
```

```python
import functools
import itertools
import math

import jax
import jax.numpy as jnp
from jax import lax
from jax.experimental import pallas as pl
from jax.experimental.pallas import tpu as pltpu
from jax.sharding import PartitionSpec as P

AXES = ("row", "col", "mom")
VMEM_BYTES = 56 * 1024 * 1024


class Plan:
    def __init__(self, mesh, moments, side):
        self.rows = mesh.shape["row"]
        self.cols = mesh.shape["col"]
        self.moms = mesh.shape["mom"]
        self.moments = moments
        self.side = side
        self.groups = self.rows // moments
        self.half = side // self.moms
        self.width = side // self.groups
        self.keys = [
            (b, j)
            for b in range(moments)
            for j in range(self.cols - 1)
            if (b + 1) * self.groups - 1 > j
        ]

    def send(self, value, target):
        pairs = []
        index = lambda r, c, m: (r * self.cols + c) * self.moms + m
        for place in itertools.product(range(self.rows), range(self.cols), range(self.moms)):
            goal = target(*place)
            if goal is not None:
                pairs.append((index(*place), index(*goal)))
        return lax.ppermute(value, AXES, pairs)

    def ring(self):
        top, last = self.moments - 1, self.cols - 1
        sends, queue = {}, []
        for col in range(last):
            queue = [((top, col), None)] + [(key, n) for n, (key, _) in enumerate(queue)]
            for n, (key, step) in enumerate(queue):
                sends[n, col] = (key, col + 1, step)
        wanted = [
            (key, to)
            for key in self.keys
            if key[0] < top
            for to in range(self.cols)
            if to not in (key[1], last)
        ]
        for key, to in wanted:
            for n in range(1, last):
                if (n, key[1]) in sends or (n, to - 1) in sends and sends[n, to - 1][1] == to:
                    continue
                if to not in [goal for (m, _), (_, goal, _) in sends.items() if m == n]:
                    sends[n, key[1]] = (key, to, None)
                    break
        return sends

    def rest(self):
        done = {(key, to) for key, to, _ in self.ring().values()}
        wanted = [
            (key, to)
            for key in self.keys
            for to in range(self.cols)
            if to != key[1] and (key, to) not in done
        ]
        steps = []
        for key, to in sorted(wanted, key=lambda item: (item[0][0], -item[1], -item[0][1])):
            for step in steps:
                if key[1] not in step and to not in [goal for _, goal in step.values()]:
                    break
            else:
                step = {}
                steps.append(step)
            step[key[1]] = (key, to)
        return steps


def hbm(count):
    return [pl.BlockSpec(memory_space=pl.ANY)] * count


def smem():
    return pl.BlockSpec(memory_space=pltpu.SMEM)


def run_copies(copies):
    for copy in copies:
        copy.start()
    for copy in copies:
        copy.wait()


def sigma_kernel(plan, pair_count, chunks, place, quads, thirds, *refs):
    moms, moments, groups = plan.moms, plan.moments, plan.groups
    half, side, count = plan.half, plan.side, plan.moms * plan.moments
    lesser_in, partner_in = refs[:moms], refs[moms : 2 * moms]
    outs = refs[2 * moms : 2 * moms + count]
    lesser, partner, pairs, third, held, in_sems, out_sems = refs[2 * moms + count :]
    x, y = place[0] // groups, place[2]
    height = half // chunks
    copies = [[] for _ in range(chunks)]
    for chunk in range(chunks):
        rows = pl.ds(chunk * height, height)
        for which, (sources, target) in enumerate(((lesser_in, lesser), (partner_in, partner))):
            for q in range(moms):
                source = sources[q].at[:, :, rows, :]
                if q == 0:
                    start = pl.multiple_of(y * half + chunk * height, 16)
                    source = sources[q].at[:, :, pl.ds(start, height), :]
                copy = pltpu.make_async_copy(
                    source,
                    target.at[pl.ds((y ^ q) * moments, moments), :, rows, :],
                    in_sems.at[(chunk * 2 + which) * moms + q],
                )
                copy.start()
                copies[chunk].append(copy)
    scale = 1.0 / pair_count
    lanes = 128 if side % 128 == 0 else side
    order = [(q, b) for q in reversed(range(moms)) for b in range(moments)]
    sent = []
    for chunk in range(chunks):
        for copy in copies[chunk]:
            copy.wait()

        def block(index, _, chunk=chunk):
            rows = pl.ds(pl.multiple_of(chunk * height + index * 16, 16), 16)
            for c in range(count):
                for p in range(2):
                    third[c, p] = partner[c, p, rows, :].astype(jnp.float32)
            n = 0
            for a in range(count):
                for b in range(a + 1):
                    for lane in range(0, side, lanes):
                        cols = pl.ds(lane, lanes)
                        a_re = lesser[a, 0, rows, cols].astype(jnp.float32)
                        a_im = lesser[a, 1, rows, cols].astype(jnp.float32)
                        b_re = lesser[b, 0, rows, cols].astype(jnp.float32)
                        b_im = lesser[b, 1, rows, cols].astype(jnp.float32)
                        pairs[n, 0, :, cols] = a_re * b_re - a_im * b_im
                        pairs[n, 1, :, cols] = a_re * b_im + a_im * b_re
                    n += 1
            for q, b in order:
                moment = (y ^ q) * moments + (x ^ b)
                for lane in range(0, side, lanes):
                    cols = pl.ds(lane, lanes)
                    total_re = total_im = None
                    for m in range(pair_count):
                        quad, c = quads[moment, m], thirds[moment, m]
                        p_re, p_im = pairs[quad, 0, :, cols], pairs[quad, 1, :, cols]
                        c_re, c_im = third[c, 0, :, cols], third[c, 1, :, cols]
                        f_re = p_re * c_re - p_im * c_im
                        f_im = p_re * c_im + p_im * c_re
                        total_re = f_re if total_re is None else total_re + f_re
                        total_im = f_im if total_im is None else total_im + f_im
                    held[q * moments + b, 0, rows, cols] = (total_re * scale).astype(jnp.bfloat16)
                    held[q * moments + b, 1, rows, cols] = (total_im * scale).astype(jnp.bfloat16)
            return 0

        lax.fori_loop(0, height // 16, block, 0)
        rows = pl.ds(chunk * height, height)
        for index in range(count):
            copy = pltpu.make_async_copy(
                held.at[index, :, rows, :], outs[index].at[:, rows, :], out_sems.at[chunk * count + index]
            )
            copy.start()
            sent.append(copy)
    for copy in sent:
        copy.wait()


def place_kernel(plan, place, *refs):
    ins, out, sems = refs[:-2], refs[-2], refs[-1]
    x, y = place[0] // plan.groups, place[2]
    copies = []
    for q in range(plan.moms):
        rows = pl.ds(pl.multiple_of((y ^ q) * plan.half, plan.half), plan.half)
        for b in range(plan.moments):
            index = q * plan.moments + b
            copies.append(pltpu.make_async_copy(ins[index], out.at[x ^ b, :, rows, :], sems.at[index]))
    run_copies(copies)


def solve_kernel(plan, sources, place, diag, right, *refs):
    rows, moms, groups, side = plan.rows, plan.moms, plan.groups, plan.side
    moments, half, width, keys = plan.moments, plan.half, plan.width, plan.keys
    top = moments - 1
    sig_in, outs = refs[: -rows - 4], refs[-rows - 4 : -4]
    sig, solved, sems, out_sems = refs[-4:]
    r, y = place[0], place[2]
    g = r % groups
    for key in sorted(keys, key=lambda key: key[0]):
        for col in range(plan.cols):

            @pl.when(place[1] == col)
            def _(key=key, col=col):
                for t in range(groups):
                    row = key[0] * groups + (g ^ t)
                    for q in range(moms):
                        index, part = sources[key, col, q, t]
                        ref = sig_in[index] if part is None else sig_in[index].at[part]
                        at = pl.ds(pl.multiple_of((y ^ q) * half, half), half)
                        for p in range(2):
                            lane = pl.ds((2 * key[1] + p) * side, side)
                            pltpu.make_async_copy(
                                ref.at[p], sig.at[row, at, lane], sems.at[key[0]]
                            ).start()

    weight = 1.0 / math.sqrt(side * rows)

    def turn(value):
        return jnp.concatenate([-value[:, width:], value[:, :width]], axis=1)

    for row in range(rows):
        if row == max(1, row // groups * groups):
            for key in keys:
                if key[0] == row // groups:
                    for t in range(groups * moms * 2):
                        pltpu.make_async_copy(
                            sig.at[0, pl.ds(0, half), pl.ds(0, side)],
                            sig.at[0, pl.ds(0, half), pl.ds(0, side)],
                            sems.at[key[0]],
                        ).wait()
        pending = right[r ^ row].astype(jnp.float32)
        if row > 0:
            depth = 2 * side * row
            pending = pending + weight * jnp.dot(
                sig[row, :, :depth], solved[:depth, :], preferred_element_type=jnp.float32
            )
        both = jnp.concatenate([pending, turn(pending)], axis=0).astype(jnp.bfloat16)
        value = jnp.dot(
            diag[(row // groups) * groups + (g ^ (row % groups))],
            both,
            preferred_element_type=jnp.float32,
        )
        solved[pl.ds(2 * row * side, side), :] = value.astype(jnp.bfloat16)
        solved[pl.ds((2 * row + 1) * side, side), :] = turn(value).astype(jnp.bfloat16)
        for s in range(rows):

            @pl.when((r ^ s) == row)
            def _(s=s, row=row):
                at = pl.ds(2 * row * side, side)
                pltpu.make_async_copy(solved.at[at, :], outs[s], out_sems.at[s]).start()

    for s in range(rows):
        pltpu.make_async_copy(solved.at[pl.ds(0, side), :], outs[s], out_sems.at[s]).wait()


def after(value, *others):
    return lax.optimization_barrier((value, others))[0]


def on_device(mesh, lesser, greater, triples, diag_inverse, right_side):
    moments, _, side, _ = lesser.shape
    plan = Plan(mesh, moments, side)
    rows, cols, moms, groups = plan.rows, plan.cols, plan.moms, plan.groups
    half, width = plan.half, plan.width
    pair_count = triples.shape[1]
    count = moms * moments
    r, z, y = (lax.axis_index(axis) for axis in AXES)
    x = r // groups
    place = jnp.stack([r, z, y]).astype(jnp.int32)
    bf16, f32 = jnp.bfloat16, jnp.float32
    params = pltpu.CompilerParams(vmem_limit_bytes=VMEM_BYTES)
    dma = lambda *shape: pltpu.SemaphoreType.DMA(shape)

    def exchange_mom(value, q):
        return plan.send(value, lambda a, b, c: (a, b, c ^ q))

    def exchange_row(value, s):
        return plan.send(value, lambda a, b, c: (a ^ s, b, c))

    def half_of(value, q):
        return lax.dynamic_slice_in_dim(value, (y ^ q) * half, half, 2)

    halves = [half_of(lesser, q) for q in range(1, moms)]
    greater, diag_inverse, right_side = after((greater, diag_inverse, right_side), halves)
    lesser_all = [lesser] + [exchange_mom(halves[q - 1], q) for q in range(1, moms)]
    partner = jnp.swapaxes(greater, 2, 3)
    halves = [half_of(partner, q) for q in range(1, moms)]
    diag_inverse, right_side = after((diag_inverse, right_side), halves)
    partner_all = [partner] + [exchange_mom(halves[q - 1], q) for q in range(1, moms)]

    came = [lax.dynamic_index_in_dim(diag_inverse, x ^ b, 0, keepdims=False) for b in range(moments)]
    came = came[:1] + [exchange_row(came[b], b * groups) for b in range(1, moments)]
    diag = [lax.select_n(x ^ b, *came) for b in range(moments)]

    right = right_side.reshape(moments, side, 2, groups, width).transpose(0, 3, 1, 2, 4)
    right = right.reshape(rows, side, 2 * width)
    right_all = [lax.dynamic_index_in_dim(right, r ^ s, 0, keepdims=False) for s in range(rows)]
    diag = [jnp.concatenate([value[0], value[1]], axis=1) for value in diag]
    diag_all = [
        diag[b] if t == 0 else exchange_row(diag[b], t) for b in range(moments) for t in range(groups)
    ]
    lesser_all, partner_all, right_all, diag_all = lax.optimization_barrier(
        (lesser_all, partner_all, right_all, diag_all)
    )
    diag_came = jnp.stack(diag_all)

    high = jnp.maximum(triples[..., 0], triples[..., 1])
    low = jnp.minimum(triples[..., 0], triples[..., 1])
    quads, thirds = high * (high + 1) // 2 + low, triples[..., 2]
    chunks = 4 if half % 64 == 0 else 1
    slots = pl.pallas_call(
        functools.partial(sigma_kernel, plan, pair_count, chunks),
        out_shape=[jax.ShapeDtypeStruct((2, half, side), bf16)] * count,
        in_specs=[smem()] * 3 + hbm(2 * moms),
        out_specs=hbm(count),
        scratch_shapes=[
            pltpu.VMEM((count, 2, half, side), bf16),
            pltpu.VMEM((count, 2, half, side), bf16),
            pltpu.VMEM((count * (count + 1) // 2, 2, 16, side), f32),
            pltpu.VMEM((count, 2, 16, side), f32),
            pltpu.VMEM((count, 2, half, side), bf16),
            dma(chunks * 2 * moms),
            dma(chunks * count),
        ],
        compiler_params=params,
        name="self_energy",
    )(place, quads, thirds, *lesser_all, *partner_all)

    came = []

    def own_tiles(q):
        mine = slots[q * moments : (q + 1) * moments]
        if came:
            mine = mine[:1] + after(mine[1:], came[-1][1:])
        got = []
        for b in range(1, moments):
            got.append(
                plan.send(mine[b], lambda a, c, m: (a ^ (b * groups), c, m ^ q) if a > c else None)
            )
        came.append([mine[0] if q == 0 else exchange_mom(mine[0], q)] + got)

    def by_block(came):
        return [lax.select_n(x ^ b, *came) for b in range(moments)]

    for q in range(moms):
        own_tiles(q)
    right_all = after(right_all, came[-1])
    right_all = right_all[:1] + [exchange_row(right_all[s], s) for s in range(1, rows)]
    right_came = jnp.stack(right_all)

    def valid(key, a):
        return key[0] * groups + a % groups > key[1]

    found = {}
    own = [by_block(came[q]) for q in range(moms)]
    both = [jnp.stack([own[q][b] for q in range(moms)]) for b in range(moments)]
    for key in plan.keys:
        for q in range(moms):
            found[key, key[1], q] = (both[key[0]], q)

    def choose(values):
        chosen = used = None
        for col, value in values.items():
            if chosen is None:
                chosen = used = value
            elif value is not used:
                chosen = jnp.where(z == col, value, chosen)
        return chosen

    def shift(values, goals):
        goal = lambda a, c, m: (a, goals[c][1], m) if c in goals and valid(goals[c][0], a) else None
        return plan.send(choose(values), goal)

    ring, rest = plan.ring(), plan.rest()
    got = [[] for _ in range(moms)]

    def ring_step(q, number, *behind):
        sends = {col: item for (n, col), item in ring.items() if n == number}
        values = {
            col: own[q][key[0]] if step is None else got[q][step]
            for col, (key, _, step) in sends.items()
        }
        value = shift(after(values, behind), {col: item[:2] for col, item in sends.items()})
        got[q].append(value)
        for key, to, _ in sends.values():
            found[key, to, q] = (value, None)

    def rest_step(number, *behind):
        step = rest[number]
        value = shift(after({col: both[key[0]] for col, (key, _) in step.items()}, behind), step)
        for key, to in step.values():
            for q in range(moms):
                found[key, to, q] = (value, q)

    for number in range(cols - 1):
        for q in range(moms):
            behind = [got[p][number] for p in range(q)]
            if number == 1 and q + 1 < moms:
                behind += [came[q + 1], diag_came]
            if number == cols - 2 and q + 1 == moms:
                behind.append(right_came)
            ring_step(q, number, *behind)
    for number in range(len(rest)):
        rest_step(number, got[0][1], got[-1][0])

    buffers = []

    def number_of(value):
        for index, held in enumerate(buffers):
            if held is value:
                return index
        buffers.append(value)
        return len(buffers) - 1

    sources = {name + (0,): (number_of(value), part) for name, (value, part) in found.items()}
    sig_all = list(buffers)
    for t in range(1, groups):
        for name, (value, part) in found.items():
            sources[name + (t,)] = (len(sig_all) + number_of(value), part)
        sig_all += [exchange_row(value, t) for value in buffers]

    solved = pl.pallas_call(
        functools.partial(solve_kernel, plan, sources),
        out_shape=[jax.ShapeDtypeStruct((side, 2 * width), bf16)] * rows,
        in_specs=[smem()] + [pl.BlockSpec(memory_space=pltpu.VMEM)] * 2 + hbm(len(sig_all)),
        out_specs=hbm(rows),
        scratch_shapes=[
            pltpu.VMEM((rows, side, 2 * side * (cols - 1)), bf16),
            pltpu.VMEM((rows * 2 * side, 2 * width), bf16),
            dma(moments),
            dma(rows),
        ],
        compiler_params=params,
        name="substitution",
    )(place, diag_came, right_came, *sig_all)

    whole = [slots[b] for b in range(moments)]
    for q in range(1, moms):
        whole.append(came[q][0])
        for b in range(1, moments):
            whole.append(exchange_mom(after(slots[q * moments + b], solved), q))
    sigma = pl.pallas_call(
        functools.partial(place_kernel, plan),
        out_shape=jax.ShapeDtypeStruct(lesser.shape, bf16),
        in_specs=[smem()] + hbm(count),
        scratch_shapes=[dma(count)],
        compiler_params=params,
        name="place_sigma",
    )(place, *whole)

    back = [solved[0]] + [exchange_row(solved[s], s) for s in range(1, rows)]
    back = after(back, sigma)
    pieces = jnp.stack([lax.select_n(r ^ s, *back) for s in range(rows)])
    pieces = pieces.reshape(moments, groups, side, 2, width).transpose(0, 2, 3, 1, 4)
    return sigma, pieces.reshape(moments, side, 2, side)


def solution(mesh):
    placed = (
        P("mom", None, "row", "col"),
        P("mom", None, "col", "row"),
        P(),
        P("mom", None, "row", None),
        P("mom", "row", None, "col"),
    )
    return jax.shard_map(
        functools.partial(on_device, mesh),
        mesh=mesh,
        in_specs=placed,
        out_specs=(P("mom", None, "row", "col"), P("mom", "row", None, "col")),
        check_vma=False,
    )
```

```python
import functools
import itertools
import math

import jax
import jax.numpy as jnp
from jax import lax
from jax.experimental import pallas as pl
from jax.experimental.pallas import tpu as pltpu
from jax.sharding import PartitionSpec as P

AXES = ("row", "col", "mom")
VMEM_BYTES = 56 * 1024 * 1024


class Plan:
    def __init__(self, mesh, moments, side):
        self.rows = mesh.shape["row"]
        self.cols = mesh.shape["col"]
        self.moms = mesh.shape["mom"]
        self.moments = moments
        self.side = side
        self.groups = self.rows // moments
        self.half = side // self.moms
        self.width = side // self.groups
        self.subs = 2 if self.half % 32 == 0 else 1
        self.sub = self.half // self.subs
        self.chunks = [(0, u * self.sub, self.sub) for u in range(self.subs)]
        self.chunks += [(q, 0, self.half) for q in range(1, self.moms)]
        self.starts = [0]
        for _, _, height in self.chunks:
            self.starts.append(self.starts[-1] + height)
        self.keys = [
            (b, j)
            for b in range(moments)
            for j in range(self.cols - 1)
            if (b + 1) * self.groups - 1 > j
        ]

    def send(self, value, target):
        pairs = []
        index = lambda r, c, m: (r * self.cols + c) * self.moms + m
        for place in itertools.product(range(self.rows), range(self.cols), range(self.moms)):
            goal = target(*place)
            if goal is not None:
                pairs.append((index(*place), index(*goal)))
        return lax.ppermute(value, AXES, pairs)

    def ring(self):
        top, last = self.moments - 1, self.cols - 1
        sends, queue = {}, []
        for col in range(last):
            queue = [((top, col), None)] + [(key, n) for n, (key, _) in enumerate(queue)]
            for n, (key, step) in enumerate(queue):
                sends[n, col] = (key, col + 1, step)
        wanted = [
            (key, to)
            for key in self.keys
            if key[0] < top
            for to in range(self.cols)
            if to not in (key[1], last)
        ]
        for key, to in wanted:
            for n in range(1, last):
                if (n, key[1]) in sends or (n, to - 1) in sends and sends[n, to - 1][1] == to:
                    continue
                if to not in [goal for (m, _), (_, goal, _) in sends.items() if m == n]:
                    sends[n, key[1]] = (key, to, None)
                    break
        return sends

    def rest(self):
        done = {(key, to) for key, to, _ in self.ring().values()}
        wanted = [
            (key, to)
            for key in self.keys
            for to in range(self.cols)
            if to != key[1] and (key, to) not in done
        ]
        steps = []
        for key, to in sorted(wanted, key=lambda item: (item[0][0], -item[1], -item[0][1])):
            for step in steps:
                if key[1] not in step and to not in [goal for _, goal in step.values()]:
                    break
            else:
                step = {}
                steps.append(step)
            step[key[1]] = (key, to)
        return steps


def hbm(count):
    return [pl.BlockSpec(memory_space=pl.ANY)] * count


def smem():
    return pl.BlockSpec(memory_space=pltpu.SMEM)


def run_copies(copies):
    for copy in copies:
        copy.start()
    for copy in copies:
        copy.wait()


def sigma_kernel(plan, pair_count, u, chunks, place, quads, thirds, *refs):
    moms, moments, groups = plan.moms, plan.moments, plan.groups
    half, sub, side, count = plan.half, plan.sub, plan.side, plan.moms * plan.moments
    refs = list(refs)
    take = lambda number: [refs.pop(0) for _ in range(number)]
    lesser_in, partner_in = take(moms), take(moms)
    before, outs = take(count - moments if u else 0), take(count)
    lesser, partner, pairs, third, held, in_sems, out_sems, before_sems = refs
    x, y = place[0] // groups, place[2]
    height = sub // chunks
    copies = [[] for _ in range(chunks)]
    for chunk in range(chunks):
        rows = pl.ds(chunk * height, height)
        for which, (sources, target) in enumerate(((lesser_in, lesser), (partner_in, partner))):
            for q in range(moms):
                source = sources[q].at[:, :, rows, :]
                if q == 0:
                    start = pl.multiple_of(y * half + u * sub + chunk * height, 16)
                    source = sources[q].at[:, :, pl.ds(start, height), :]
                copy = pltpu.make_async_copy(
                    source,
                    target.at[pl.ds((y ^ q) * moments, moments), :, rows, :],
                    in_sems.at[(chunk * 2 + which) * moms + q],
                )
                copy.start()
                copies[chunk].append(copy)
    earlier = [
        pltpu.make_async_copy(
            before[n], held.at[moments + n, :, pl.ds(0, u * sub), :], before_sems.at[n]
        )
        for n in range(len(before))
    ]
    for copy in earlier:
        copy.start()
    scale = 1.0 / pair_count
    lanes = 128 if side % 128 == 0 else side
    order = [(q, b) for q in reversed(range(moms)) for b in range(moments)]
    sent = []
    for chunk in range(chunks):
        for copy in copies[chunk]:
            copy.wait()

        def block(index, _, chunk=chunk):
            row = chunk * height + index * 16
            rows = pl.ds(pl.multiple_of(row, 16), 16)
            for c in range(count):
                for p in range(2):
                    third[c, p] = partner[c, p, rows, :].astype(jnp.float32)
            n = 0
            for a in range(count):
                for b in range(a + 1):
                    for lane in range(0, side, lanes):
                        cols = pl.ds(lane, lanes)
                        a_re = lesser[a, 0, rows, cols].astype(jnp.float32)
                        a_im = lesser[a, 1, rows, cols].astype(jnp.float32)
                        b_re = lesser[b, 0, rows, cols].astype(jnp.float32)
                        b_im = lesser[b, 1, rows, cols].astype(jnp.float32)
                        pairs[n, 0, :, cols] = a_re * b_re - a_im * b_im
                        pairs[n, 1, :, cols] = a_re * b_im + a_im * b_re
                    n += 1
            for q, b in order:
                moment = (y ^ q) * moments + (x ^ b)
                to = rows if q == 0 else pl.ds(pl.multiple_of(u * sub + row, 16), 16)
                for lane in range(0, side, lanes):
                    cols = pl.ds(lane, lanes)
                    total_re = total_im = None
                    for m in range(pair_count):
                        quad, c = quads[moment, m], thirds[moment, m]
                        p_re, p_im = pairs[quad, 0, :, cols], pairs[quad, 1, :, cols]
                        c_re, c_im = third[c, 0, :, cols], third[c, 1, :, cols]
                        f_re = p_re * c_re - p_im * c_im
                        f_im = p_re * c_im + p_im * c_re
                        total_re = f_re if total_re is None else total_re + f_re
                        total_im = f_im if total_im is None else total_im + f_im
                    held[q * moments + b, 0, to, cols] = (total_re * scale).astype(jnp.bfloat16)
                    held[q * moments + b, 1, to, cols] = (total_im * scale).astype(jnp.bfloat16)
            return 0

        lax.fori_loop(0, height // 16, block, 0)
        for index in range(count):
            offset = chunk * height + (u * sub if index >= moments else 0)
            rows = pl.ds(offset, height)
            copy = pltpu.make_async_copy(
                held.at[index, :, rows, :], outs[index].at[:, rows, :], out_sems.at[chunk * count + index]
            )
            copy.start()
            sent.append(copy)
    for copy in earlier:
        copy.wait()
    for n in range(len(before)):
        rows = pl.ds(0, u * sub)
        copy = pltpu.make_async_copy(
            held.at[moments + n, :, rows, :], outs[moments + n].at[:, rows, :], before_sems.at[n]
        )
        copy.start()
        sent.append(copy)
    for copy in sent:
        copy.wait()


def place_kernel(plan, place, *refs):
    ins, out, sems = refs[:-2], refs[-2], refs[-1]
    x, y = place[0] // plan.groups, place[2]
    copies = []
    for k, (q, first, height) in enumerate(plan.chunks):
        rows = pl.ds(pl.multiple_of((y ^ q) * plan.half + first, 16), height)
        for b in range(plan.moments):
            index = k * plan.moments + b
            copies.append(pltpu.make_async_copy(ins[index], out.at[x ^ b, :, rows, :], sems.at[index]))
    run_copies(copies)


def solve_kernel(plan, sources, place, diag, right, *refs):
    rows, moms, groups, side = plan.rows, plan.moms, plan.groups, plan.side
    moments, half, width, keys = plan.moments, plan.half, plan.width, plan.keys
    top = moments - 1
    sig_in, outs = refs[: -rows - 4], refs[-rows - 4 : -4]
    sig, solved, sems, out_sems = refs[-4:]
    r, y = place[0], place[2]
    g = r % groups
    for key in sorted(keys, key=lambda key: key[0]):
        for col in range(plan.cols):

            @pl.when(place[1] == col)
            def _(key=key, col=col):
                for t in range(groups):
                    row = key[0] * groups + (g ^ t)
                    for k, (q, first, height) in enumerate(plan.chunks):
                        index, start = sources[key, col, k, t]
                        at = pl.ds(pl.multiple_of((y ^ q) * half + first, 16), height)
                        for p in range(2):
                            lane = pl.ds((2 * key[1] + p) * side, side)
                            pltpu.make_async_copy(
                                sig_in[index].at[p, pl.ds(start, height), :],
                                sig.at[row, at, lane],
                                sems.at[key[0]],
                            ).start()

    weight = 1.0 / math.sqrt(side * rows)

    def turn(value):
        return jnp.concatenate([-value[:, width:], value[:, :width]], axis=1)

    for row in range(rows):
        if row == max(1, row // groups * groups):
            for key in keys:
                if key[0] == row // groups:
                    for _ in range(groups * 2):
                        tile = sig.at[0, :, pl.ds(0, side)]
                        pltpu.make_async_copy(tile, tile, sems.at[key[0]]).wait()
        pending = right[r ^ row].astype(jnp.float32)
        if row > 0:
            depth = 2 * side * row
            pending = pending + weight * jnp.dot(
                sig[row, :, :depth], solved[:depth, :], preferred_element_type=jnp.float32
            )
        both = jnp.concatenate([pending, turn(pending)], axis=0).astype(jnp.bfloat16)
        value = jnp.dot(
            diag[(row // groups) * groups + (g ^ (row % groups))],
            both,
            preferred_element_type=jnp.float32,
        )
        solved[pl.ds(2 * row * side, side), :] = value.astype(jnp.bfloat16)
        solved[pl.ds((2 * row + 1) * side, side), :] = turn(value).astype(jnp.bfloat16)
        for s in range(rows):

            @pl.when((r ^ s) == row)
            def _(s=s, row=row):
                at = pl.ds(2 * row * side, side)
                pltpu.make_async_copy(solved.at[at, :], outs[s], out_sems.at[s]).start()

    for s in range(rows):
        pltpu.make_async_copy(solved.at[pl.ds(0, side), :], outs[s], out_sems.at[s]).wait()


def after(value, *others):
    return lax.optimization_barrier((value, others))[0]


def on_device(mesh, lesser, greater, triples, diag_inverse, right_side):
    moments, _, side, _ = lesser.shape
    plan = Plan(mesh, moments, side)
    rows, cols, moms, groups = plan.rows, plan.cols, plan.moms, plan.groups
    half, width = plan.half, plan.width
    pair_count = triples.shape[1]
    count = moms * moments
    r, z, y = (lax.axis_index(axis) for axis in AXES)
    x = r // groups
    place = jnp.stack([r, z, y]).astype(jnp.int32)
    bf16, f32 = jnp.bfloat16, jnp.float32
    params = pltpu.CompilerParams(vmem_limit_bytes=VMEM_BYTES)
    dma = lambda *shape: pltpu.SemaphoreType.DMA(shape)

    def exchange_mom(value, q):
        return plan.send(value, lambda a, b, c: (a, b, c ^ q))

    def exchange_row(value, s):
        return plan.send(value, lambda a, b, c: (a ^ s, b, c))

    def by_block(came):
        return [lax.select_n(x ^ b, *came) for b in range(moments)]

    def part_of(value, q, u):
        return lax.dynamic_slice_in_dim(value, (y ^ q) * half + u * plan.sub, plan.sub, 2)

    parts = [part_of(lesser, q, 0) for q in range(1, moms)]
    greater, diag_inverse, right_side = after((greater, diag_inverse, right_side), parts)
    lesser_came = [[exchange_mom(parts[q - 1], q) for q in range(1, moms)]]
    partner = jnp.swapaxes(greater, 2, 3)
    parts = [part_of(partner, q, 0) for q in range(1, moms)]
    diag_inverse, right_side = after((diag_inverse, right_side), parts)
    partner_came = [[exchange_mom(parts[q - 1], q) for q in range(1, moms)]]
    for u in range(1, plan.subs):
        parts = [(part_of(lesser, q, u), part_of(partner, q, u)) for q in range(1, moms)]
        parts = after(parts, lesser_came[-1])
        lesser_came.append([exchange_mom(parts[q - 1][0], q) for q in range(1, moms)])
        partner_came.append([exchange_mom(parts[q - 1][1], q) for q in range(1, moms)])

    mine = [lax.dynamic_index_in_dim(diag_inverse, x ^ b, 0, keepdims=False) for b in range(moments)]
    diag = mine[:1] + [exchange_row(mine[b], b * groups) for b in range(1, moments)]

    right = right_side.reshape(moments, side, 2, groups, width).transpose(0, 3, 1, 2, 4)
    right = right.reshape(rows, side, 2 * width)
    right_all = [lax.dynamic_index_in_dim(right, r ^ s, 0, keepdims=False) for s in range(rows)]
    high = jnp.maximum(triples[..., 0], triples[..., 1])
    low = jnp.minimum(triples[..., 0], triples[..., 1])
    quads, thirds = high * (high + 1) // 2 + low, triples[..., 2]
    copies = 2 if plan.sub % 32 == 0 else 1
    came = []
    whole = []
    rest_of = []

    def self_energy(u, *behind):
        height = (u + 1) * plan.sub
        shapes = [(2, plan.sub, side)] * moments + [(2, height, side)] * (count - moments)
        return pl.pallas_call(
            functools.partial(sigma_kernel, plan, pair_count, u, copies),
            out_shape=[jax.ShapeDtypeStruct(shape, bf16) for shape in shapes],
            in_specs=[smem()] * 3 + hbm(2 * moms + len(rest_of)),
            out_specs=hbm(count),
            scratch_shapes=[
                pltpu.VMEM((count, 2, plan.sub, side), bf16),
                pltpu.VMEM((count, 2, plan.sub, side), bf16),
                pltpu.VMEM((count * (count + 1) // 2, 2, 16, side), f32),
                pltpu.VMEM((count, 2, 16, side), f32),
                pltpu.VMEM((count, 2, height, side), bf16),
                dma(copies * 2 * moms),
                dma(copies * count),
                dma(count),
            ],
            compiler_params=params,
            name="self_energy",
        )(
            *after((place, quads, thirds), behind),
            *([lesser] + lesser_came[u]),
            *([partner] + partner_came[u]),
            *rest_of,
        )

    def to_row(value, b, q):
        goal = lambda a, c, m: (a ^ (b * groups), c, m ^ q) if a > c else None
        return plan.send(value, goal)

    for u in range(plan.subs):
        slots = list(self_energy(u, right_all, diag))
        came = [after(tiles, rest_of, slots) for tiles in came]
        rest_of = slots[moments:]
        came.append(slots[:1] + [to_row(slots[b], b, 0) for b in range(1, moments)])
        whole += slots[:moments]
    late = []
    for q in range(1, moms):
        mine = rest_of[(q - 1) * moments : q * moments]
        came.append(
            [exchange_mom(mine[0], q)] + [to_row(mine[b], b, q) for b in range(1, moments)]
        )
        late += [(came[-1][0], None)] + [(mine[b], q) for b in range(1, moments)]
    right_all = after(right_all, came[-1])
    right_all = right_all[:1] + [exchange_row(right_all[s], s) for s in range(1, rows)]
    right_came = jnp.stack(right_all)
    diag = after(by_block(diag), came[-1])
    diag = [jnp.concatenate([value[0], value[1]], axis=1) for value in diag]
    diag_all = [
        diag[b] if t == 0 else exchange_row(diag[b], t) for b in range(moments) for t in range(groups)
    ]
    diag_came = jnp.stack(diag_all)

    def valid(key, a):
        return key[0] * groups + a % groups > key[1]

    found = {}
    own = [by_block(tiles) for tiles in came]
    both = [jnp.concatenate([tiles[b] for tiles in own], axis=1) for b in range(moments)]
    for key in plan.keys:
        for k in range(len(plan.chunks)):
            found[key, key[1], k] = (both[key[0]], plan.starts[k])

    def choose(values, behind):
        distinct = list({id(value): value for value in values.values()}.values())
        number = {id(value): n for n, value in enumerate(distinct)}
        distinct = after(distinct, behind)
        chosen = distinct[0]
        for col, value in values.items():
            if number[id(value)]:
                chosen = jnp.where(z == col, distinct[number[id(value)]], chosen)
        return chosen

    def shift(values, goals, behind):
        goal = lambda a, c, m: (a, goals[c][1], m) if c in goals and valid(goals[c][0], a) else None
        return plan.send(choose(values, behind), goal)

    ring, rest = plan.ring(), plan.rest()
    got = [[] for _ in plan.chunks]

    def ring_step(q, number, *behind):
        sends = {col: item for (n, col), item in ring.items() if n == number}
        values = {
            col: own[q][key[0]] if step is None else got[q][step]
            for col, (key, _, step) in sends.items()
        }
        value = shift(values, {col: item[:2] for col, item in sends.items()}, behind)
        got[q].append(value)
        for key, to, _ in sends.values():
            found[key, to, q] = (value, 0)

    def rest_step(number, *behind):
        step = rest[number]
        value = shift({col: both[key[0]] for col, (key, _) in step.items()}, step, behind)
        for key, to in step.values():
            for k in range(len(plan.chunks)):
                found[key, to, k] = (value, plan.starts[k])

    for number in range(cols - 1):
        for k in range(len(plan.chunks)):
            behind = [got[k - 1][number]] if k else []
            if number == 1 and k + 1 < len(plan.chunks):
                behind.append(came[k + 1])
            ring_step(k, number, *behind)
    for number in range(len(rest)):
        rest_step(number, got[0][1], got[-1][0], right_all)

    buffers = []

    def number_of(value):
        for index, held in enumerate(buffers):
            if held is value:
                return index
        buffers.append(value)
        return len(buffers) - 1

    sources = {name + (0,): (number_of(value), part) for name, (value, part) in found.items()}
    sig_all = list(buffers)
    for t in range(1, groups):
        for name, (value, part) in found.items():
            sources[name + (t,)] = (len(sig_all) + number_of(value), part)
        sig_all += [exchange_row(value, t) for value in buffers]

    solved = pl.pallas_call(
        functools.partial(solve_kernel, plan, sources),
        out_shape=[jax.ShapeDtypeStruct((side, 2 * width), bf16)] * rows,
        in_specs=[smem()] + [pl.BlockSpec(memory_space=pltpu.VMEM)] * 2 + hbm(len(sig_all)),
        out_specs=hbm(rows),
        scratch_shapes=[
            pltpu.VMEM((rows, side, 2 * side * (cols - 1)), bf16),
            pltpu.VMEM((rows * 2 * side, 2 * width), bf16),
            dma(moments),
            dma(rows),
        ],
        compiler_params=params,
        name="substitution",
    )(place, diag_came, right_came, *sig_all)

    for value, q in late:
        whole.append(value if q is None else exchange_mom(after(value, solved), q))
    sigma = pl.pallas_call(
        functools.partial(place_kernel, plan),
        out_shape=jax.ShapeDtypeStruct(lesser.shape, bf16),
        in_specs=[smem()] + hbm(len(whole)),
        scratch_shapes=[dma(len(whole))],
        compiler_params=params,
        name="place_sigma",
    )(place, *whole)

    back = [solved[0]] + [exchange_row(solved[s], s) for s in range(1, rows)]
    back = after(back, sigma)
    pieces = jnp.stack([lax.select_n(r ^ s, *back) for s in range(rows)])
    pieces = pieces.reshape(moments, groups, side, 2, width).transpose(0, 2, 3, 1, 4)
    return sigma, pieces.reshape(moments, side, 2, side)


def solution(mesh):
    placed = (
        P("mom", None, "row", "col"),
        P("mom", None, "col", "row"),
        P(),
        P("mom", None, "row", None),
        P("mom", "row", None, "col"),
    )
    return jax.shard_map(
        functools.partial(on_device, mesh),
        mesh=mesh,
        in_specs=placed,
        out_specs=(P("mom", None, "row", "col"), P("mom", "row", None, "col")),
        check_vma=False,
    )
```

```python
import functools
import itertools
import math

import jax
import jax.numpy as jnp
from jax import lax
from jax.experimental import pallas as pl
from jax.experimental.pallas import tpu as pltpu
from jax.sharding import PartitionSpec as P

AXES = ("row", "col", "mom")
VMEM_BYTES = 56 * 1024 * 1024


class Plan:
    def __init__(self, mesh, moments, side):
        self.rows = mesh.shape["row"]
        self.cols = mesh.shape["col"]
        self.moms = mesh.shape["mom"]
        self.moments = moments
        self.side = side
        self.groups = self.rows // moments
        self.half = side // self.moms
        self.width = side // self.groups
        self.subs = 2 if self.half % 32 == 0 else 1
        self.sub = self.half // self.subs
        self.chunks = [(q, 0, self.half) for q in range(self.moms)]
        self.starts = [0]
        for _, _, height in self.chunks:
            self.starts.append(self.starts[-1] + height)
        self.keys = [
            (b, j)
            for b in range(moments)
            for j in range(self.cols - 1)
            if (b + 1) * self.groups - 1 > j
        ]

    def send(self, value, target):
        pairs = []
        index = lambda r, c, m: (r * self.cols + c) * self.moms + m
        for place in itertools.product(range(self.rows), range(self.cols), range(self.moms)):
            goal = target(*place)
            if goal is not None:
                pairs.append((index(*place), index(*goal)))
        return lax.ppermute(value, AXES, pairs)

    def ring(self):
        top, last = self.moments - 1, self.cols - 1
        sends, queue = {}, []
        for col in range(last):
            queue = [((top, col), None)] + [(key, n) for n, (key, _) in enumerate(queue)]
            for n, (key, step) in enumerate(queue):
                sends[n, col] = (key, col + 1, step)
        wanted = [
            (key, to)
            for key in self.keys
            if key[0] < top
            for to in range(self.cols)
            if to not in (key[1], last)
        ]
        for key, to in wanted:
            for n in range(1, last):
                if (n, key[1]) in sends or (n, to - 1) in sends and sends[n, to - 1][1] == to:
                    continue
                if to not in [goal for (m, _), (_, goal, _) in sends.items() if m == n]:
                    sends[n, key[1]] = (key, to, None)
                    break
        return sends

    def rest(self):
        done = {(key, to) for key, to, _ in self.ring().values()}
        wanted = [
            (key, to)
            for key in self.keys
            for to in range(self.cols)
            if to != key[1] and (key, to) not in done
        ]
        steps = []
        for key, to in sorted(wanted, key=lambda item: (item[0][0], -item[1], -item[0][1])):
            for step in steps:
                if key[1] not in step and to not in [goal for _, goal in step.values()]:
                    break
            else:
                step = {}
                steps.append(step)
            step[key[1]] = (key, to)
        return steps


def hbm(count):
    return [pl.BlockSpec(memory_space=pl.ANY)] * count


def smem():
    return pl.BlockSpec(memory_space=pltpu.SMEM)


def run_copies(copies):
    for copy in copies:
        copy.start()
    for copy in copies:
        copy.wait()


def sigma_kernel(plan, pair_count, u, chunks, place, quads, thirds, *refs):
    moms, moments, groups = plan.moms, plan.moments, plan.groups
    half, sub, side, count = plan.half, plan.sub, plan.side, plan.moms * plan.moments
    refs = list(refs)
    take = lambda number: [refs.pop(0) for _ in range(number)]
    lesser_in, partner_in = take(moms), take(moms)
    before, outs = take(count if u else 0), take(count)
    lesser, partner, pairs, third, held, in_sems, out_sems, before_sems = refs
    x, y = place[0] // groups, place[2]
    height = sub // chunks
    copies = [[] for _ in range(chunks)]
    for chunk in range(chunks):
        rows = pl.ds(chunk * height, height)
        for which, (sources, target) in enumerate(((lesser_in, lesser), (partner_in, partner))):
            for q in range(moms):
                source = sources[q].at[:, :, rows, :]
                if q == 0:
                    start = pl.multiple_of(y * half + u * sub + chunk * height, 16)
                    source = sources[q].at[:, :, pl.ds(start, height), :]
                copy = pltpu.make_async_copy(
                    source,
                    target.at[pl.ds((y ^ q) * moments, moments), :, rows, :],
                    in_sems.at[(chunk * 2 + which) * moms + q],
                )
                copy.start()
                copies[chunk].append(copy)
    earlier = [
        pltpu.make_async_copy(
            before[n], held.at[n, :, pl.ds(0, u * sub), :], before_sems.at[n]
        )
        for n in range(len(before))
    ]
    for copy in earlier:
        copy.start()
    scale = 1.0 / pair_count
    lanes = 128 if side % 128 == 0 else side
    order = [(q, b) for q in reversed(range(moms)) for b in range(moments)]
    sent = []
    for chunk in range(chunks):
        for copy in copies[chunk]:
            copy.wait()

        def block(index, _, chunk=chunk):
            row = chunk * height + index * 16
            rows = pl.ds(pl.multiple_of(row, 16), 16)
            for c in range(count):
                for p in range(2):
                    third[c, p] = partner[c, p, rows, :].astype(jnp.float32)
            n = 0
            for a in range(count):
                for b in range(a + 1):
                    for lane in range(0, side, lanes):
                        cols = pl.ds(lane, lanes)
                        a_re = lesser[a, 0, rows, cols].astype(jnp.float32)
                        a_im = lesser[a, 1, rows, cols].astype(jnp.float32)
                        b_re = lesser[b, 0, rows, cols].astype(jnp.float32)
                        b_im = lesser[b, 1, rows, cols].astype(jnp.float32)
                        pairs[n, 0, :, cols] = a_re * b_re - a_im * b_im
                        pairs[n, 1, :, cols] = a_re * b_im + a_im * b_re
                    n += 1
            for q, b in order:
                moment = (y ^ q) * moments + (x ^ b)
                to = pl.ds(pl.multiple_of(u * sub + row, 16), 16)
                for lane in range(0, side, lanes):
                    cols = pl.ds(lane, lanes)
                    total_re = total_im = None
                    for m in range(pair_count):
                        quad, c = quads[moment, m], thirds[moment, m]
                        p_re, p_im = pairs[quad, 0, :, cols], pairs[quad, 1, :, cols]
                        c_re, c_im = third[c, 0, :, cols], third[c, 1, :, cols]
                        f_re = p_re * c_re - p_im * c_im
                        f_im = p_re * c_im + p_im * c_re
                        total_re = f_re if total_re is None else total_re + f_re
                        total_im = f_im if total_im is None else total_im + f_im
                    held[q * moments + b, 0, to, cols] = (total_re * scale).astype(jnp.bfloat16)
                    held[q * moments + b, 1, to, cols] = (total_im * scale).astype(jnp.bfloat16)
            return 0

        lax.fori_loop(0, height // 16, block, 0)
        for index in range(count):
            rows = pl.ds(u * sub + chunk * height, height)
            copy = pltpu.make_async_copy(
                held.at[index, :, rows, :], outs[index].at[:, rows, :], out_sems.at[chunk * count + index]
            )
            copy.start()
            sent.append(copy)
    for copy in earlier:
        copy.wait()
    for n in range(len(before)):
        rows = pl.ds(0, u * sub)
        copy = pltpu.make_async_copy(
            held.at[n, :, rows, :], outs[n].at[:, rows, :], before_sems.at[n]
        )
        copy.start()
        sent.append(copy)
    for copy in sent:
        copy.wait()


def place_kernel(plan, place, *refs):
    ins, out, sems = refs[:-2], refs[-2], refs[-1]
    x, y = place[0] // plan.groups, place[2]
    copies = []
    for k, (q, first, height) in enumerate(plan.chunks):
        rows = pl.ds(pl.multiple_of((y ^ q) * plan.half + first, 16), height)
        for b in range(plan.moments):
            index = k * plan.moments + b
            copies.append(pltpu.make_async_copy(ins[index], out.at[x ^ b, :, rows, :], sems.at[index]))
    run_copies(copies)


def solve_kernel(plan, sources, place, *refs):
    rows, moms, groups, side = plan.rows, plan.moms, plan.groups, plan.side
    moments, half, width, keys = plan.moments, plan.half, plan.width, plan.keys
    top = moments - 1
    diag, right = refs[:rows], refs[rows : 2 * rows]
    sig_in, outs = refs[2 * rows : -rows - 4], refs[-rows - 4 : -4]
    sig, solved, sems, out_sems = refs[-4:]
    r, y = place[0], place[2]
    g = r % groups
    for key in sorted(keys, key=lambda key: key[0]):
        for col in range(plan.cols):

            @pl.when(place[1] == col)
            def _(key=key, col=col):
                for t in range(groups):
                    row = key[0] * groups + (g ^ t)
                    for k, (q, first, height) in enumerate(plan.chunks):
                        index, start = sources[key, col, k, t]
                        at = pl.ds(pl.multiple_of((y ^ q) * half + first, 16), height)
                        for p in range(2):
                            lane = pl.ds((2 * key[1] + p) * side, side)
                            pltpu.make_async_copy(
                                sig_in[index].at[p, pl.ds(start, height), :],
                                sig.at[row, at, lane],
                                sems.at[key[0]],
                            ).start()

    weight = 1.0 / math.sqrt(side * rows)

    def pick(held, number):
        value = held[0][...]
        for n in range(1, len(held)):
            value = jnp.where(number == n, held[n][...], value)
        return value

    def turn(value):
        return jnp.concatenate([-value[:, width:], value[:, :width]], axis=1)

    for row in range(rows):
        if row == max(1, row // groups * groups):
            for key in keys:
                if key[0] == row // groups:
                    for _ in range(groups * 2):
                        tile = sig.at[0, :, pl.ds(0, side)]
                        pltpu.make_async_copy(tile, tile, sems.at[key[0]]).wait()
        pending = pick(right, r ^ row).astype(jnp.float32)
        if row > 0:
            depth = 2 * side * row
            pending = pending + weight * jnp.dot(
                sig[row, :, :depth], solved[:depth, :], preferred_element_type=jnp.float32
            )
        both = jnp.concatenate([pending, turn(pending)], axis=0).astype(jnp.bfloat16)
        value = jnp.dot(
            pick(diag[row // groups * groups :][:groups], g ^ (row % groups)),
            both,
            preferred_element_type=jnp.float32,
        )
        solved[pl.ds(2 * row * side, side), :] = value.astype(jnp.bfloat16)
        solved[pl.ds((2 * row + 1) * side, side), :] = turn(value).astype(jnp.bfloat16)
        for s in range(rows):

            @pl.when((r ^ s) == row)
            def _(s=s, row=row):
                at = pl.ds(2 * row * side, side)
                pltpu.make_async_copy(solved.at[at, :], outs[s], out_sems.at[s]).start()

    for s in range(rows):
        pltpu.make_async_copy(solved.at[pl.ds(0, side), :], outs[s], out_sems.at[s]).wait()


def after(value, *others):
    return lax.optimization_barrier((value, others))[0]


def on_device(mesh, lesser, greater, triples, diag_inverse, right_side):
    moments, _, side, _ = lesser.shape
    plan = Plan(mesh, moments, side)
    rows, cols, moms, groups = plan.rows, plan.cols, plan.moms, plan.groups
    half, width = plan.half, plan.width
    pair_count = triples.shape[1]
    count = moms * moments
    r, z, y = (lax.axis_index(axis) for axis in AXES)
    x = r // groups
    place = jnp.stack([r, z, y]).astype(jnp.int32)
    bf16, f32 = jnp.bfloat16, jnp.float32
    params = pltpu.CompilerParams(vmem_limit_bytes=VMEM_BYTES)
    dma = lambda *shape: pltpu.SemaphoreType.DMA(shape)

    def exchange_mom(value, q):
        return plan.send(value, lambda a, b, c: (a, b, c ^ q))

    def exchange_row(value, s):
        return plan.send(value, lambda a, b, c: (a ^ s, b, c))

    def by_block(came):
        return [lax.select_n(x ^ b, *came) for b in range(moments)]

    def part_of(value, q, u):
        return lax.dynamic_slice_in_dim(value, (y ^ q) * half + u * plan.sub, plan.sub, 2)

    parts = [part_of(lesser, q, 0) for q in range(1, moms)]
    greater, diag_inverse, right_side = after((greater, diag_inverse, right_side), parts)
    lesser_came = [[exchange_mom(parts[q - 1], q) for q in range(1, moms)]]
    partner = jnp.swapaxes(greater, 2, 3)
    parts = [part_of(partner, q, 0) for q in range(1, moms)]
    diag_inverse, right_side = after((diag_inverse, right_side), parts)
    partner_came = [[exchange_mom(parts[q - 1], q) for q in range(1, moms)]]
    for u in range(1, plan.subs):
        parts = [(part_of(lesser, q, u), part_of(partner, q, u)) for q in range(1, moms)]
        parts = after(parts, lesser_came[-1])
        lesser_came.append([exchange_mom(parts[q - 1][0], q) for q in range(1, moms)])
        partner_came.append([exchange_mom(parts[q - 1][1], q) for q in range(1, moms)])

    mine = [lax.dynamic_index_in_dim(diag_inverse, x ^ b, 0, keepdims=False) for b in range(moments)]
    diag = mine[:1] + [exchange_row(mine[b], b * groups) for b in range(1, moments)]

    right = right_side.reshape(moments, side, 2, groups, width).transpose(0, 3, 1, 2, 4)
    right = right.reshape(rows, side, 2 * width)
    right_all = [lax.dynamic_index_in_dim(right, r ^ s, 0, keepdims=False) for s in range(rows)]
    high = jnp.maximum(triples[..., 0], triples[..., 1])
    low = jnp.minimum(triples[..., 0], triples[..., 1])
    quads, thirds = high * (high + 1) // 2 + low, triples[..., 2]
    copies = 2 if plan.sub % 32 == 0 else 1
    came = []
    whole = []
    so_far = []

    def self_energy(u, *behind):
        height = (u + 1) * plan.sub
        shapes = [(2, height, side)] * count
        return pl.pallas_call(
            functools.partial(sigma_kernel, plan, pair_count, u, copies),
            out_shape=[jax.ShapeDtypeStruct(shape, bf16) for shape in shapes],
            in_specs=[smem()] * 3 + hbm(2 * moms + len(so_far)),
            out_specs=hbm(count),
            scratch_shapes=[
                pltpu.VMEM((count, 2, plan.sub, side), bf16),
                pltpu.VMEM((count, 2, plan.sub, side), bf16),
                pltpu.VMEM((count * (count + 1) // 2, 2, 16, side), f32),
                pltpu.VMEM((count, 2, 16, side), f32),
                pltpu.VMEM((count, 2, height, side), bf16),
                dma(copies * 2 * moms),
                dma(copies * count),
                dma(count),
            ],
            compiler_params=params,
            name="self_energy",
        )(
            *after((place, quads, thirds), behind),
            *([lesser] + lesser_came[u]),
            *([partner] + partner_came[u]),
            *so_far,
        )

    def to_row(value, b, q):
        goal = lambda a, c, m: (a ^ (b * groups), c, m ^ q) if a > c else None
        return plan.send(value, goal)

    for u in range(plan.subs):
        so_far = list(self_energy(u, right_all, diag))
    came.append(so_far[:1] + [to_row(so_far[b], b, 0) for b in range(1, moments)])
    whole += so_far[:moments]
    late = []
    for q in range(1, moms):
        mine = so_far[q * moments : (q + 1) * moments]
        came.append(
            [exchange_mom(mine[0], q)] + [to_row(mine[b], b, q) for b in range(1, moments)]
        )
        late += [(came[-1][0], None)] + [(mine[b], q) for b in range(1, moments)]
    right_all = after(right_all, came[-1])
    right_all = right_all[:1] + [exchange_row(right_all[s], s) for s in range(1, rows)]
    diag = after(by_block(diag), came[-1])
    diag = [jnp.concatenate([value[0], value[1]], axis=1) for value in diag]
    diag_all = [
        diag[b] if t == 0 else exchange_row(diag[b], t) for b in range(moments) for t in range(groups)
    ]

    def valid(key, a):
        return key[0] * groups + a % groups > key[1]

    found = {}
    own = [by_block(tiles) for tiles in came]
    both = [jnp.concatenate([tiles[b] for tiles in own], axis=1) for b in range(moments)]
    for key in plan.keys:
        for k in range(len(plan.chunks)):
            found[key, key[1], k] = (both[key[0]], plan.starts[k])

    def choose(values, behind):
        distinct = list({id(value): value for value in values.values()}.values())
        number = {id(value): n for n, value in enumerate(distinct)}
        distinct = after(distinct, behind)
        chosen = distinct[0]
        for col, value in values.items():
            if number[id(value)]:
                chosen = jnp.where(z == col, distinct[number[id(value)]], chosen)
        return chosen

    def shift(values, goals, behind):
        goal = lambda a, c, m: (a, goals[c][1], m) if c in goals and valid(goals[c][0], a) else None
        return plan.send(choose(values, behind), goal)

    ring, rest = plan.ring(), plan.rest()
    got = [[] for _ in plan.chunks]

    def ring_step(q, number, *behind):
        sends = {col: item for (n, col), item in ring.items() if n == number}
        values = {
            col: own[q][key[0]] if step is None else got[q][step]
            for col, (key, _, step) in sends.items()
        }
        value = shift(values, {col: item[:2] for col, item in sends.items()}, behind)
        got[q].append(value)
        for key, to, _ in sends.values():
            found[key, to, q] = (value, 0)

    def rest_step(number, *behind):
        step = rest[number]
        value = shift({col: both[key[0]] for col, (key, _) in step.items()}, step, behind)
        for key, to in step.values():
            for k in range(len(plan.chunks)):
                found[key, to, k] = (value, plan.starts[k])

    for number in range(cols - 1):
        for k in range(len(plan.chunks)):
            behind = [got[k - 1][number]] if k else []
            if number == 1 and k + 1 < len(plan.chunks):
                behind.append(came[k + 1])
            ring_step(k, number, *behind)
    for number in range(len(rest)):
        rest_step(number, got[0][1], got[-1][0], right_all)

    buffers = []

    def number_of(value):
        for index, held in enumerate(buffers):
            if held is value:
                return index
        buffers.append(value)
        return len(buffers) - 1

    sources = {name + (0,): (number_of(value), part) for name, (value, part) in found.items()}
    sig_all = list(buffers)
    for t in range(1, groups):
        for name, (value, part) in found.items():
            sources[name + (t,)] = (len(sig_all) + number_of(value), part)
        sig_all += [exchange_row(value, t) for value in buffers]

    solved = pl.pallas_call(
        functools.partial(solve_kernel, plan, sources),
        out_shape=[jax.ShapeDtypeStruct((side, 2 * width), bf16)] * rows,
        in_specs=[smem()] + [pl.BlockSpec(memory_space=pltpu.VMEM)] * (2 * rows) + hbm(len(sig_all)),
        out_specs=hbm(rows),
        scratch_shapes=[
            pltpu.VMEM((rows, side, 2 * side * (cols - 1)), bf16),
            pltpu.VMEM((rows * 2 * side, 2 * width), bf16),
            dma(moments),
            dma(rows),
        ],
        compiler_params=params,
        name="substitution",
    )(place, *diag_all, *right_all, *sig_all)

    for value, q in late:
        whole.append(value if q is None else exchange_mom(after(value, solved), q))
    sigma = pl.pallas_call(
        functools.partial(place_kernel, plan),
        out_shape=jax.ShapeDtypeStruct(lesser.shape, bf16),
        in_specs=[smem()] + hbm(len(whole)),
        scratch_shapes=[dma(len(whole))],
        compiler_params=params,
        name="place_sigma",
    )(place, *whole)

    back = [solved[0]] + [exchange_row(solved[s], s) for s in range(1, rows)]
    back = after(back, sigma)
    pieces = jnp.stack([lax.select_n(r ^ s, *back) for s in range(rows)])
    pieces = pieces.reshape(moments, groups, side, 2, width).transpose(0, 2, 3, 1, 4)
    return sigma, pieces.reshape(moments, side, 2, side)


def solution(mesh):
    placed = (
        P("mom", None, "row", "col"),
        P("mom", None, "col", "row"),
        P(),
        P("mom", None, "row", None),
        P("mom", "row", None, "col"),
    )
    return jax.shard_map(
        functools.partial(on_device, mesh),
        mesh=mesh,
        in_specs=placed,
        out_specs=(P("mom", None, "row", "col"), P("mom", "row", None, "col")),
        check_vma=False,
    )
```

```python
import functools
import itertools
import math

import jax
import jax.numpy as jnp
from jax import lax
from jax.experimental import pallas as pl
from jax.experimental.pallas import tpu as pltpu
from jax.sharding import PartitionSpec as P

AXES = ("row", "col", "mom")
VMEM_BYTES = 56 * 1024 * 1024


class Plan:
    def __init__(self, mesh, moments, side):
        self.rows = mesh.shape["row"]
        self.cols = mesh.shape["col"]
        self.moms = mesh.shape["mom"]
        self.moments = moments
        self.side = side
        self.groups = self.rows // moments
        self.half = side // self.moms
        self.width = side // self.groups
        self.subs = 2 if self.half % 32 == 0 else 1
        self.sub = self.half // self.subs
        self.chunks = [(q, 0, self.half) for q in range(self.moms)]
        self.starts = [0]
        for _, _, height in self.chunks:
            self.starts.append(self.starts[-1] + height)
        self.keys = [
            (b, j)
            for b in range(moments)
            for j in range(self.cols - 1)
            if (b + 1) * self.groups - 1 > j
        ]

    def send(self, value, target):
        pairs = []
        index = lambda r, c, m: (r * self.cols + c) * self.moms + m
        for place in itertools.product(range(self.rows), range(self.cols), range(self.moms)):
            goal = target(*place)
            if goal is not None:
                pairs.append((index(*place), index(*goal)))
        return lax.ppermute(value, AXES, pairs)

    def ring(self):
        top, last = self.moments - 1, self.cols - 1
        sends, queue = {}, []
        for col in range(last):
            queue = [((top, col), None)] + [(key, n) for n, (key, _) in enumerate(queue)]
            for n, (key, step) in enumerate(queue):
                sends[n, col] = (key, col + 1, step)
        wanted = [
            (key, to)
            for key in self.keys
            if key[0] < top
            for to in range(self.cols)
            if to not in (key[1], last)
        ]
        for key, to in wanted:
            for n in range(1, last):
                if (n, key[1]) in sends or (n, to - 1) in sends and sends[n, to - 1][1] == to:
                    continue
                if to not in [goal for (m, _), (_, goal, _) in sends.items() if m == n]:
                    sends[n, key[1]] = (key, to, None)
                    break
        return sends

    def left(self):
        top = self.moments - 1
        return {col: ((top, col), col - 1) for col in range(1, self.cols - 1)}

    def rest(self):
        done = {(key, to) for key, to, _ in self.ring().values()} | set(self.left().values())
        wanted = [
            (key, to)
            for key in self.keys
            for to in range(self.cols)
            if to != key[1] and (key, to) not in done
        ]
        steps = []
        for key, to in sorted(wanted, key=lambda item: (item[0][0], -item[1], -item[0][1])):
            for step in steps:
                if key[1] not in step and to not in [goal for _, goal in step.values()]:
                    break
            else:
                step = {}
                steps.append(step)
            step[key[1]] = (key, to)
        return steps


def hbm(count):
    return [pl.BlockSpec(memory_space=pl.ANY)] * count


def smem():
    return pl.BlockSpec(memory_space=pltpu.SMEM)


def run_copies(copies):
    for copy in copies:
        copy.start()
    for copy in copies:
        copy.wait()


def sigma_kernel(plan, pair_count, u, chunks, place, quads, thirds, *refs):
    moms, moments, groups = plan.moms, plan.moments, plan.groups
    half, sub, side, count = plan.half, plan.sub, plan.side, plan.moms * plan.moments
    refs = list(refs)
    take = lambda number: [refs.pop(0) for _ in range(number)]
    lesser_in, partner_in = take(moms), take(moms)
    before, outs = take(count if u else 0), take(count)
    lesser, partner, pairs, third, held, in_sems, out_sems, before_sems = refs
    x, y = place[0] // groups, place[2]
    height = sub // chunks
    copies = [[] for _ in range(chunks)]
    for chunk in range(chunks):
        rows = pl.ds(chunk * height, height)
        for which, (sources, target) in enumerate(((lesser_in, lesser), (partner_in, partner))):
            for q in range(moms):
                source = sources[q].at[:, :, rows, :]
                if q == 0:
                    start = pl.multiple_of(y * half + u * sub + chunk * height, 16)
                    source = sources[q].at[:, :, pl.ds(start, height), :]
                copy = pltpu.make_async_copy(
                    source,
                    target.at[pl.ds((y ^ q) * moments, moments), :, rows, :],
                    in_sems.at[(chunk * 2 + which) * moms + q],
                )
                copy.start()
                copies[chunk].append(copy)
    earlier = [
        pltpu.make_async_copy(
            before[n], held.at[n, :, pl.ds(0, u * sub), :], before_sems.at[n]
        )
        for n in range(len(before))
    ]
    for copy in earlier:
        copy.start()
    scale = 1.0 / pair_count
    lanes = 128 if side % 128 == 0 else side
    order = [(q, b) for q in reversed(range(moms)) for b in range(moments)]
    sent = []
    for chunk in range(chunks):
        for copy in copies[chunk]:
            copy.wait()

        def block(index, _, chunk=chunk):
            row = chunk * height + index * 16
            rows = pl.ds(pl.multiple_of(row, 16), 16)
            for c in range(count):
                for p in range(2):
                    third[c, p] = partner[c, p, rows, :].astype(jnp.float32)
            n = 0
            for a in range(count):
                for b in range(a + 1):
                    for lane in range(0, side, lanes):
                        cols = pl.ds(lane, lanes)
                        a_re = lesser[a, 0, rows, cols].astype(jnp.float32)
                        a_im = lesser[a, 1, rows, cols].astype(jnp.float32)
                        b_re = lesser[b, 0, rows, cols].astype(jnp.float32)
                        b_im = lesser[b, 1, rows, cols].astype(jnp.float32)
                        pairs[n, 0, :, cols] = a_re * b_re - a_im * b_im
                        pairs[n, 1, :, cols] = a_re * b_im + a_im * b_re
                    n += 1
            for q, b in order:
                moment = (y ^ q) * moments + (x ^ b)
                to = pl.ds(pl.multiple_of(u * sub + row, 16), 16)
                for lane in range(0, side, lanes):
                    cols = pl.ds(lane, lanes)
                    total_re = total_im = None
                    for m in range(pair_count):
                        quad, c = quads[moment, m], thirds[moment, m]
                        p_re, p_im = pairs[quad, 0, :, cols], pairs[quad, 1, :, cols]
                        c_re, c_im = third[c, 0, :, cols], third[c, 1, :, cols]
                        f_re = p_re * c_re - p_im * c_im
                        f_im = p_re * c_im + p_im * c_re
                        total_re = f_re if total_re is None else total_re + f_re
                        total_im = f_im if total_im is None else total_im + f_im
                    held[q * moments + b, 0, to, cols] = (total_re * scale).astype(jnp.bfloat16)
                    held[q * moments + b, 1, to, cols] = (total_im * scale).astype(jnp.bfloat16)
            return 0

        lax.fori_loop(0, height // 16, block, 0)
        for index in range(count):
            rows = pl.ds(u * sub + chunk * height, height)
            copy = pltpu.make_async_copy(
                held.at[index, :, rows, :], outs[index].at[:, rows, :], out_sems.at[chunk * count + index]
            )
            copy.start()
            sent.append(copy)
    for copy in earlier:
        copy.wait()
    for n in range(len(before)):
        rows = pl.ds(0, u * sub)
        copy = pltpu.make_async_copy(
            held.at[n, :, rows, :], outs[n].at[:, rows, :], before_sems.at[n]
        )
        copy.start()
        sent.append(copy)
    for copy in sent:
        copy.wait()


def place_kernel(plan, place, *refs):
    ins, out, sems = refs[:-2], refs[-2], refs[-1]
    x, y = place[0] // plan.groups, place[2]
    copies = []
    for k, (q, first, height) in enumerate(plan.chunks):
        rows = pl.ds(pl.multiple_of((y ^ q) * plan.half + first, 16), height)
        for b in range(plan.moments):
            index = k * plan.moments + b
            copies.append(pltpu.make_async_copy(ins[index], out.at[x ^ b, :, rows, :], sems.at[index]))
    run_copies(copies)


def solve_kernel(plan, sources, place, *refs):
    rows, moms, groups, side = plan.rows, plan.moms, plan.groups, plan.side
    moments, half, width, keys = plan.moments, plan.half, plan.width, plan.keys
    top = moments - 1
    diag, right = refs[:rows], refs[rows : 2 * rows]
    sig_in, outs = refs[2 * rows : -rows - 4], refs[-rows - 4 : -4]
    sig, solved, sems, out_sems = refs[-4:]
    r, y = place[0], place[2]
    g = r % groups
    for key in sorted(keys, key=lambda key: key[0]):
        for col in range(plan.cols):

            @pl.when(place[1] == col)
            def _(key=key, col=col):
                for t in range(groups):
                    row = key[0] * groups + (g ^ t)
                    for k, (q, first, height) in enumerate(plan.chunks):
                        index, start = sources[key, col, k, t]
                        at = pl.ds(pl.multiple_of((y ^ q) * half + first, 16), height)
                        for p in range(2):
                            lane = pl.ds((2 * key[1] + p) * side, side)
                            pltpu.make_async_copy(
                                sig_in[index].at[p, pl.ds(start, height), :],
                                sig.at[row, at, lane],
                                sems.at[key[0]],
                            ).start()

    weight = 1.0 / math.sqrt(side * rows)

    def pick(held, number):
        value = held[0][...]
        for n in range(1, len(held)):
            value = jnp.where(number == n, held[n][...], value)
        return value

    def turn(value):
        return jnp.concatenate([-value[:, width:], value[:, :width]], axis=1)

    for row in range(rows):
        if row == max(1, row // groups * groups):
            for key in keys:
                if key[0] == row // groups:
                    for _ in range(groups * 2):
                        tile = sig.at[0, :, pl.ds(0, side)]
                        pltpu.make_async_copy(tile, tile, sems.at[key[0]]).wait()
        pending = pick(right, r ^ row).astype(jnp.float32)
        if row > 0:
            depth = 2 * side * row
            pending = pending + weight * jnp.dot(
                sig[row, :, :depth], solved[:depth, :], preferred_element_type=jnp.float32
            )
        both = jnp.concatenate([pending, turn(pending)], axis=0).astype(jnp.bfloat16)
        value = jnp.dot(
            pick(diag[row // groups * groups :][:groups], g ^ (row % groups)),
            both,
            preferred_element_type=jnp.float32,
        )
        solved[pl.ds(2 * row * side, side), :] = value.astype(jnp.bfloat16)
        solved[pl.ds((2 * row + 1) * side, side), :] = turn(value).astype(jnp.bfloat16)
        for s in range(rows):

            @pl.when((r ^ s) == row)
            def _(s=s, row=row):
                at = pl.ds(2 * row * side, side)
                pltpu.make_async_copy(solved.at[at, :], outs[s], out_sems.at[s]).start()

    for s in range(rows):
        pltpu.make_async_copy(solved.at[pl.ds(0, side), :], outs[s], out_sems.at[s]).wait()


def after(value, *others):
    return lax.optimization_barrier((value, others))[0]


def spread_kernel(plan, place, *refs):
    groups, width = plan.groups, plan.width
    ins, out, held, sems = refs[:-3], refs[-3], refs[-2], refs[-1]
    run_copies(
        [
            pltpu.make_async_copy(ins[s], held.at[place[0] ^ s], sems.at[s])
            for s in range(plan.rows)
        ]
    )
    for m in range(plan.moments):
        parts = [held[m * groups + g] for g in range(groups)]
        for p in range(2):
            out[m, :, p, :] = jnp.concatenate(
                [part[:, p * width : (p + 1) * width] for part in parts], axis=1
            )


def on_device(mesh, lesser, greater, triples, diag_inverse, right_side):
    moments, _, side, _ = lesser.shape
    plan = Plan(mesh, moments, side)
    rows, cols, moms, groups = plan.rows, plan.cols, plan.moms, plan.groups
    half, width = plan.half, plan.width
    pair_count = triples.shape[1]
    count = moms * moments
    r, z, y = (lax.axis_index(axis) for axis in AXES)
    x = r // groups
    place = jnp.stack([r, z, y]).astype(jnp.int32)
    bf16, f32 = jnp.bfloat16, jnp.float32
    params = pltpu.CompilerParams(vmem_limit_bytes=VMEM_BYTES)
    dma = lambda *shape: pltpu.SemaphoreType.DMA(shape)

    def exchange_mom(value, q):
        return plan.send(value, lambda a, b, c: (a, b, c ^ q))

    def exchange_row(value, s):
        return plan.send(value, lambda a, b, c: (a ^ s, b, c))

    def by_block(came):
        return [lax.select_n(x ^ b, *came) for b in range(moments)]

    def part_of(value, q, u):
        return lax.dynamic_slice_in_dim(value, (y ^ q) * half + u * plan.sub, plan.sub, 2)

    parts = [part_of(lesser, q, 0) for q in range(1, moms)]
    greater, diag_inverse, right_side = after((greater, diag_inverse, right_side), parts)
    lesser_came = [[exchange_mom(parts[q - 1], q) for q in range(1, moms)]]
    partner = jnp.swapaxes(greater, 2, 3)
    parts = [part_of(partner, q, 0) for q in range(1, moms)]
    diag_inverse, right_side = after((diag_inverse, right_side), parts)
    partner_came = [[exchange_mom(parts[q - 1], q) for q in range(1, moms)]]
    for u in range(1, plan.subs):
        parts = [(part_of(lesser, q, u), part_of(partner, q, u)) for q in range(1, moms)]
        parts = after(parts, lesser_came[-1])
        lesser_came.append([exchange_mom(parts[q - 1][0], q) for q in range(1, moms)])
        partner_came.append([exchange_mom(parts[q - 1][1], q) for q in range(1, moms)])

    mine = [lax.dynamic_index_in_dim(diag_inverse, x ^ b, 0, keepdims=False) for b in range(moments)]
    diag = mine[:1] + [exchange_row(mine[b], b * groups) for b in range(1, moments)]

    right = right_side.reshape(moments, side, 2, groups, width).transpose(0, 3, 1, 2, 4)
    right = right.reshape(rows, side, 2 * width)
    right_all = [lax.dynamic_index_in_dim(right, r ^ s, 0, keepdims=False) for s in range(rows)]
    high = jnp.maximum(triples[..., 0], triples[..., 1])
    low = jnp.minimum(triples[..., 0], triples[..., 1])
    quads, thirds = high * (high + 1) // 2 + low, triples[..., 2]
    copies = 2 if plan.sub % 32 == 0 else 1
    came = []
    whole = []
    so_far = []

    def self_energy(u, *behind):
        height = (u + 1) * plan.sub
        shapes = [(2, height, side)] * count
        return pl.pallas_call(
            functools.partial(sigma_kernel, plan, pair_count, u, copies),
            out_shape=[jax.ShapeDtypeStruct(shape, bf16) for shape in shapes],
            in_specs=[smem()] * 3 + hbm(2 * moms + len(so_far)),
            out_specs=hbm(count),
            scratch_shapes=[
                pltpu.VMEM((count, 2, plan.sub, side), bf16),
                pltpu.VMEM((count, 2, plan.sub, side), bf16),
                pltpu.VMEM((count * (count + 1) // 2, 2, 16, side), f32),
                pltpu.VMEM((count, 2, 16, side), f32),
                pltpu.VMEM((count, 2, height, side), bf16),
                dma(copies * 2 * moms),
                dma(copies * count),
                dma(count),
            ],
            compiler_params=params,
            name="self_energy",
        )(
            *after((place, quads, thirds), behind),
            *([lesser] + lesser_came[u]),
            *([partner] + partner_came[u]),
            *so_far,
        )

    def to_row(value, b, q):
        goal = lambda a, c, m: (a ^ (b * groups), c, m ^ q) if a > c else None
        return plan.send(value, goal)

    for u in range(plan.subs):
        so_far = list(self_energy(u, right_all, diag))
    came.append(so_far[:1] + [to_row(so_far[b], b, 0) for b in range(1, moments)])
    whole += so_far[:moments]
    late = []
    for q in range(1, moms):
        mine = so_far[q * moments : (q + 1) * moments]
        came.append(
            [exchange_mom(mine[0], q)] + [to_row(mine[b], b, q) for b in range(1, moments)]
        )
        late += [(came[-1][0], None)] + [(mine[b], q) for b in range(1, moments)]
    right_all = after(right_all, came[-1])
    right_all = right_all[:1] + [exchange_row(right_all[s], s) for s in range(1, rows)]
    diag = after(by_block(diag), came[-1])
    diag = [jnp.concatenate([value[0], value[1]], axis=1) for value in diag]
    diag_all = [
        diag[b] if t == 0 else exchange_row(diag[b], t) for b in range(moments) for t in range(groups)
    ]

    def valid(key, a):
        return key[0] * groups + a % groups > key[1]

    found = {}
    own = [by_block(tiles) for tiles in came]
    both = [jnp.concatenate([tiles[b] for tiles in own], axis=1) for b in range(moments)]
    for key in plan.keys:
        for k in range(len(plan.chunks)):
            found[key, key[1], k] = (both[key[0]], plan.starts[k])

    def choose(values, behind):
        distinct = list({id(value): value for value in values.values()}.values())
        number = {id(value): n for n, value in enumerate(distinct)}
        distinct = after(distinct, behind)
        chosen = distinct[0]
        for col, value in values.items():
            if number[id(value)]:
                chosen = jnp.where(z == col, distinct[number[id(value)]], chosen)
        return chosen

    def shift(values, goals, behind):
        goal = lambda a, c, m: (a, goals[c][1], m) if c in goals and valid(goals[c][0], a) else None
        return plan.send(choose(values, behind), goal)

    top, ring, rest = moments - 1, plan.ring(), plan.rest()
    got = [[] for _ in plan.chunks]

    def ring_step(q, number, *behind):
        sends = {col: item for (n, col), item in ring.items() if n == number}
        values = {
            col: own[q][key[0]] if step is None else got[q][step]
            for col, (key, _, step) in sends.items()
        }
        value = shift(values, {col: item[:2] for col, item in sends.items()}, behind)
        got[q].append(value)
        for key, to, _ in sends.values():
            found[key, to, q] = (value, 0)

    def left_step(k):
        value = shift({col: own[k][top] for col in plan.left()}, plan.left(), ())
        for key, to in plan.left().values():
            found[key, to, k] = (value, 0)
        return value

    def rest_step(number, *behind):
        step = rest[number]
        value = shift({col: both[key[0]] for col, (key, _) in step.items()}, step, behind)
        for key, to in step.values():
            for k in range(len(plan.chunks)):
                found[key, to, k] = (value, plan.starts[k])

    lefts = [left_step(k) for k in range(len(plan.chunks))]
    for number in range(cols - 1):
        for k in range(len(plan.chunks)):
            behind = [got[k - 1][number]] if k else []
            if number == 1 and k + 1 < len(plan.chunks):
                behind.append(came[k + 1])
            if number == 1:
                behind.append(lefts[k])
            ring_step(k, number, *behind)
    for number in range(len(rest)):
        rest_step(number, got[0][1], got[-1][0], right_all)

    buffers = []

    def number_of(value):
        for index, held in enumerate(buffers):
            if held is value:
                return index
        buffers.append(value)
        return len(buffers) - 1

    sources = {name + (0,): (number_of(value), part) for name, (value, part) in found.items()}
    sig_all = list(buffers)
    for t in range(1, groups):
        for name, (value, part) in found.items():
            sources[name + (t,)] = (len(sig_all) + number_of(value), part)
        sig_all += [exchange_row(value, t) for value in buffers]

    solved = pl.pallas_call(
        functools.partial(solve_kernel, plan, sources),
        out_shape=[jax.ShapeDtypeStruct((side, 2 * width), bf16)] * rows,
        in_specs=[smem()] + [pl.BlockSpec(memory_space=pltpu.VMEM)] * (2 * rows) + hbm(len(sig_all)),
        out_specs=hbm(rows),
        scratch_shapes=[
            pltpu.VMEM((rows, side, 2 * side * (cols - 1)), bf16),
            pltpu.VMEM((rows * 2 * side, 2 * width), bf16),
            dma(moments),
            dma(rows),
        ],
        compiler_params=params,
        name="substitution",
    )(place, *diag_all, *right_all, *sig_all)

    for value, q in late:
        whole.append(value if q is None else exchange_mom(after(value, solved), q))
    sigma = pl.pallas_call(
        functools.partial(place_kernel, plan),
        out_shape=jax.ShapeDtypeStruct(lesser.shape, bf16),
        in_specs=[smem()] + hbm(len(whole)),
        scratch_shapes=[dma(len(whole))],
        compiler_params=params,
        name="place_sigma",
    )(place, *whole)

    back = [solved[0]] + [exchange_row(solved[s], s) for s in range(1, rows)]
    back = after(back, sigma)
    spread = pl.pallas_call(
        functools.partial(spread_kernel, plan),
        out_shape=jax.ShapeDtypeStruct(right_side.shape, bf16),
        in_specs=[smem()] + hbm(rows),
        scratch_shapes=[pltpu.VMEM((rows, side, 2 * width), bf16), dma(rows)],
        compiler_params=params,
        name="place_solution",
    )
    return sigma, spread(place, *back)


def solution(mesh):
    placed = (
        P("mom", None, "row", "col"),
        P("mom", None, "col", "row"),
        P(),
        P("mom", None, "row", None),
        P("mom", "row", None, "col"),
    )
    return jax.shard_map(
        functools.partial(on_device, mesh),
        mesh=mesh,
        in_specs=placed,
        out_specs=(P("mom", None, "row", "col"), P("mom", "row", None, "col")),
        check_vma=False,
    )
```

```python
import functools
import itertools
import math

import jax
import jax.numpy as jnp
from jax import lax
from jax.experimental import pallas as pl
from jax.experimental.pallas import tpu as pltpu
from jax.sharding import PartitionSpec as P

AXES = ("row", "col", "mom")
VMEM_BYTES = 60 * 1024 * 1024


class Plan:
    def __init__(self, mesh, moments, side):
        self.rows = mesh.shape["row"]
        self.cols = mesh.shape["col"]
        self.moms = mesh.shape["mom"]
        self.moments = moments
        self.side = side
        self.groups = self.rows // moments
        self.half = side // self.moms
        self.width = side // self.groups
        self.subs = 2 if self.half % 32 == 0 else 1
        self.sub = self.half // self.subs
        self.chunks = [(q, 0, self.half) for q in range(self.moms)]
        self.starts = [0]
        for _, _, height in self.chunks:
            self.starts.append(self.starts[-1] + height)
        self.keys = [
            (b, j)
            for b in range(moments)
            for j in range(self.cols - 1)
            if (b + 1) * self.groups - 1 > j
        ]

    def send(self, value, target):
        pairs = []
        index = lambda r, c, m: (r * self.cols + c) * self.moms + m
        for place in itertools.product(range(self.rows), range(self.cols), range(self.moms)):
            goal = target(*place)
            if goal is not None:
                pairs.append((index(*place), index(*goal)))
        return lax.ppermute(value, AXES, pairs)

    def ring(self):
        top, last = self.moments - 1, self.cols - 1
        sends, queue = {}, []
        for col in range(last):
            queue = [((top, col), None)] + [(key, n) for n, (key, _) in enumerate(queue)]
            for n, (key, step) in enumerate(queue):
                sends[n, col] = (key, col + 1, step)
        wanted = [
            (key, to)
            for key in self.keys
            if key[0] < top
            for to in range(self.cols)
            if to not in (key[1], last)
        ]
        for key, to in wanted:
            for n in range(1, last):
                if (n, key[1]) in sends or (n, to - 1) in sends and sends[n, to - 1][1] == to:
                    continue
                if to not in [goal for (m, _), (_, goal, _) in sends.items() if m == n]:
                    sends[n, key[1]] = (key, to, None)
                    break
        return sends

    def rest(self):
        done = {(key, to) for key, to, _ in self.ring().values()}
        wanted = [
            (key, to)
            for key in self.keys
            for to in range(self.cols)
            if to != key[1] and (key, to) not in done
        ]
        steps = []
        for key, to in sorted(wanted, key=lambda item: (item[0][0], -item[1], -item[0][1])):
            for step in steps:
                free = key[1] not in step and to not in [goal for _, goal in step.values()]
                if free and all(other[0] == key[0] for other, _ in step.values()):
                    break
            else:
                step = {}
                steps.append(step)
            step[key[1]] = (key, to)
        return steps


def hbm(count):
    return [pl.BlockSpec(memory_space=pl.ANY)] * count


def smem():
    return pl.BlockSpec(memory_space=pltpu.SMEM)


def run_copies(copies):
    for copy in copies:
        copy.start()
    for copy in copies:
        copy.wait()


def sigma_kernel(plan, pair_count, u, chunks, place, quads, thirds, *refs):
    moms, moments, groups = plan.moms, plan.moments, plan.groups
    half, sub, side, count = plan.half, plan.sub, plan.side, plan.moms * plan.moments
    refs = list(refs)
    take = lambda number: [refs.pop(0) for _ in range(number)]
    lesser_in, partner_in = take(moms), take(moms)
    before, outs = take(count if u else 0), take(count)
    lesser, partner, pairs, third, held, in_sems, out_sems, before_sems = refs
    x, y = place[0] // groups, place[2]
    height = sub // chunks
    copies = [[] for _ in range(chunks)]
    for chunk in range(chunks):
        rows = pl.ds(chunk * height, height)
        for which, (sources, target) in enumerate(((lesser_in, lesser), (partner_in, partner))):
            for q in range(moms):
                source = sources[q].at[:, :, rows, :]
                if q == 0:
                    start = pl.multiple_of(y * half + u * sub + chunk * height, 16)
                    source = sources[q].at[:, :, pl.ds(start, height), :]
                copy = pltpu.make_async_copy(
                    source,
                    target.at[pl.ds((y ^ q) * moments, moments), :, rows, :],
                    in_sems.at[(chunk * 2 + which) * moms + q],
                )
                copy.start()
                copies[chunk].append(copy)
    earlier = [
        pltpu.make_async_copy(
            before[n], held.at[n, :, pl.ds(0, u * sub), :], before_sems.at[n]
        )
        for n in range(len(before))
    ]
    for copy in earlier:
        copy.start()
    scale = 1.0 / pair_count
    lanes = 128 if side % 128 == 0 else side
    order = [(q, b) for q in reversed(range(moms)) for b in range(moments)]
    sent = []
    for chunk in range(chunks):
        for copy in copies[chunk]:
            copy.wait()

        def block(index, _, chunk=chunk):
            row = chunk * height + index * 16
            rows = pl.ds(pl.multiple_of(row, 16), 16)
            for c in range(count):
                for p in range(2):
                    third[c, p] = partner[c, p, rows, :].astype(jnp.float32)
            n = 0
            for a in range(count):
                for b in range(a + 1):
                    for lane in range(0, side, lanes):
                        cols = pl.ds(lane, lanes)
                        a_re = lesser[a, 0, rows, cols].astype(jnp.float32)
                        a_im = lesser[a, 1, rows, cols].astype(jnp.float32)
                        b_re = lesser[b, 0, rows, cols].astype(jnp.float32)
                        b_im = lesser[b, 1, rows, cols].astype(jnp.float32)
                        pairs[n, 0, :, cols] = a_re * b_re - a_im * b_im
                        pairs[n, 1, :, cols] = a_re * b_im + a_im * b_re
                    n += 1
            for q, b in order:
                moment = (y ^ q) * moments + (x ^ b)
                to = pl.ds(pl.multiple_of(u * sub + row, 16), 16)
                for lane in range(0, side, lanes):
                    cols = pl.ds(lane, lanes)
                    total_re = total_im = None
                    for m in range(pair_count):
                        quad, c = quads[moment, m], thirds[moment, m]
                        p_re, p_im = pairs[quad, 0, :, cols], pairs[quad, 1, :, cols]
                        c_re, c_im = third[c, 0, :, cols], third[c, 1, :, cols]
                        f_re = p_re * c_re - p_im * c_im
                        f_im = p_re * c_im + p_im * c_re
                        total_re = f_re if total_re is None else total_re + f_re
                        total_im = f_im if total_im is None else total_im + f_im
                    held[q * moments + b, 0, to, cols] = (total_re * scale).astype(jnp.bfloat16)
                    held[q * moments + b, 1, to, cols] = (total_im * scale).astype(jnp.bfloat16)
            return 0

        lax.fori_loop(0, height // 16, block, 0)
        for index in range(count):
            rows = pl.ds(u * sub + chunk * height, height)
            copy = pltpu.make_async_copy(
                held.at[index, :, rows, :], outs[index].at[:, rows, :], out_sems.at[chunk * count + index]
            )
            copy.start()
            sent.append(copy)
    for copy in earlier:
        copy.wait()
    for n in range(len(before)):
        rows = pl.ds(0, u * sub)
        copy = pltpu.make_async_copy(
            held.at[n, :, rows, :], outs[n].at[:, rows, :], before_sems.at[n]
        )
        copy.start()
        sent.append(copy)
    for copy in sent:
        copy.wait()


def place_kernel(plan, place, *refs):
    ins, out, sems = refs[:-2], refs[-2], refs[-1]
    x, y = place[0] // plan.groups, place[2]
    copies = []
    for k, (q, first, height) in enumerate(plan.chunks):
        rows = pl.ds(pl.multiple_of((y ^ q) * plan.half + first, 16), height)
        for b in range(plan.moments):
            index = k * plan.moments + b
            copies.append(pltpu.make_async_copy(ins[index], out.at[x ^ b, :, rows, :], sems.at[index]))
    run_copies(copies)


def solve_kernel(plan, sources, place, *refs):
    rows, moms, groups, side = plan.rows, plan.moms, plan.groups, plan.side
    moments, half, width, keys = plan.moments, plan.half, plan.width, plan.keys
    top = moments - 1
    diag, right = refs[:rows], refs[rows : 2 * rows]
    sig_in, outs = refs[2 * rows : -rows - 4], refs[-rows - 4 : -4]
    sig, solved, sems, out_sems = refs[-4:]
    r, y = place[0], place[2]
    g = r % groups
    for key in sorted(keys, key=lambda key: key[0]):
        for col in range(plan.cols):

            @pl.when(place[1] == col)
            def _(key=key, col=col):
                for t in range(groups):
                    row = key[0] * groups + (g ^ t)
                    for k, (q, first, height) in enumerate(plan.chunks):
                        index, start = sources[key, col, k, t]
                        at = pl.ds(pl.multiple_of((y ^ q) * half + first, 16), height)
                        for p in range(2):
                            lane = pl.ds((2 * key[1] + p) * side, side)
                            pltpu.make_async_copy(
                                sig_in[index].at[p, pl.ds(start, height), :],
                                sig.at[row, at, lane],
                                sems.at[key[0]],
                            ).start()

    weight = 1.0 / math.sqrt(side * rows)

    def turn(value):
        return jnp.concatenate([-value[:, width:], value[:, :width]], axis=1)

    for row in range(rows):
        if row == max(1, row // groups * groups):
            for key in keys:
                if key[0] == row // groups:
                    for _ in range(groups * 2):
                        tile = sig.at[0, :, pl.ds(0, side)]
                        pltpu.make_async_copy(tile, tile, sems.at[key[0]]).wait()
        pending = pick(right, r ^ row).astype(jnp.float32)
        if row > 0:
            depth = 2 * side * row
            pending = pending + weight * jnp.dot(
                sig[row, :, :depth], solved[:depth, :], preferred_element_type=jnp.float32
            )
        both = jnp.concatenate([pending, turn(pending)], axis=0).astype(jnp.bfloat16)
        value = jnp.dot(
            pick(diag[row // groups * groups :][:groups], g ^ (row % groups)),
            both,
            preferred_element_type=jnp.float32,
        )
        solved[pl.ds(2 * row * side, side), :] = value.astype(jnp.bfloat16)
        solved[pl.ds((2 * row + 1) * side, side), :] = turn(value).astype(jnp.bfloat16)
        for s in range(rows):

            @pl.when((r ^ s) == row)
            def _(s=s, row=row):
                at = pl.ds(2 * row * side, side)
                pltpu.make_async_copy(solved.at[at, :], outs[s], out_sems.at[s]).start()

    for s in range(rows):
        pltpu.make_async_copy(solved.at[pl.ds(0, side), :], outs[s], out_sems.at[s]).wait()


def after(value, *others):
    return lax.optimization_barrier((value, others))[0]


def pick(held, number):
    value = held[0][...]
    for n in range(1, len(held)):
        value = jnp.where(number == n, held[n][...], value)
    return value


def spread_kernel(plan, place, *refs):
    groups, width = plan.groups, plan.width
    ins, out = refs[:-1], refs[-1]
    for m in range(plan.moments):
        parts = [pick(ins, place[0] ^ (m * groups + g)) for g in range(groups)]
        for p in range(2):
            out[m, :, p, :] = jnp.concatenate(
                [part[:, p * width : (p + 1) * width] for part in parts], axis=1
            )


def on_device(mesh, lesser, greater, triples, diag_inverse, right_side):
    moments, _, side, _ = lesser.shape
    plan = Plan(mesh, moments, side)
    rows, cols, moms, groups = plan.rows, plan.cols, plan.moms, plan.groups
    half, width = plan.half, plan.width
    pair_count = triples.shape[1]
    count = moms * moments
    r, z, y = (lax.axis_index(axis) for axis in AXES)
    x = r // groups
    place = jnp.stack([r, z, y]).astype(jnp.int32)
    bf16, f32 = jnp.bfloat16, jnp.float32
    params = pltpu.CompilerParams(vmem_limit_bytes=VMEM_BYTES)
    dma = lambda *shape: pltpu.SemaphoreType.DMA(shape)

    def exchange_mom(value, q):
        return plan.send(value, lambda a, b, c: (a, b, c ^ q))

    def exchange_row(value, s):
        return plan.send(value, lambda a, b, c: (a ^ s, b, c))

    def by_block(came):
        return [lax.select_n(x ^ b, *came) for b in range(moments)]

    def part_of(value, q, u):
        return lax.dynamic_slice_in_dim(value, (y ^ q) * half + u * plan.sub, plan.sub, 2)

    parts = [part_of(lesser, q, 0) for q in range(1, moms)]
    greater, diag_inverse, right_side = after((greater, diag_inverse, right_side), parts)
    lesser_came = [[exchange_mom(parts[q - 1], q) for q in range(1, moms)]]
    partner = jnp.swapaxes(greater, 2, 3)
    parts = [part_of(partner, q, 0) for q in range(1, moms)]
    diag_inverse, right_side = after((diag_inverse, right_side), parts)
    partner_came = [[exchange_mom(parts[q - 1], q) for q in range(1, moms)]]
    for u in range(1, plan.subs):
        parts = [(part_of(lesser, q, u), part_of(partner, q, u)) for q in range(1, moms)]
        parts = after(parts, lesser_came[-1])
        lesser_came.append([exchange_mom(parts[q - 1][0], q) for q in range(1, moms)])
        partner_came.append([exchange_mom(parts[q - 1][1], q) for q in range(1, moms)])

    mine = [lax.dynamic_index_in_dim(diag_inverse, x ^ b, 0, keepdims=False) for b in range(moments)]
    diag = mine[:1] + [exchange_row(mine[b], b * groups) for b in range(1, moments)]

    right = right_side.reshape(moments, side, 2, groups, width).transpose(0, 3, 1, 2, 4)
    right = right.reshape(rows, side, 2 * width)
    right_all = [lax.dynamic_index_in_dim(right, r ^ s, 0, keepdims=False) for s in range(rows)]
    high = jnp.maximum(triples[..., 0], triples[..., 1])
    low = jnp.minimum(triples[..., 0], triples[..., 1])
    quads, thirds = high * (high + 1) // 2 + low, triples[..., 2]
    copies = 2 if plan.sub % 32 == 0 else 1
    came = []
    whole = []
    so_far = []

    def self_energy(u, *behind):
        height = (u + 1) * plan.sub
        shapes = [(2, height, side)] * count
        return pl.pallas_call(
            functools.partial(sigma_kernel, plan, pair_count, u, copies),
            out_shape=[jax.ShapeDtypeStruct(shape, bf16) for shape in shapes],
            in_specs=[smem()] * 3 + hbm(2 * moms + len(so_far)),
            out_specs=hbm(count),
            scratch_shapes=[
                pltpu.VMEM((count, 2, plan.sub, side), bf16),
                pltpu.VMEM((count, 2, plan.sub, side), bf16),
                pltpu.VMEM((count * (count + 1) // 2, 2, 16, side), f32),
                pltpu.VMEM((count, 2, 16, side), f32),
                pltpu.VMEM((count, 2, height, side), bf16),
                dma(copies * 2 * moms),
                dma(copies * count),
                dma(count),
            ],
            compiler_params=params,
            name="self_energy",
        )(
            *after((place, quads, thirds), behind),
            *([lesser] + lesser_came[u]),
            *([partner] + partner_came[u]),
            *so_far,
        )

    def to_row(value, b, q):
        goal = lambda a, c, m: (a ^ (b * groups), c, m ^ q) if a > c else None
        return plan.send(value, goal)

    for u in range(plan.subs):
        so_far = list(self_energy(u, right_all, diag))
    came.append(so_far[:1] + [to_row(so_far[b], b, 0) for b in range(1, moments)])
    whole += so_far[:moments]
    late = []
    for q in range(1, moms):
        mine = so_far[q * moments : (q + 1) * moments]
        came.append(
            [exchange_mom(mine[0], q)] + [to_row(mine[b], b, q) for b in range(1, moments)]
        )
        late += [(came[-1][0], None)] + [(mine[b], q) for b in range(1, moments)]
    right_all = after(right_all, came[-1])
    right_all = right_all[:1] + [exchange_row(right_all[s], s) for s in range(1, rows)]
    diag = after(by_block(diag), came[-1])
    diag = [jnp.concatenate([value[0], value[1]], axis=1) for value in diag]
    diag_all = [
        diag[b] if t == 0 else exchange_row(diag[b], t) for b in range(moments) for t in range(groups)
    ]

    def valid(key, a):
        return key[0] * groups + a % groups > key[1]

    found = {}
    own = [by_block(tiles) for tiles in came]
    both = [jnp.concatenate([tiles[b] for tiles in own], axis=1) for b in range(moments)]
    for key in plan.keys:
        for k in range(len(plan.chunks)):
            found[key, key[1], k] = (both[key[0]], plan.starts[k])

    def choose(values, behind):
        distinct = list({id(value): value for value in values.values()}.values())
        number = {id(value): n for n, value in enumerate(distinct)}
        distinct = after(distinct, behind)
        chosen = distinct[0]
        for col, value in values.items():
            if number[id(value)]:
                chosen = jnp.where(z == col, distinct[number[id(value)]], chosen)
        return chosen

    def shift(values, goals, behind):
        goal = lambda a, c, m: (a, goals[c][1], m) if c in goals and valid(goals[c][0], a) else None
        return plan.send(choose(values, behind), goal)

    top, ring, rest = moments - 1, plan.ring(), plan.rest()
    got = [[] for _ in plan.chunks]

    def ring_step(q, number, *behind):
        sends = {col: item for (n, col), item in ring.items() if n == number}
        values = {
            col: own[q][key[0]] if step is None else got[q][step]
            for col, (key, _, step) in sends.items()
        }
        value = shift(values, {col: item[:2] for col, item in sends.items()}, behind)
        got[q].append(value)
        for key, to, _ in sends.values():
            found[key, to, q] = (value, 0)

    def rest_step(number, *behind):
        step = rest[number]
        value = shift({col: both[key[0]] for col, (key, _) in step.items()}, step, behind)
        for key, to in step.values():
            for k in range(len(plan.chunks)):
                found[key, to, k] = (value, plan.starts[k])

    for number in range(cols - 1):
        for k in range(len(plan.chunks)):
            behind = [got[k - 1][number]] if k else []
            if number == 1 and k + 1 < len(plan.chunks):
                behind.append(came[k + 1])
            ring_step(k, number, *behind)
    for number in range(len(rest)):
        low = any(key[0] < top for key, _ in rest[number].values())
        rest_step(number, *([got[0][1], got[-1][0], right_all] if low else [got[0][0]]))

    buffers = []

    def number_of(value):
        for index, held in enumerate(buffers):
            if held is value:
                return index
        buffers.append(value)
        return len(buffers) - 1

    sources = {name + (0,): (number_of(value), part) for name, (value, part) in found.items()}
    sig_all = list(buffers)
    for t in range(1, groups):
        for name, (value, part) in found.items():
            sources[name + (t,)] = (len(sig_all) + number_of(value), part)
        sig_all += [exchange_row(value, t) for value in buffers]

    solved = pl.pallas_call(
        functools.partial(solve_kernel, plan, sources),
        out_shape=[jax.ShapeDtypeStruct((side, 2 * width), bf16)] * rows,
        in_specs=[smem()] + [pl.BlockSpec(memory_space=pltpu.VMEM)] * (2 * rows) + hbm(len(sig_all)),
        out_specs=hbm(rows),
        scratch_shapes=[
            pltpu.VMEM((rows, side, 2 * side * (cols - 1)), bf16),
            pltpu.VMEM((rows * 2 * side, 2 * width), bf16),
            dma(moments),
            dma(rows),
        ],
        compiler_params=params,
        name="substitution",
    )(place, *diag_all, *right_all, *sig_all)

    for value, q in late:
        whole.append(value if q is None else exchange_mom(after(value, solved), q))
    sigma = pl.pallas_call(
        functools.partial(place_kernel, plan),
        out_shape=jax.ShapeDtypeStruct(lesser.shape, bf16),
        in_specs=[smem()] + hbm(len(whole)),
        scratch_shapes=[dma(len(whole))],
        compiler_params=params,
        name="place_sigma",
    )(place, *whole)

    back = [solved[0]] + [exchange_row(solved[s], s) for s in range(1, rows)]
    back = after(back, sigma)
    spread = pl.pallas_call(
        functools.partial(spread_kernel, plan),
        out_shape=jax.ShapeDtypeStruct(right_side.shape, bf16),
        in_specs=[smem()] + [pl.BlockSpec(memory_space=pltpu.VMEM)] * rows,
        compiler_params=pltpu.CompilerParams(vmem_limit_bytes=VMEM_BYTES // 2),
        name="place_solution",
    )
    return sigma, spread(place, *back)


def solution(mesh):
    placed = (
        P("mom", None, "row", "col"),
        P("mom", None, "col", "row"),
        P(),
        P("mom", None, "row", None),
        P("mom", "row", None, "col"),
    )
    return jax.shard_map(
        functools.partial(on_device, mesh),
        mesh=mesh,
        in_specs=placed,
        out_specs=(P("mom", None, "row", "col"), P("mom", "row", None, "col")),
        check_vma=False,
    )
```

```python
import functools
import itertools
import math

import jax
import jax.numpy as jnp
from jax import lax
from jax.experimental import pallas as pl
from jax.experimental.pallas import tpu as pltpu
from jax.sharding import PartitionSpec as P

AXES = ("row", "col", "mom")
VMEM_BYTES = 60 * 1024 * 1024


class Plan:
    def __init__(self, mesh, moments, side):
        self.rows = mesh.shape["row"]
        self.cols = mesh.shape["col"]
        self.moms = mesh.shape["mom"]
        self.moments = moments
        self.side = side
        self.groups = self.rows // moments
        self.half = side // self.moms
        self.width = side // self.groups
        self.subs = 2 if self.half % 32 == 0 else 1
        self.sub = self.half // self.subs
        self.chunks = [(q, 0, self.half) for q in range(self.moms)]
        self.starts = [0]
        for _, _, height in self.chunks:
            self.starts.append(self.starts[-1] + height)
        self.keys = [
            (b, j)
            for b in range(moments)
            for j in range(self.cols - 1)
            if (b + 1) * self.groups - 1 > j
        ]

    def send(self, value, target):
        pairs = []
        index = lambda r, c, m: (r * self.cols + c) * self.moms + m
        for place in itertools.product(range(self.rows), range(self.cols), range(self.moms)):
            goal = target(*place)
            if goal is not None:
                pairs.append((index(*place), index(*goal)))
        return lax.ppermute(value, AXES, pairs)

    def ring(self):
        top, last = self.moments - 1, self.cols - 1
        sends, queue = {}, []
        for col in range(last):
            queue = [((top, col), None)] + [(key, n) for n, (key, _) in enumerate(queue)]
            for n, (key, step) in enumerate(queue):
                sends[n, col] = (key, col + 1, step)
        wanted = [
            (key, to)
            for key in self.keys
            if key[0] < top
            for to in range(self.cols)
            if to not in (key[1], last)
        ]
        for key, to in wanted:
            for n in range(1, last):
                if (n, key[1]) in sends or (n, to - 1) in sends and sends[n, to - 1][1] == to:
                    continue
                if to not in [goal for (m, _), (_, goal, _) in sends.items() if m == n]:
                    sends[n, key[1]] = (key, to, None)
                    break
        return sends

    def rest(self):
        done = {(key, to) for key, to, _ in self.ring().values()}
        wanted = [
            (key, to)
            for key in self.keys
            for to in range(self.cols)
            if to != key[1] and (key, to) not in done
        ]
        steps = []
        for key, to in sorted(wanted, key=lambda item: (item[0][0], -item[1], -item[0][1])):
            for step in steps:
                free = key[1] not in step and to not in [goal for _, goal in step.values()]
                if free and all(other[0] == key[0] for other, _ in step.values()):
                    break
            else:
                step = {}
                steps.append(step)
            step[key[1]] = (key, to)
        return steps


def hbm(count):
    return [pl.BlockSpec(memory_space=pltpu.HBM)] * count


def smem():
    return pl.BlockSpec(memory_space=pltpu.SMEM)


def run_copies(copies):
    for copy in copies:
        copy.start()
    for copy in copies:
        copy.wait()


def sigma_kernel(plan, pair_count, u, chunks, place, quads, thirds, *refs):
    moms, moments, groups = plan.moms, plan.moments, plan.groups
    half, sub, side, count = plan.half, plan.sub, plan.side, plan.moms * plan.moments
    refs = list(refs)
    take = lambda number: [refs.pop(0) for _ in range(number)]
    lesser_in, partner_in = take(moms), take(moms)
    before, outs = take(count if u else 0), take(count)
    lesser, partner, pairs, third, held, in_sems, out_sems, before_sems = refs
    x, y = place[0] // groups, place[2]
    height = sub // chunks
    copies = [[] for _ in range(chunks)]
    for chunk in range(chunks):
        rows = pl.ds(chunk * height, height)
        for which, (sources, target) in enumerate(((lesser_in, lesser), (partner_in, partner))):
            for q in range(moms):
                source = sources[q].at[:, :, rows, :]
                if q == 0:
                    start = pl.multiple_of(y * half + u * sub + chunk * height, 16)
                    source = sources[q].at[:, :, pl.ds(start, height), :]
                copy = pltpu.make_async_copy(
                    source,
                    target.at[pl.ds((y ^ q) * moments, moments), :, rows, :],
                    in_sems.at[(chunk * 2 + which) * moms + q],
                )
                copy.start()
                copies[chunk].append(copy)
    earlier = [
        pltpu.make_async_copy(
            before[n], held.at[n, :, pl.ds(0, u * sub), :], before_sems.at[n]
        )
        for n in range(len(before))
    ]
    for copy in earlier:
        copy.start()
    scale = 1.0 / pair_count
    lanes = 128 if side % 128 == 0 else side
    order = [(q, b) for q in reversed(range(moms)) for b in range(moments)]
    sent = []
    for chunk in range(chunks):
        for copy in copies[chunk]:
            copy.wait()

        def block(index, _, chunk=chunk):
            row = chunk * height + index * 16
            rows = pl.ds(pl.multiple_of(row, 16), 16)
            for c in range(count):
                for p in range(2):
                    third[c, p] = partner[c, p, rows, :].astype(jnp.float32)
            n = 0
            for a in range(count):
                for b in range(a + 1):
                    for lane in range(0, side, lanes):
                        cols = pl.ds(lane, lanes)
                        a_re = lesser[a, 0, rows, cols].astype(jnp.float32)
                        a_im = lesser[a, 1, rows, cols].astype(jnp.float32)
                        b_re = lesser[b, 0, rows, cols].astype(jnp.float32)
                        b_im = lesser[b, 1, rows, cols].astype(jnp.float32)
                        pairs[n, 0, :, cols] = a_re * b_re - a_im * b_im
                        pairs[n, 1, :, cols] = a_re * b_im + a_im * b_re
                    n += 1
            for q, b in order:
                moment = (y ^ q) * moments + (x ^ b)
                to = pl.ds(pl.multiple_of(u * sub + row, 16), 16)
                for lane in range(0, side, lanes):
                    cols = pl.ds(lane, lanes)
                    total_re = total_im = None
                    for m in range(pair_count):
                        quad, c = quads[moment, m], thirds[moment, m]
                        p_re, p_im = pairs[quad, 0, :, cols], pairs[quad, 1, :, cols]
                        c_re, c_im = third[c, 0, :, cols], third[c, 1, :, cols]
                        f_re = p_re * c_re - p_im * c_im
                        f_im = p_re * c_im + p_im * c_re
                        total_re = f_re if total_re is None else total_re + f_re
                        total_im = f_im if total_im is None else total_im + f_im
                    held[q * moments + b, 0, to, cols] = (total_re * scale).astype(jnp.bfloat16)
                    held[q * moments + b, 1, to, cols] = (total_im * scale).astype(jnp.bfloat16)
            return 0

        lax.fori_loop(0, height // 16, block, 0)
        for index in range(count):
            rows = pl.ds(u * sub + chunk * height, height)
            copy = pltpu.make_async_copy(
                held.at[index, :, rows, :], outs[index].at[:, rows, :], out_sems.at[chunk * count + index]
            )
            copy.start()
            sent.append(copy)
    for copy in earlier:
        copy.wait()
    for n in range(len(before)):
        rows = pl.ds(0, u * sub)
        copy = pltpu.make_async_copy(
            held.at[n, :, rows, :], outs[n].at[:, rows, :], before_sems.at[n]
        )
        copy.start()
        sent.append(copy)
    for copy in sent:
        copy.wait()


def place_kernel(plan, place, *refs):
    ins, out, sems = refs[:-2], refs[-2], refs[-1]
    x, y = place[0] // plan.groups, place[2]
    copies = []
    for k, (q, first, height) in enumerate(plan.chunks):
        rows = pl.ds(pl.multiple_of((y ^ q) * plan.half + first, 16), height)
        for b in range(plan.moments):
            index = k * plan.moments + b
            copies.append(pltpu.make_async_copy(ins[index], out.at[x ^ b, :, rows, :], sems.at[index]))
    run_copies(copies)


def solve_kernel(plan, sources, place, *refs):
    rows, moms, groups, side = plan.rows, plan.moms, plan.groups, plan.side
    moments, half, width, keys = plan.moments, plan.half, plan.width, plan.keys
    top = moments - 1
    diag, right = refs[:rows], refs[rows : 2 * rows]
    sig_in, outs = refs[2 * rows : -rows - 4], refs[-rows - 4 : -4]
    sig, solved, sems, out_sems = refs[-4:]
    r, y = place[0], place[2]
    g = r % groups
    for key in sorted(keys, key=lambda key: key[0]):
        for col in range(plan.cols):

            @pl.when(place[1] == col)
            def _(key=key, col=col):
                for t in range(groups):
                    row = key[0] * groups + (g ^ t)
                    for k, (q, first, height) in enumerate(plan.chunks):
                        index, start = sources[key, col, k, t]
                        at = pl.ds(pl.multiple_of((y ^ q) * half + first, 16), height)
                        for p in range(2):
                            lane = pl.ds((2 * key[1] + p) * side, side)
                            pltpu.make_async_copy(
                                sig_in[index].at[p, pl.ds(start, height), :],
                                sig.at[row, at, lane],
                                sems.at[key[0]],
                            ).start()

    weight = 1.0 / math.sqrt(side * rows)

    def turn(value):
        return jnp.concatenate([-value[:, width:], value[:, :width]], axis=1)

    for row in range(rows):
        if row == max(1, row // groups * groups):
            for key in keys:
                if key[0] == row // groups:
                    for _ in range(groups * 2):
                        tile = sig.at[0, :, pl.ds(0, side)]
                        pltpu.make_async_copy(tile, tile, sems.at[key[0]]).wait()
        pending = pick(right, r ^ row).astype(jnp.float32)
        if row > 0:
            depth = 2 * side * row
            pending = pending + weight * jnp.dot(
                sig[row, :, :depth], solved[:depth, :], preferred_element_type=jnp.float32
            )
        both = jnp.concatenate([pending, turn(pending)], axis=0).astype(jnp.bfloat16)
        value = jnp.dot(
            pick(diag[row // groups * groups :][:groups], g ^ (row % groups)),
            both,
            preferred_element_type=jnp.float32,
        )
        solved[pl.ds(2 * row * side, side), :] = value.astype(jnp.bfloat16)
        solved[pl.ds((2 * row + 1) * side, side), :] = turn(value).astype(jnp.bfloat16)
        for s in range(rows):

            @pl.when((r ^ s) == row)
            def _(s=s, row=row):
                at = pl.ds(2 * row * side, side)
                pltpu.make_async_copy(solved.at[at, :], outs[s], out_sems.at[s]).start()

    for s in range(rows):
        pltpu.make_async_copy(solved.at[pl.ds(0, side), :], outs[s], out_sems.at[s]).wait()


def after(value, *others):
    return lax.optimization_barrier((value, others))[0]


def pick(held, number):
    value = held[0][...]
    for n in range(1, len(held)):
        value = jnp.where(number == n, held[n][...], value)
    return value


def spread_kernel(plan, place, *refs):
    groups, width = plan.groups, plan.width
    ins, out = refs[:-1], refs[-1]
    for m in range(plan.moments):
        parts = [pick(ins, place[0] ^ (m * groups + g)) for g in range(groups)]
        for p in range(2):
            out[m, :, p, :] = jnp.concatenate(
                [part[:, p * width : (p + 1) * width] for part in parts], axis=1
            )


def on_device(mesh, lesser, greater, triples, diag_inverse, right_side):
    moments, _, side, _ = lesser.shape
    plan = Plan(mesh, moments, side)
    rows, cols, moms, groups = plan.rows, plan.cols, plan.moms, plan.groups
    half, width = plan.half, plan.width
    pair_count = triples.shape[1]
    count = moms * moments
    r, z, y = (lax.axis_index(axis) for axis in AXES)
    x = r // groups
    place = jnp.stack([r, z, y]).astype(jnp.int32)
    bf16, f32 = jnp.bfloat16, jnp.float32
    params = pltpu.CompilerParams(vmem_limit_bytes=VMEM_BYTES)
    dma = lambda *shape: pltpu.SemaphoreType.DMA(shape)

    def exchange_mom(value, q):
        return plan.send(value, lambda a, b, c: (a, b, c ^ q))

    def exchange_row(value, s):
        return plan.send(value, lambda a, b, c: (a ^ s, b, c))

    def by_block(came):
        return [lax.select_n(x ^ b, *came) for b in range(moments)]

    def part_of(value, q, u):
        return lax.dynamic_slice_in_dim(value, (y ^ q) * half + u * plan.sub, plan.sub, 2)

    parts = [part_of(lesser, q, 0) for q in range(1, moms)]
    greater, diag_inverse, right_side = after((greater, diag_inverse, right_side), parts)
    lesser_came = [[exchange_mom(parts[q - 1], q) for q in range(1, moms)]]
    partner = jnp.swapaxes(greater, 2, 3)
    parts = [part_of(partner, q, 0) for q in range(1, moms)]
    diag_inverse, right_side = after((diag_inverse, right_side), parts)
    partner_came = [[exchange_mom(parts[q - 1], q) for q in range(1, moms)]]
    for u in range(1, plan.subs):
        parts = [(part_of(lesser, q, u), part_of(partner, q, u)) for q in range(1, moms)]
        parts = after(parts, lesser_came[-1])
        lesser_came.append([exchange_mom(parts[q - 1][0], q) for q in range(1, moms)])
        partner_came.append([exchange_mom(parts[q - 1][1], q) for q in range(1, moms)])

    mine = [lax.dynamic_index_in_dim(diag_inverse, x ^ b, 0, keepdims=False) for b in range(moments)]
    diag = mine[:1] + [exchange_row(mine[b], b * groups) for b in range(1, moments)]

    right = right_side.reshape(moments, side, 2, groups, width).transpose(0, 3, 1, 2, 4)
    right = right.reshape(rows, side, 2 * width)
    right_all = [lax.dynamic_index_in_dim(right, r ^ s, 0, keepdims=False) for s in range(rows)]
    high = jnp.maximum(triples[..., 0], triples[..., 1])
    low = jnp.minimum(triples[..., 0], triples[..., 1])
    quads, thirds = high * (high + 1) // 2 + low, triples[..., 2]
    copies = 2 if plan.sub % 32 == 0 else 1
    came = []
    whole = []
    so_far = []

    def self_energy(u, *behind):
        height = (u + 1) * plan.sub
        shapes = [(2, height, side)] * count
        return pl.pallas_call(
            functools.partial(sigma_kernel, plan, pair_count, u, copies),
            out_shape=[jax.ShapeDtypeStruct(shape, bf16) for shape in shapes],
            in_specs=[smem()] * 3 + hbm(2 * moms + len(so_far)),
            out_specs=hbm(count),
            scratch_shapes=[
                pltpu.VMEM((count, 2, plan.sub, side), bf16),
                pltpu.VMEM((count, 2, plan.sub, side), bf16),
                pltpu.VMEM((count * (count + 1) // 2, 2, 16, side), f32),
                pltpu.VMEM((count, 2, 16, side), f32),
                pltpu.VMEM((count, 2, height, side), bf16),
                dma(copies * 2 * moms),
                dma(copies * count),
                dma(count),
            ],
            compiler_params=params,
            name="self_energy",
        )(
            *after((place, quads, thirds), behind),
            *([lesser] + lesser_came[u]),
            *([partner] + partner_came[u]),
            *so_far,
        )

    def to_row(value, b, q):
        goal = lambda a, c, m: (a ^ (b * groups), c, m ^ q) if a > c else None
        return plan.send(value, goal)

    for u in range(plan.subs):
        so_far = list(self_energy(u, right_all, diag))
    came.append(so_far[:1] + [to_row(so_far[b], b, 0) for b in range(1, moments)])
    whole += so_far[:moments]
    late = []
    for q in range(1, moms):
        mine = so_far[q * moments : (q + 1) * moments]
        came.append(
            [exchange_mom(mine[0], q)] + [to_row(mine[b], b, q) for b in range(1, moments)]
        )
        late += [(came[-1][0], None)] + [(mine[b], q) for b in range(1, moments)]
    right_all = after(right_all, came[-1])
    right_all = right_all[:1] + [exchange_row(right_all[s], s) for s in range(1, rows)]
    diag = after(by_block(diag), came[-1])
    diag = [jnp.concatenate([value[0], value[1]], axis=1) for value in diag]
    diag_all = [
        diag[b] if t == 0 else exchange_row(diag[b], t) for b in range(moments) for t in range(groups)
    ]

    def valid(key, a):
        return key[0] * groups + a % groups > key[1]

    found = {}
    own = [by_block(tiles) for tiles in came]
    both = [jnp.concatenate([tiles[b] for tiles in own], axis=1) for b in range(moments)]
    for key in plan.keys:
        for k in range(len(plan.chunks)):
            found[key, key[1], k] = (both[key[0]], plan.starts[k])

    def choose(values, behind):
        distinct = list({id(value): value for value in values.values()}.values())
        number = {id(value): n for n, value in enumerate(distinct)}
        distinct = after(distinct, behind)
        chosen = distinct[0]
        for col, value in values.items():
            if number[id(value)]:
                chosen = jnp.where(z == col, distinct[number[id(value)]], chosen)
        return chosen

    def shift(values, goals, behind):
        goal = lambda a, c, m: (a, goals[c][1], m) if c in goals and valid(goals[c][0], a) else None
        return plan.send(choose(values, behind), goal)

    top, ring, rest = moments - 1, plan.ring(), plan.rest()
    got = [[] for _ in plan.chunks]

    def ring_step(q, number, *behind):
        sends = {col: item for (n, col), item in ring.items() if n == number}
        values = {
            col: own[q][key[0]] if step is None else got[q][step]
            for col, (key, _, step) in sends.items()
        }
        value = shift(values, {col: item[:2] for col, item in sends.items()}, behind)
        got[q].append(value)
        for key, to, _ in sends.values():
            found[key, to, q] = (value, 0)

    def rest_step(number, *behind):
        step = rest[number]
        value = shift({col: both[key[0]] for col, (key, _) in step.items()}, step, behind)
        for key, to in step.values():
            for k in range(len(plan.chunks)):
                found[key, to, k] = (value, plan.starts[k])

    for number in range(cols - 1):
        for k in range(len(plan.chunks)):
            behind = [got[k - 1][number]] if k and number else []
            if number == 1 and k + 1 < len(plan.chunks):
                behind.append(came[k + 1])
            ring_step(k, number, *behind)
    for number in range(len(rest)):
        low = any(key[0] < top for key, _ in rest[number].values())
        rest_step(number, *([got[0][1], got[-1][0], right_all] if low else [got[0][0]]))

    buffers = []

    def number_of(value):
        for index, held in enumerate(buffers):
            if held is value:
                return index
        buffers.append(value)
        return len(buffers) - 1

    sources = {name + (0,): (number_of(value), part) for name, (value, part) in found.items()}
    sig_all = list(buffers)
    for t in range(1, groups):
        for name, (value, part) in found.items():
            sources[name + (t,)] = (len(sig_all) + number_of(value), part)
        sig_all += [exchange_row(value, t) for value in buffers]

    solved = pl.pallas_call(
        functools.partial(solve_kernel, plan, sources),
        out_shape=[jax.ShapeDtypeStruct((side, 2 * width), bf16)] * rows,
        in_specs=[smem()] + [pl.BlockSpec(memory_space=pltpu.VMEM)] * (2 * rows) + hbm(len(sig_all)),
        out_specs=hbm(rows),
        scratch_shapes=[
            pltpu.VMEM((rows, side, 2 * side * (cols - 1)), bf16),
            pltpu.VMEM((rows * 2 * side, 2 * width), bf16),
            dma(moments),
            dma(rows),
        ],
        compiler_params=params,
        name="substitution",
    )(place, *diag_all, *right_all, *sig_all)

    for value, q in late:
        whole.append(value if q is None else exchange_mom(after(value, solved), q))
    sigma = pl.pallas_call(
        functools.partial(place_kernel, plan),
        out_shape=jax.ShapeDtypeStruct(lesser.shape, bf16),
        in_specs=[smem()] + hbm(len(whole)),
        scratch_shapes=[dma(len(whole))],
        compiler_params=params,
        name="place_sigma",
    )(place, *whole)

    back = [solved[0]] + [exchange_row(solved[s], s) for s in range(1, rows)]
    back = after(back, sigma)
    spread = pl.pallas_call(
        functools.partial(spread_kernel, plan),
        out_shape=jax.ShapeDtypeStruct(right_side.shape, bf16),
        in_specs=[smem()] + [pl.BlockSpec(memory_space=pltpu.VMEM)] * rows,
        compiler_params=pltpu.CompilerParams(vmem_limit_bytes=VMEM_BYTES // 2),
        name="place_solution",
    )
    return sigma, spread(place, *back)


def solution(mesh):
    placed = (
        P("mom", None, "row", "col"),
        P("mom", None, "col", "row"),
        P(),
        P("mom", None, "row", None),
        P("mom", "row", None, "col"),
    )
    return jax.shard_map(
        functools.partial(on_device, mesh),
        mesh=mesh,
        in_specs=placed,
        out_specs=(P("mom", None, "row", "col"), P("mom", "row", None, "col")),
        check_vma=False,
    )
```

```python
import functools
import itertools
import math

import jax
import jax.numpy as jnp
from jax import lax
from jax.experimental import pallas as pl
from jax.experimental.pallas import tpu as pltpu
from jax.sharding import PartitionSpec as P

AXES = ("row", "col", "mom")
VMEM_BYTES = 60 * 1024 * 1024


class Plan:
    def __init__(self, mesh, moments, side):
        self.rows = mesh.shape["row"]
        self.cols = mesh.shape["col"]
        self.moms = mesh.shape["mom"]
        self.moments = moments
        self.side = side
        self.groups = self.rows // moments
        self.half = side // self.moms
        self.width = side // self.groups
        self.subs = 2 if self.half % 32 == 0 else 1
        self.sub = self.half // self.subs
        self.chunks = [(q, 0, self.half) for q in range(self.moms)]
        self.starts = [0]
        for _, _, height in self.chunks:
            self.starts.append(self.starts[-1] + height)
        self.keys = [
            (b, j)
            for b in range(moments)
            for j in range(self.cols - 1)
            if (b + 1) * self.groups - 1 > j
        ]

    def send(self, value, target):
        pairs = []
        index = lambda r, c, m: (r * self.cols + c) * self.moms + m
        for place in itertools.product(range(self.rows), range(self.cols), range(self.moms)):
            goal = target(*place)
            if goal is not None:
                pairs.append((index(*place), index(*goal)))
        return lax.ppermute(value, AXES, pairs)

    def ring(self):
        top, last = self.moments - 1, self.cols - 1
        sends, queue = {}, []
        for col in range(last):
            queue = [((top, col), None)] + [(key, n) for n, (key, _) in enumerate(queue)]
            for n, (key, step) in enumerate(queue):
                sends[n, col] = (key, col + 1, step)
        wanted = [
            (key, to)
            for key in self.keys
            if key[0] < top
            for to in range(self.cols)
            if to not in (key[1], last)
        ]
        for key, to in wanted:
            for n in range(1, last):
                if (n, key[1]) in sends or (n, to - 1) in sends and sends[n, to - 1][1] == to:
                    continue
                if to not in [goal for (m, _), (_, goal, _) in sends.items() if m == n]:
                    sends[n, key[1]] = (key, to, None)
                    break
        return sends

    def left(self):
        top = self.moments - 1
        return {col: ((top, col), col - 1) for col in range(1, self.cols - 1)}

    def rest(self):
        done = {(key, to) for key, to, _ in self.ring().values()} | set(self.left().values())
        wanted = [
            (key, to)
            for key in self.keys
            for to in range(self.cols)
            if to != key[1] and (key, to) not in done
        ]
        steps = []
        for key, to in sorted(wanted, key=lambda item: (item[0][0], -item[1], -item[0][1])):
            for step in steps:
                free = key[1] not in step and to not in [goal for _, goal in step.values()]
                if free and all(other[0] == key[0] for other, _ in step.values()):
                    break
            else:
                step = {}
                steps.append(step)
            step[key[1]] = (key, to)
        return steps


def hbm(count):
    return [pl.BlockSpec(memory_space=pltpu.HBM)] * count


def smem():
    return pl.BlockSpec(memory_space=pltpu.SMEM)


def run_copies(copies):
    for copy in copies:
        copy.start()
    for copy in copies:
        copy.wait()


def sigma_kernel(plan, pair_count, u, chunks, place, quads, thirds, *refs):
    moms, moments, groups = plan.moms, plan.moments, plan.groups
    half, sub, side, count = plan.half, plan.sub, plan.side, plan.moms * plan.moments
    refs = list(refs)
    take = lambda number: [refs.pop(0) for _ in range(number)]
    lesser_in, partner_in = take(moms), take(moms)
    before, outs = take(count if u else 0), take(count)
    lesser, partner, pairs, third, held, in_sems, out_sems, before_sems = refs
    x, y = place[0] // groups, place[2]
    height = sub // chunks
    copies = [[] for _ in range(chunks)]
    for chunk in range(chunks):
        rows = pl.ds(chunk * height, height)
        for which, (sources, target) in enumerate(((lesser_in, lesser), (partner_in, partner))):
            for q in range(moms):
                source = sources[q].at[:, :, rows, :]
                if q == 0:
                    start = pl.multiple_of(y * half + u * sub + chunk * height, 16)
                    source = sources[q].at[:, :, pl.ds(start, height), :]
                copy = pltpu.make_async_copy(
                    source,
                    target.at[pl.ds((y ^ q) * moments, moments), :, rows, :],
                    in_sems.at[(chunk * 2 + which) * moms + q],
                )
                copy.start()
                copies[chunk].append(copy)
    earlier = [
        pltpu.make_async_copy(
            before[n], held.at[n, :, pl.ds(0, u * sub), :], before_sems.at[n]
        )
        for n in range(len(before))
    ]
    for copy in earlier:
        copy.start()
    scale = 1.0 / pair_count
    lanes = 128 if side % 128 == 0 else side
    order = [(q, b) for q in reversed(range(moms)) for b in range(moments)]
    sent = []
    for chunk in range(chunks):
        for copy in copies[chunk]:
            copy.wait()

        def block(index, _, chunk=chunk):
            row = chunk * height + index * 16
            rows = pl.ds(pl.multiple_of(row, 16), 16)
            for c in range(count):
                for p in range(2):
                    third[c, p] = partner[c, p, rows, :].astype(jnp.float32)
            n = 0
            for a in range(count):
                for b in range(a + 1):
                    for lane in range(0, side, lanes):
                        cols = pl.ds(lane, lanes)
                        a_re = lesser[a, 0, rows, cols].astype(jnp.float32)
                        a_im = lesser[a, 1, rows, cols].astype(jnp.float32)
                        b_re = lesser[b, 0, rows, cols].astype(jnp.float32)
                        b_im = lesser[b, 1, rows, cols].astype(jnp.float32)
                        pairs[n, 0, :, cols] = a_re * b_re - a_im * b_im
                        pairs[n, 1, :, cols] = a_re * b_im + a_im * b_re
                    n += 1
            for q, b in order:
                moment = (y ^ q) * moments + (x ^ b)
                to = pl.ds(pl.multiple_of(u * sub + row, 16), 16)
                for lane in range(0, side, lanes):
                    cols = pl.ds(lane, lanes)
                    total_re = total_im = None
                    for m in range(pair_count):
                        quad, c = quads[moment, m], thirds[moment, m]
                        p_re, p_im = pairs[quad, 0, :, cols], pairs[quad, 1, :, cols]
                        c_re, c_im = third[c, 0, :, cols], third[c, 1, :, cols]
                        f_re = p_re * c_re - p_im * c_im
                        f_im = p_re * c_im + p_im * c_re
                        total_re = f_re if total_re is None else total_re + f_re
                        total_im = f_im if total_im is None else total_im + f_im
                    held[q * moments + b, 0, to, cols] = (total_re * scale).astype(jnp.bfloat16)
                    held[q * moments + b, 1, to, cols] = (total_im * scale).astype(jnp.bfloat16)
            return 0

        lax.fori_loop(0, height // 16, block, 0)
        for index in range(count):
            rows = pl.ds(u * sub + chunk * height, height)
            copy = pltpu.make_async_copy(
                held.at[index, :, rows, :], outs[index].at[:, rows, :], out_sems.at[chunk * count + index]
            )
            copy.start()
            sent.append(copy)
    for copy in earlier:
        copy.wait()
    for n in range(len(before)):
        rows = pl.ds(0, u * sub)
        copy = pltpu.make_async_copy(
            held.at[n, :, rows, :], outs[n].at[:, rows, :], before_sems.at[n]
        )
        copy.start()
        sent.append(copy)
    for copy in sent:
        copy.wait()


def place_kernel(plan, place, *refs):
    ins, out, sems = refs[:-2], refs[-2], refs[-1]
    x, y = place[0] // plan.groups, place[2]
    copies = []
    for k, (q, first, height) in enumerate(plan.chunks):
        rows = pl.ds(pl.multiple_of((y ^ q) * plan.half + first, 16), height)
        for b in range(plan.moments):
            index = k * plan.moments + b
            copies.append(pltpu.make_async_copy(ins[index], out.at[x ^ b, :, rows, :], sems.at[index]))
    run_copies(copies)


def solve_kernel(plan, sources, place, *refs):
    rows, moms, groups, side = plan.rows, plan.moms, plan.groups, plan.side
    moments, half, width, keys = plan.moments, plan.half, plan.width, plan.keys
    top = moments - 1
    diag, right = refs[:rows], refs[rows : 2 * rows]
    sig_in, outs = refs[2 * rows : -rows - 4], refs[-rows - 4 : -4]
    sig, solved, sems, out_sems = refs[-4:]
    r, y = place[0], place[2]
    g = r % groups
    for key in sorted(keys, key=lambda key: key[0]):
        for col in range(plan.cols):

            @pl.when(place[1] == col)
            def _(key=key, col=col):
                for t in range(groups):
                    row = key[0] * groups + (g ^ t)
                    for k, (q, first, height) in enumerate(plan.chunks):
                        index, start = sources[key, col, k, t]
                        at = pl.ds(pl.multiple_of((y ^ q) * half + first, 16), height)
                        for p in range(2):
                            lane = pl.ds((2 * key[1] + p) * side, side)
                            pltpu.make_async_copy(
                                sig_in[index].at[p, pl.ds(start, height), :],
                                sig.at[row, at, lane],
                                sems.at[key[0]],
                            ).start()

    weight = 1.0 / math.sqrt(side * rows)

    def turn(value):
        return jnp.concatenate([-value[:, width:], value[:, :width]], axis=1)

    for row in range(rows):
        if row == max(1, row // groups * groups):
            for key in keys:
                if key[0] == row // groups:
                    for _ in range(groups * 2):
                        tile = sig.at[0, :, pl.ds(0, side)]
                        pltpu.make_async_copy(tile, tile, sems.at[key[0]]).wait()
        pending = pick(right, r ^ row).astype(jnp.float32)
        if row > 0:
            depth = 2 * side * row
            pending = pending + weight * jnp.dot(
                sig[row, :, :depth], solved[:depth, :], preferred_element_type=jnp.float32
            )
        both = jnp.concatenate([pending, turn(pending)], axis=0).astype(jnp.bfloat16)
        value = jnp.dot(
            pick(diag[row // groups * groups :][:groups], g ^ (row % groups)),
            both,
            preferred_element_type=jnp.float32,
        )
        solved[pl.ds(2 * row * side, side), :] = value.astype(jnp.bfloat16)
        solved[pl.ds((2 * row + 1) * side, side), :] = turn(value).astype(jnp.bfloat16)
        for s in range(rows):

            @pl.when((r ^ s) == row)
            def _(s=s, row=row):
                at = pl.ds(2 * row * side, side)
                pltpu.make_async_copy(solved.at[at, :], outs[s], out_sems.at[s]).start()

    for s in range(rows):
        pltpu.make_async_copy(solved.at[pl.ds(0, side), :], outs[s], out_sems.at[s]).wait()


def after(value, *others):
    return lax.optimization_barrier((value, others))[0]


def pick(held, number):
    value = held[0][...]
    for n in range(1, len(held)):
        value = jnp.where(number == n, held[n][...], value)
    return value


def spread_kernel(plan, place, *refs):
    groups, width = plan.groups, plan.width
    ins, out = refs[:-1], refs[-1]
    for m in range(plan.moments):
        parts = [pick(ins, place[0] ^ (m * groups + g)) for g in range(groups)]
        for p in range(2):
            out[m, :, p, :] = jnp.concatenate(
                [part[:, p * width : (p + 1) * width] for part in parts], axis=1
            )


def on_device(mesh, lesser, greater, triples, diag_inverse, right_side):
    moments, _, side, _ = lesser.shape
    plan = Plan(mesh, moments, side)
    rows, cols, moms, groups = plan.rows, plan.cols, plan.moms, plan.groups
    half, width = plan.half, plan.width
    pair_count = triples.shape[1]
    count = moms * moments
    r, z, y = (lax.axis_index(axis) for axis in AXES)
    x = r // groups
    place = jnp.stack([r, z, y]).astype(jnp.int32)
    bf16, f32 = jnp.bfloat16, jnp.float32
    params = pltpu.CompilerParams(vmem_limit_bytes=VMEM_BYTES)
    dma = lambda *shape: pltpu.SemaphoreType.DMA(shape)

    def exchange_mom(value, q):
        return plan.send(value, lambda a, b, c: (a, b, c ^ q))

    def exchange_row(value, s):
        return plan.send(value, lambda a, b, c: (a ^ s, b, c))

    def by_block(came):
        return [lax.select_n(x ^ b, *came) for b in range(moments)]

    def part_of(value, q, u):
        return lax.dynamic_slice_in_dim(value, (y ^ q) * half + u * plan.sub, plan.sub, 2)

    parts = [part_of(lesser, q, 0) for q in range(1, moms)]
    greater, diag_inverse, right_side = after((greater, diag_inverse, right_side), parts)
    lesser_came = [[exchange_mom(parts[q - 1], q) for q in range(1, moms)]]
    partner = jnp.swapaxes(greater, 2, 3)
    parts = [part_of(partner, q, 0) for q in range(1, moms)]
    diag_inverse, right_side = after((diag_inverse, right_side), parts)
    partner_came = [[exchange_mom(parts[q - 1], q) for q in range(1, moms)]]
    for u in range(1, plan.subs):
        parts = [(part_of(lesser, q, u), part_of(partner, q, u)) for q in range(1, moms)]
        parts = after(parts, lesser_came[-1])
        lesser_came.append([exchange_mom(parts[q - 1][0], q) for q in range(1, moms)])
        partner_came.append([exchange_mom(parts[q - 1][1], q) for q in range(1, moms)])

    mine = [lax.dynamic_index_in_dim(diag_inverse, x ^ b, 0, keepdims=False) for b in range(moments)]
    diag = mine[:1] + [exchange_row(mine[b], b * groups) for b in range(1, moments)]

    right = right_side.reshape(moments, side, 2, groups, width).transpose(0, 3, 1, 2, 4)
    right = right.reshape(rows, side, 2 * width)
    right_all = [lax.dynamic_index_in_dim(right, r ^ s, 0, keepdims=False) for s in range(rows)]
    high = jnp.maximum(triples[..., 0], triples[..., 1])
    low = jnp.minimum(triples[..., 0], triples[..., 1])
    quads, thirds = high * (high + 1) // 2 + low, triples[..., 2]
    copies = 2 if plan.sub % 32 == 0 else 1
    came = []
    whole = []
    so_far = []

    def self_energy(u, *behind):
        height = (u + 1) * plan.sub
        shapes = [(2, height, side)] * count
        return pl.pallas_call(
            functools.partial(sigma_kernel, plan, pair_count, u, copies),
            out_shape=[jax.ShapeDtypeStruct(shape, bf16) for shape in shapes],
            in_specs=[smem()] * 3 + hbm(2 * moms + len(so_far)),
            out_specs=hbm(count),
            scratch_shapes=[
                pltpu.VMEM((count, 2, plan.sub, side), bf16),
                pltpu.VMEM((count, 2, plan.sub, side), bf16),
                pltpu.VMEM((count * (count + 1) // 2, 2, 16, side), f32),
                pltpu.VMEM((count, 2, 16, side), f32),
                pltpu.VMEM((count, 2, height, side), bf16),
                dma(copies * 2 * moms),
                dma(copies * count),
                dma(count),
            ],
            compiler_params=params,
            name="self_energy",
        )(
            *after((place, quads, thirds), behind),
            *([lesser] + lesser_came[u]),
            *([partner] + partner_came[u]),
            *so_far,
        )

    def to_row(value, b, q):
        goal = lambda a, c, m: (a ^ (b * groups), c, m ^ q) if a > c else None
        return plan.send(value, goal)

    for u in range(plan.subs):
        so_far = list(self_energy(u, right_all, diag))
    came.append(so_far[:1] + [to_row(so_far[b], b, 0) for b in range(1, moments)])
    whole += so_far[:moments]
    late = []
    for q in range(1, moms):
        mine = so_far[q * moments : (q + 1) * moments]
        came.append(
            [exchange_mom(mine[0], q)] + [to_row(mine[b], b, q) for b in range(1, moments)]
        )
        late += [(came[-1][0], None)] + [(mine[b], q) for b in range(1, moments)]
    right_all = after(right_all, came[-1])
    right_all = right_all[:1] + [exchange_row(right_all[s], s) for s in range(1, rows)]
    diag = after(by_block(diag), came[-1])
    diag = [jnp.concatenate([value[0], value[1]], axis=1) for value in diag]
    diag_all = [
        diag[b] if t == 0 else exchange_row(diag[b], t) for b in range(moments) for t in range(groups)
    ]

    def valid(key, a):
        return key[0] * groups + a % groups > key[1]

    found = {}
    own = [by_block(tiles) for tiles in came]
    both = [jnp.concatenate([tiles[b] for tiles in own], axis=1) for b in range(moments)]
    for key in plan.keys:
        for k in range(len(plan.chunks)):
            found[key, key[1], k] = (both[key[0]], plan.starts[k])

    def choose(values, behind):
        distinct = list({id(value): value for value in values.values()}.values())
        number = {id(value): n for n, value in enumerate(distinct)}
        distinct = after(distinct, behind)
        chosen = distinct[0]
        for col, value in values.items():
            if number[id(value)]:
                chosen = jnp.where(z == col, distinct[number[id(value)]], chosen)
        return chosen

    def shift(values, goals, behind):
        goal = lambda a, c, m: (a, goals[c][1], m) if c in goals and valid(goals[c][0], a) else None
        return plan.send(choose(values, behind), goal)

    top, ring, rest = moments - 1, plan.ring(), plan.rest()
    got = [[] for _ in plan.chunks]

    def ring_step(q, number, *behind):
        sends = {col: item for (n, col), item in ring.items() if n == number}
        values = {
            col: own[q][key[0]] if step is None else got[q][step]
            for col, (key, _, step) in sends.items()
        }
        value = shift(values, {col: item[:2] for col, item in sends.items()}, behind)
        got[q].append(value)
        for key, to, _ in sends.values():
            found[key, to, q] = (value, 0)

    def left_step(k):
        value = shift({col: own[k][top] for col in plan.left()}, plan.left(), ())
        for key, to in plan.left().values():
            found[key, to, k] = (value, 0)
        return value

    def rest_step(number, *behind):
        step = rest[number]
        value = shift({col: both[key[0]] for col, (key, _) in step.items()}, step, behind)
        for key, to in step.values():
            for k in range(len(plan.chunks)):
                found[key, to, k] = (value, plan.starts[k])

    lefts = [left_step(k) for k in range(len(plan.chunks))]
    for number in range(cols - 1):
        for k in range(len(plan.chunks)):
            behind = [got[k - 1][number]] if k and number else []
            if number == 1 and k + 1 < len(plan.chunks):
                behind += [came[k + 1], lefts[k]]
            ring_step(k, number, *behind)
    for number in range(len(rest)):
        low = any(key[0] < top for key, _ in rest[number].values())
        rest_step(number, *([got[0][1], got[-1][0], right_all] if low else [got[0][0]]))

    buffers = []

    def number_of(value):
        for index, held in enumerate(buffers):
            if held is value:
                return index
        buffers.append(value)
        return len(buffers) - 1

    sources = {name + (0,): (number_of(value), part) for name, (value, part) in found.items()}
    sig_all = list(buffers)
    for t in range(1, groups):
        for name, (value, part) in found.items():
            sources[name + (t,)] = (len(sig_all) + number_of(value), part)
        sig_all += [exchange_row(value, t) for value in buffers]

    solved = pl.pallas_call(
        functools.partial(solve_kernel, plan, sources),
        out_shape=[jax.ShapeDtypeStruct((side, 2 * width), bf16)] * rows,
        in_specs=[smem()] + [pl.BlockSpec(memory_space=pltpu.VMEM)] * (2 * rows) + hbm(len(sig_all)),
        out_specs=hbm(rows),
        scratch_shapes=[
            pltpu.VMEM((rows, side, 2 * side * (cols - 1)), bf16),
            pltpu.VMEM((rows * 2 * side, 2 * width), bf16),
            dma(moments),
            dma(rows),
        ],
        compiler_params=params,
        name="substitution",
    )(place, *diag_all, *right_all, *sig_all)

    for value, q in late:
        whole.append(value if q is None else exchange_mom(after(value, solved), q))
    sigma = pl.pallas_call(
        functools.partial(place_kernel, plan),
        out_shape=jax.ShapeDtypeStruct(lesser.shape, bf16),
        in_specs=[smem()] + hbm(len(whole)),
        scratch_shapes=[dma(len(whole))],
        compiler_params=params,
        name="place_sigma",
    )(place, *whole)

    back = [solved[0]] + [exchange_row(solved[s], s) for s in range(1, rows)]
    back = after(back, sigma)
    spread = pl.pallas_call(
        functools.partial(spread_kernel, plan),
        out_shape=jax.ShapeDtypeStruct(right_side.shape, bf16),
        in_specs=[smem()] + [pl.BlockSpec(memory_space=pltpu.VMEM)] * rows,
        compiler_params=pltpu.CompilerParams(vmem_limit_bytes=VMEM_BYTES // 2),
        name="place_solution",
    )
    return sigma, spread(place, *back)


def solution(mesh):
    placed = (
        P("mom", None, "row", "col"),
        P("mom", None, "col", "row"),
        P(),
        P("mom", None, "row", None),
        P("mom", "row", None, "col"),
    )
    return jax.shard_map(
        functools.partial(on_device, mesh),
        mesh=mesh,
        in_specs=placed,
        out_specs=(P("mom", None, "row", "col"), P("mom", "row", None, "col")),
        check_vma=False,
    )
```

```python
import functools
import itertools
import math

import jax
import jax.numpy as jnp
from jax import lax
from jax.experimental import pallas as pl
from jax.experimental.pallas import tpu as pltpu
from jax.sharding import PartitionSpec as P

AXES = ("row", "col", "mom")
VMEM_BYTES = 32 * 1024 * 1024


class Plan:
    def __init__(self, mesh, moments, side):
        self.rows = mesh.shape["row"]
        self.cols = mesh.shape["col"]
        self.moms = mesh.shape["mom"]
        self.moments = moments
        self.side = side
        self.groups = self.rows // moments
        self.half = side // self.moms
        self.width = side // self.groups
        self.subs = 2 if self.half % 32 == 0 else 1
        self.sub = self.half // self.subs
        self.chunks = [(q, 0, self.half) for q in range(self.moms)]
        self.starts = [0]
        for _, _, height in self.chunks:
            self.starts.append(self.starts[-1] + height)
        self.keys = [
            (b, j)
            for b in range(moments)
            for j in range(self.cols - 1)
            if (b + 1) * self.groups - 1 > j
        ]

    def send(self, value, target):
        pairs = []
        index = lambda r, c, m: (r * self.cols + c) * self.moms + m
        for place in itertools.product(range(self.rows), range(self.cols), range(self.moms)):
            goal = target(*place)
            if goal is not None:
                pairs.append((index(*place), index(*goal)))
        return lax.ppermute(value, AXES, pairs)

    def ring(self):
        top, last = self.moments - 1, self.cols - 1
        sends, queue = {}, []
        for col in range(last):
            queue = [((top, col), None)] + [(key, n) for n, (key, _) in enumerate(queue)]
            for n, (key, step) in enumerate(queue):
                sends[n, col] = (key, col + 1, step)
        wanted = [
            (key, to)
            for key in self.keys
            if key[0] < top
            for to in range(self.cols)
            if to not in (key[1], last)
        ]
        for key, to in wanted:
            for n in range(1, last):
                if (n, key[1]) in sends or (n, to - 1) in sends and sends[n, to - 1][1] == to:
                    continue
                if to not in [goal for (m, _), (_, goal, _) in sends.items() if m == n]:
                    sends[n, key[1]] = (key, to, None)
                    break
        return sends

    def left(self):
        top = self.moments - 1
        return {col: ((top, col), col - 1) for col in range(1, self.cols - 1)}

    def rest(self):
        done = {(key, to) for key, to, _ in self.ring().values()} | set(self.left().values())
        wanted = [
            (key, to)
            for key in self.keys
            for to in range(self.cols)
            if to != key[1] and (key, to) not in done
        ]
        steps = []
        for key, to in sorted(wanted, key=lambda item: (item[0][0], -item[1], -item[0][1])):
            for step in steps:
                free = key[1] not in step and to not in [goal for _, goal in step.values()]
                if free and all(other[0] == key[0] for other, _ in step.values()):
                    break
            else:
                step = {}
                steps.append(step)
            step[key[1]] = (key, to)
        return steps


def hbm(count):
    return [pl.BlockSpec(memory_space=pltpu.HBM)] * count


def smem():
    return pl.BlockSpec(memory_space=pltpu.SMEM)


def run_copies(copies):
    for copy in copies:
        copy.start()
    for copy in copies:
        copy.wait()


def sigma_kernel(plan, pair_count, u, chunks, place, quads, thirds, *refs):
    moms, moments, groups = plan.moms, plan.moments, plan.groups
    half, sub, side, count = plan.half, plan.sub, plan.side, plan.moms * plan.moments
    refs = list(refs)
    take = lambda number: [refs.pop(0) for _ in range(number)]
    lesser_in, partner_in = take(moms), take(moms)
    before, outs = take(count if u else 0), take(count)
    lesser, partner, pairs, third, held, in_sems, out_sems, before_sems = refs
    x, y = place[0] // groups, place[2]
    height = sub // chunks
    copies = [[] for _ in range(chunks)]
    for chunk in range(chunks):
        rows = pl.ds(chunk * height, height)
        for which, (sources, target) in enumerate(((lesser_in, lesser), (partner_in, partner))):
            for q in range(moms):
                source = sources[q].at[:, :, rows, :]
                if q == 0:
                    start = pl.multiple_of(y * half + u * sub + chunk * height, 16)
                    source = sources[q].at[:, :, pl.ds(start, height), :]
                copy = pltpu.make_async_copy(
                    source,
                    target.at[pl.ds((y ^ q) * moments, moments), :, rows, :],
                    in_sems.at[(chunk * 2 + which) * moms + q],
                )
                copy.start()
                copies[chunk].append(copy)
    earlier = [
        pltpu.make_async_copy(
            before[n], held.at[n, :, pl.ds(0, u * sub), :], before_sems.at[n]
        )
        for n in range(len(before))
    ]
    for copy in earlier:
        copy.start()
    scale = 1.0 / pair_count
    lanes = 128 if side % 128 == 0 else side
    order = [(q, b) for q in reversed(range(moms)) for b in range(moments)]
    sent = []
    for chunk in range(chunks):
        for copy in copies[chunk]:
            copy.wait()

        def block(index, _, chunk=chunk):
            row = chunk * height + index * 16
            rows = pl.ds(pl.multiple_of(row, 16), 16)
            for c in range(count):
                for p in range(2):
                    third[c, p] = partner[c, p, rows, :].astype(jnp.float32)
            n = 0
            for a in range(count):
                for b in range(a + 1):
                    for lane in range(0, side, lanes):
                        cols = pl.ds(lane, lanes)
                        a_re = lesser[a, 0, rows, cols].astype(jnp.float32)
                        a_im = lesser[a, 1, rows, cols].astype(jnp.float32)
                        b_re = lesser[b, 0, rows, cols].astype(jnp.float32)
                        b_im = lesser[b, 1, rows, cols].astype(jnp.float32)
                        pairs[n, 0, :, cols] = a_re * b_re - a_im * b_im
                        pairs[n, 1, :, cols] = a_re * b_im + a_im * b_re
                    n += 1
            for q, b in order:
                moment = (y ^ q) * moments + (x ^ b)
                to = pl.ds(pl.multiple_of(u * sub + row, 16), 16)
                for lane in range(0, side, lanes):
                    cols = pl.ds(lane, lanes)
                    total_re = total_im = None
                    for m in range(pair_count):
                        quad, c = quads[moment, m], thirds[moment, m]
                        p_re, p_im = pairs[quad, 0, :, cols], pairs[quad, 1, :, cols]
                        c_re, c_im = third[c, 0, :, cols], third[c, 1, :, cols]
                        f_re = p_re * c_re - p_im * c_im
                        f_im = p_re * c_im + p_im * c_re
                        total_re = f_re if total_re is None else total_re + f_re
                        total_im = f_im if total_im is None else total_im + f_im
                    held[q * moments + b, 0, to, cols] = (total_re * scale).astype(jnp.bfloat16)
                    held[q * moments + b, 1, to, cols] = (total_im * scale).astype(jnp.bfloat16)
            return 0

        lax.fori_loop(0, height // 16, block, 0)
        for index in range(count):
            rows = pl.ds(u * sub + chunk * height, height)
            copy = pltpu.make_async_copy(
                held.at[index, :, rows, :], outs[index].at[:, rows, :], out_sems.at[chunk * count + index]
            )
            copy.start()
            sent.append(copy)
    for copy in earlier:
        copy.wait()
    for n in range(len(before)):
        rows = pl.ds(0, u * sub)
        copy = pltpu.make_async_copy(
            held.at[n, :, rows, :], outs[n].at[:, rows, :], before_sems.at[n]
        )
        copy.start()
        sent.append(copy)
    for copy in sent:
        copy.wait()


def place_kernel(plan, place, *refs):
    ins, out, sems = refs[:-2], refs[-2], refs[-1]
    x, y = place[0] // plan.groups, place[2]
    copies = []
    for k, (q, first, height) in enumerate(plan.chunks):
        rows = pl.ds(pl.multiple_of((y ^ q) * plan.half + first, 16), height)
        for b in range(plan.moments):
            index = k * plan.moments + b
            copies.append(pltpu.make_async_copy(ins[index], out.at[x ^ b, :, rows, :], sems.at[index]))
    run_copies(copies)


def solve_kernel(plan, sources, place, *refs):
    rows, moms, groups, side = plan.rows, plan.moms, plan.groups, plan.side
    moments, half, width, keys = plan.moments, plan.half, plan.width, plan.keys
    top = moments - 1
    diag, right = refs[:rows], refs[rows : 2 * rows]
    sig_in, outs = refs[2 * rows : -rows - 6], refs[-rows - 6 : -6]
    sig, solved, diag_at, right_at, sems, out_sems = refs[-6:]
    r, y = place[0], place[2]
    g = r % groups
    for key in sorted(keys, key=lambda key: key[0]):
        for col in range(plan.cols):

            @pl.when(place[1] == col)
            def _(key=key, col=col):
                for t in range(groups):
                    row = key[0] * groups + (g ^ t)

                    def start(row=row, t=t):
                        for k, (q, first, height) in enumerate(plan.chunks):
                            index, begin = sources[key, col, k, t]
                            at = pl.ds(pl.multiple_of((y ^ q) * half + first, 16), height)
                            for p in range(2):
                                lane = pl.ds((2 * key[1] + p) * side, side)
                                pltpu.make_async_copy(
                                    sig_in[index].at[p, pl.ds(begin, height), :],
                                    sig.at[row, at, lane],
                                    sems.at[key[0]],
                                ).start()

                    if key[0] * groups > key[1]:
                        start()
                    else:
                        pl.when(row > key[1])(start)

    for s in range(rows):
        right_at[r ^ s] = right[s][...]
    for n in range(rows):
        diag_at[n // groups * groups + (g ^ (n % groups))] = diag[n][...]

    weight = 1.0 / math.sqrt(side * rows)

    def turn(value):
        return jnp.concatenate([-value[:, width:], value[:, :width]], axis=1)

    for row in range(rows):
        if row == max(1, row // groups * groups):
            for key in keys:
                if key[0] == row // groups:
                    for _ in range(2 * sum(key[0] * groups + t > key[1] for t in range(groups))):
                        tile = sig.at[0, :, pl.ds(0, side)]
                        pltpu.make_async_copy(tile, tile, sems.at[key[0]]).wait()
        pending = right_at[row].astype(jnp.float32)
        if row > 0:
            depth = 2 * side * row
            pending = pending + weight * jnp.dot(
                sig[row, :, :depth], solved[:depth, :], preferred_element_type=jnp.float32
            )
        both = jnp.concatenate([pending, turn(pending)], axis=0).astype(jnp.bfloat16)
        value = jnp.dot(
            diag_at[row],
            both,
            preferred_element_type=jnp.float32,
        )
        solved[pl.ds(2 * row * side, side), :] = value.astype(jnp.bfloat16)
        solved[pl.ds((2 * row + 1) * side, side), :] = turn(value).astype(jnp.bfloat16)
        for s in range(rows):

            @pl.when((r ^ s) == row)
            def _(s=s, row=row):
                at = pl.ds(2 * row * side, side)
                pltpu.make_async_copy(solved.at[at, :], outs[s], out_sems.at[s]).start()

    for s in range(rows):
        pltpu.make_async_copy(solved.at[pl.ds(0, side), :], outs[s], out_sems.at[s]).wait()


def after(value, *others):
    return lax.optimization_barrier((value, others))[0]


def pick(held, number):
    value = held[0][...]
    for n in range(1, len(held)):
        value = jnp.where(number == n, held[n][...], value)
    return value


def spread_kernel(plan, place, *refs):
    groups, width = plan.groups, plan.width
    ins, out = refs[:-1], refs[-1]
    for m in range(plan.moments):
        parts = [pick(ins, place[0] ^ (m * groups + g)) for g in range(groups)]
        for p in range(2):
            out[m, :, p, :] = jnp.concatenate(
                [part[:, p * width : (p + 1) * width] for part in parts], axis=1
            )


def on_device(mesh, lesser, greater, triples, diag_inverse, right_side):
    moments, _, side, _ = lesser.shape
    plan = Plan(mesh, moments, side)
    rows, cols, moms, groups = plan.rows, plan.cols, plan.moms, plan.groups
    half, width = plan.half, plan.width
    pair_count = triples.shape[1]
    count = moms * moments
    r, z, y = (lax.axis_index(axis) for axis in AXES)
    x = r // groups
    place = jnp.stack([r, z, y]).astype(jnp.int32)
    bf16, f32 = jnp.bfloat16, jnp.float32
    params = pltpu.CompilerParams(vmem_limit_bytes=VMEM_BYTES)
    dma = lambda *shape: pltpu.SemaphoreType.DMA(shape)

    def exchange_mom(value, q):
        return plan.send(value, lambda a, b, c: (a, b, c ^ q))

    def exchange_row(value, s):
        return plan.send(value, lambda a, b, c: (a ^ s, b, c))

    def by_block(came):
        return [lax.select_n(x ^ b, *came) for b in range(moments)]

    def part_of(value, q, u):
        return lax.dynamic_slice_in_dim(value, (y ^ q) * half + u * plan.sub, plan.sub, 2)

    parts = [part_of(lesser, q, 0) for q in range(1, moms)]
    greater, diag_inverse, right_side = after((greater, diag_inverse, right_side), parts)
    lesser_came = [[exchange_mom(parts[q - 1], q) for q in range(1, moms)]]
    partner = jnp.swapaxes(greater, 2, 3)
    parts = [part_of(partner, q, 0) for q in range(1, moms)]
    diag_inverse, right_side = after((diag_inverse, right_side), parts)
    partner_came = [[exchange_mom(parts[q - 1], q) for q in range(1, moms)]]
    for u in range(1, plan.subs):
        parts = [(part_of(lesser, q, u), part_of(partner, q, u)) for q in range(1, moms)]
        parts = after(parts, lesser_came[-1])
        lesser_came.append([exchange_mom(parts[q - 1][0], q) for q in range(1, moms)])
        partner_came.append([exchange_mom(parts[q - 1][1], q) for q in range(1, moms)])

    mine = [lax.dynamic_index_in_dim(diag_inverse, x ^ b, 0, keepdims=False) for b in range(moments)]
    diag = mine[:1] + [exchange_row(mine[b], b * groups) for b in range(1, moments)]

    right = right_side.reshape(moments, side, 2, groups, width).transpose(0, 3, 1, 2, 4)
    right = right.reshape(rows, side, 2 * width)
    right_all = [lax.dynamic_index_in_dim(right, r ^ s, 0, keepdims=False) for s in range(rows)]
    high = jnp.maximum(triples[..., 0], triples[..., 1])
    low = jnp.minimum(triples[..., 0], triples[..., 1])
    quads, thirds = high * (high + 1) // 2 + low, triples[..., 2]
    copies = 2 if plan.sub % 32 == 0 else 1
    came = []
    whole = []
    so_far = []

    def self_energy(u, *behind):
        height = (u + 1) * plan.sub
        shapes = [(2, height, side)] * count
        return pl.pallas_call(
            functools.partial(sigma_kernel, plan, pair_count, u, copies),
            out_shape=[jax.ShapeDtypeStruct(shape, bf16) for shape in shapes],
            in_specs=[smem()] * 3 + hbm(2 * moms + len(so_far)),
            out_specs=hbm(count),
            scratch_shapes=[
                pltpu.VMEM((count, 2, plan.sub, side), bf16),
                pltpu.VMEM((count, 2, plan.sub, side), bf16),
                pltpu.VMEM((count * (count + 1) // 2, 2, 16, side), f32),
                pltpu.VMEM((count, 2, 16, side), f32),
                pltpu.VMEM((count, 2, height, side), bf16),
                dma(copies * 2 * moms),
                dma(copies * count),
                dma(count),
            ],
            compiler_params=params,
            name="self_energy",
        )(
            *after((place, quads, thirds), behind),
            *([lesser] + lesser_came[u]),
            *([partner] + partner_came[u]),
            *so_far,
        )

    def to_row(value, b, q):
        goal = lambda a, c, m: (a ^ (b * groups), c, m ^ q) if a > c else None
        return plan.send(value, goal)

    for u in range(plan.subs):
        so_far = list(self_energy(u, right_all, diag))
    came.append(so_far[:1] + [to_row(so_far[b], b, 0) for b in range(1, moments)])
    whole += so_far[:moments]
    late = []
    for q in range(1, moms):
        mine = so_far[q * moments : (q + 1) * moments]
        came.append(
            [exchange_mom(mine[0], q)] + [to_row(mine[b], b, q) for b in range(1, moments)]
        )
        late += [(came[-1][0], None)] + [(mine[b], q) for b in range(1, moments)]
    right_all = after(right_all, came[-1])
    right_all = right_all[:1] + [exchange_row(right_all[s], s) for s in range(1, rows)]
    diag = after(by_block(diag), came[-1])
    diag = [jnp.concatenate([value[0], value[1]], axis=1) for value in diag]
    diag_all = [
        diag[b] if t == 0 else exchange_row(diag[b], t) for b in range(moments) for t in range(groups)
    ]

    def valid(key, a):
        return key[0] * groups + a % groups > key[1]

    found = {}
    own = [by_block(tiles) for tiles in came]
    both = [jnp.concatenate([tiles[b] for tiles in own], axis=1) for b in range(moments)]
    for key in plan.keys:
        for k in range(len(plan.chunks)):
            found[key, key[1], k] = (both[key[0]], plan.starts[k])

    def choose(values, behind):
        distinct = list({id(value): value for value in values.values()}.values())
        number = {id(value): n for n, value in enumerate(distinct)}
        distinct = after(distinct, behind)
        chosen = distinct[0]
        for col, value in values.items():
            if number[id(value)]:
                chosen = jnp.where(z == col, distinct[number[id(value)]], chosen)
        return chosen

    def shift(values, goals, behind):
        goal = lambda a, c, m: (a, goals[c][1], m) if c in goals and valid(goals[c][0], a) else None
        return plan.send(choose(values, behind), goal)

    top, ring, rest = moments - 1, plan.ring(), plan.rest()
    got = [[] for _ in plan.chunks]

    def ring_step(q, number, *behind):
        sends = {col: item for (n, col), item in ring.items() if n == number}
        values = {
            col: own[q][key[0]] if step is None else got[q][step]
            for col, (key, _, step) in sends.items()
        }
        value = shift(values, {col: item[:2] for col, item in sends.items()}, behind)
        got[q].append(value)
        for key, to, _ in sends.values():
            found[key, to, q] = (value, 0)

    def left_step(k):
        value = shift({col: own[k][top] for col in plan.left()}, plan.left(), ())
        for key, to in plan.left().values():
            found[key, to, k] = (value, 0)
        return value

    def rest_step(number, *behind):
        step = rest[number]
        value = shift({col: both[key[0]] for col, (key, _) in step.items()}, step, behind)
        for key, to in step.values():
            for k in range(len(plan.chunks)):
                found[key, to, k] = (value, plan.starts[k])

    lefts = [left_step(k) for k in range(len(plan.chunks))]
    for number in range(cols - 1):
        for k in range(len(plan.chunks)):
            behind = [got[k - 1][number]] if k and number else []
            if number == 1 and k + 1 < len(plan.chunks):
                behind += [came[k + 1], lefts[k]]
            ring_step(k, number, *behind)
    for number in range(len(rest)):
        low = any(key[0] < top for key, _ in rest[number].values())
        rest_step(number, *([got[0][1], got[-1][0], right_all] if low else [got[0][0]]))

    buffers = []

    def number_of(value):
        for index, held in enumerate(buffers):
            if held is value:
                return index
        buffers.append(value)
        return len(buffers) - 1

    sources = {name + (0,): (number_of(value), part) for name, (value, part) in found.items()}
    sig_all = list(buffers)
    for t in range(1, groups):
        for name, (value, part) in found.items():
            sources[name + (t,)] = (len(sig_all) + number_of(value), part)
        sig_all += [exchange_row(value, t) for value in buffers]

    lanes = -(-2 * width // 128) * 128
    held = 2 * rows * side * (2 * side * (cols + 1) + 4 * lanes)
    solved = pl.pallas_call(
        functools.partial(solve_kernel, plan, sources),
        out_shape=[jax.ShapeDtypeStruct((side, 2 * width), bf16)] * rows,
        in_specs=[smem()] + [pl.BlockSpec(memory_space=pltpu.VMEM)] * (2 * rows) + hbm(len(sig_all)),
        out_specs=hbm(rows),
        scratch_shapes=[
            pltpu.VMEM((rows, side, 2 * side * (cols - 1)), bf16),
            pltpu.VMEM((rows * 2 * side, 2 * width), bf16),
            pltpu.VMEM((rows, side, 2 * side), bf16),
            pltpu.VMEM((rows, side, 2 * width), bf16),
            dma(moments),
            dma(rows),
        ],
        compiler_params=pltpu.CompilerParams(vmem_limit_bytes=held + 12 * 1024 * 1024),
        name="substitution",
    )(place, *diag_all, *right_all, *sig_all)

    for value, q in late:
        whole.append(value if q is None else exchange_mom(after(value, solved), q))
    sigma = pl.pallas_call(
        functools.partial(place_kernel, plan),
        out_shape=jax.ShapeDtypeStruct(lesser.shape, bf16),
        in_specs=[smem()] + hbm(len(whole)),
        scratch_shapes=[dma(len(whole))],
        compiler_params=params,
        name="place_sigma",
    )(place, *whole)

    back = [solved[0]] + [exchange_row(solved[s], s) for s in range(1, rows)]
    back = after(back, sigma)
    spread = pl.pallas_call(
        functools.partial(spread_kernel, plan),
        out_shape=jax.ShapeDtypeStruct(right_side.shape, bf16),
        in_specs=[smem()] + [pl.BlockSpec(memory_space=pltpu.VMEM)] * rows,
        compiler_params=params,
        name="place_solution",
    )
    return sigma, spread(place, *back)


def solution(mesh):
    placed = (
        P("mom", None, "row", "col"),
        P("mom", None, "col", "row"),
        P(),
        P("mom", None, "row", None),
        P("mom", "row", None, "col"),
    )
    return jax.shard_map(
        functools.partial(on_device, mesh),
        mesh=mesh,
        in_specs=placed,
        out_specs=(P("mom", None, "row", "col"), P("mom", "row", None, "col")),
        check_vma=False,
    )
```

```python
import functools
import itertools
import math

import jax
import jax.numpy as jnp
from jax import lax
from jax.experimental import pallas as pl
from jax.experimental.pallas import tpu as pltpu
from jax.sharding import PartitionSpec as P

AXES = ("row", "col", "mom")
VMEM_BYTES = 32 * 1024 * 1024


class Plan:
    def __init__(self, mesh, moments, side):
        self.rows = mesh.shape["row"]
        self.cols = mesh.shape["col"]
        self.moms = mesh.shape["mom"]
        self.moments = moments
        self.side = side
        self.groups = self.rows // moments
        self.half = side // self.moms
        self.width = side // self.groups
        self.subs = 2 if self.half % 32 == 0 else 1
        self.sub = self.half // self.subs
        self.chunks = [(q, 0, self.half) for q in range(self.moms)]
        self.starts = [0]
        for _, _, height in self.chunks:
            self.starts.append(self.starts[-1] + height)
        self.keys = [
            (b, j)
            for b in range(moments)
            for j in range(self.cols - 1)
            if (b + 1) * self.groups - 1 > j
        ]

    def send(self, value, target):
        pairs = []
        index = lambda r, c, m: (r * self.cols + c) * self.moms + m
        for place in itertools.product(range(self.rows), range(self.cols), range(self.moms)):
            goal = target(*place)
            if goal is not None:
                pairs.append((index(*place), index(*goal)))
        return lax.ppermute(value, AXES, pairs)

    def ring(self):
        top, last = self.moments - 1, self.cols - 1
        sends, queue = {}, []
        for col in range(last):
            queue = [((top, col), None)] + [(key, n) for n, (key, _) in enumerate(queue)]
            for n, (key, step) in enumerate(queue):
                sends[n, col] = (key, col + 1, step)
        wanted = [
            (key, to)
            for key in self.keys
            if key[0] < top
            for to in range(self.cols)
            if to not in (key[1], last)
        ]
        for key, to in wanted:
            for n in range(1, last):
                if (n, key[1]) in sends or (n, to - 1) in sends and sends[n, to - 1][1] == to:
                    continue
                if to not in [goal for (m, _), (_, goal, _) in sends.items() if m == n]:
                    sends[n, key[1]] = (key, to, None)
                    break
        return sends

    def left(self):
        top = self.moments - 1
        return {col: ((top, col), col - 1) for col in range(1, self.cols - 1)}

    def rest(self):
        done = {(key, to) for key, to, _ in self.ring().values()} | set(self.left().values())
        wanted = [
            (key, to)
            for key in self.keys
            for to in range(self.cols)
            if to != key[1] and (key, to) not in done
        ]
        steps = []
        for key, to in sorted(wanted, key=lambda item: (item[0][0], -item[1], -item[0][1])):
            for step in steps:
                free = key[1] not in step and to not in [goal for _, goal in step.values()]
                if free and all(other[0] == key[0] for other, _ in step.values()):
                    break
            else:
                step = {}
                steps.append(step)
            step[key[1]] = (key, to)
        return steps


def hbm(count):
    return [pl.BlockSpec(memory_space=pltpu.HBM)] * count


def smem():
    return pl.BlockSpec(memory_space=pltpu.SMEM)


def run_copies(copies):
    for copy in copies:
        copy.start()
    for copy in copies:
        copy.wait()


def sigma_kernel(plan, pair_count, u, chunks, place, quads, thirds, *refs):
    moms, moments, groups = plan.moms, plan.moments, plan.groups
    half, sub, side, count = plan.half, plan.sub, plan.side, plan.moms * plan.moments
    refs = list(refs)
    take = lambda number: [refs.pop(0) for _ in range(number)]
    lesser_in, partner_in = take(moms), take(moms)
    before, outs = take(count if u else 0), take(count)
    lesser, partner, pairs, third, held, in_sems, out_sems, before_sems = refs
    x, y = place[0] // groups, place[2]
    height = sub // chunks
    copies = [[] for _ in range(chunks)]
    for chunk in range(chunks):
        rows = pl.ds(chunk * height, height)
        for which, (sources, target) in enumerate(((lesser_in, lesser), (partner_in, partner))):
            for q in range(moms):
                source = sources[q].at[:, :, rows, :]
                if q == 0:
                    start = pl.multiple_of(y * half + u * sub + chunk * height, 16)
                    source = sources[q].at[:, :, pl.ds(start, height), :]
                copy = pltpu.make_async_copy(
                    source,
                    target.at[pl.ds((y ^ q) * moments, moments), :, rows, :],
                    in_sems.at[(chunk * 2 + which) * moms + q],
                )
                copy.start()
                copies[chunk].append(copy)
    earlier = [
        pltpu.make_async_copy(
            before[n], held.at[n, :, pl.ds(0, u * sub), :], before_sems.at[n]
        )
        for n in range(len(before))
    ]
    for copy in earlier:
        copy.start()
    scale = 1.0 / pair_count
    lanes = 128 if side % 128 == 0 else side
    order = [(q, b) for q in reversed(range(moms)) for b in range(moments)]
    sent = []
    for chunk in range(chunks):
        for copy in copies[chunk]:
            copy.wait()

        def block(index, _, chunk=chunk):
            row = chunk * height + index * 16
            rows = pl.ds(pl.multiple_of(row, 16), 16)
            for c in range(count):
                for p in range(2):
                    third[c, p] = partner[c, p, rows, :].astype(jnp.float32)
            n = 0
            for a in range(count):
                for b in range(a + 1):
                    for lane in range(0, side, lanes):
                        cols = pl.ds(lane, lanes)
                        a_re = lesser[a, 0, rows, cols].astype(jnp.float32)
                        a_im = lesser[a, 1, rows, cols].astype(jnp.float32)
                        b_re = lesser[b, 0, rows, cols].astype(jnp.float32)
                        b_im = lesser[b, 1, rows, cols].astype(jnp.float32)
                        pairs[n, 0, :, cols] = a_re * b_re - a_im * b_im
                        pairs[n, 1, :, cols] = a_re * b_im + a_im * b_re
                    n += 1
            for q, b in order:
                moment = (y ^ q) * moments + (x ^ b)
                to = pl.ds(pl.multiple_of(u * sub + row, 16), 16)
                for lane in range(0, side, lanes):
                    cols = pl.ds(lane, lanes)
                    total_re = total_im = None
                    for m in range(pair_count):
                        quad, c = quads[moment, m], thirds[moment, m]
                        p_re, p_im = pairs[quad, 0, :, cols], pairs[quad, 1, :, cols]
                        c_re, c_im = third[c, 0, :, cols], third[c, 1, :, cols]
                        f_re = p_re * c_re - p_im * c_im
                        f_im = p_re * c_im + p_im * c_re
                        total_re = f_re if total_re is None else total_re + f_re
                        total_im = f_im if total_im is None else total_im + f_im
                    held[q * moments + b, 0, to, cols] = (total_re * scale).astype(jnp.bfloat16)
                    held[q * moments + b, 1, to, cols] = (total_im * scale).astype(jnp.bfloat16)
            return 0

        lax.fori_loop(0, height // 16, block, 0)
        for index in range(count):
            rows = pl.ds(u * sub + chunk * height, height)
            copy = pltpu.make_async_copy(
                held.at[index, :, rows, :], outs[index].at[:, rows, :], out_sems.at[chunk * count + index]
            )
            copy.start()
            sent.append(copy)
    for copy in earlier:
        copy.wait()
    for n in range(len(before)):
        rows = pl.ds(0, u * sub)
        copy = pltpu.make_async_copy(
            held.at[n, :, rows, :], outs[n].at[:, rows, :], before_sems.at[n]
        )
        copy.start()
        sent.append(copy)
    for copy in sent:
        copy.wait()


def place_kernel(plan, place, *refs):
    ins, out, sems = refs[:-2], refs[-2], refs[-1]
    x, y = place[0] // plan.groups, place[2]
    copies = []
    for k, (q, first, height) in enumerate(plan.chunks):
        rows = pl.ds(pl.multiple_of((y ^ q) * plan.half + first, 16), height)
        for b in range(plan.moments):
            index = k * plan.moments + b
            copies.append(pltpu.make_async_copy(ins[index], out.at[x ^ b, :, rows, :], sems.at[index]))
    run_copies(copies)


def solve_kernel(plan, sources, place, *refs):
    rows, moms, groups, side = plan.rows, plan.moms, plan.groups, plan.side
    moments, half, width, keys = plan.moments, plan.half, plan.width, plan.keys
    top = moments - 1
    diag, right = refs[:rows], refs[rows : 2 * rows]
    sig_in, outs = refs[2 * rows : -rows - 6], refs[-rows - 6 : -6]
    sig, solved, diag_at, right_at, sems, out_sems = refs[-6:]
    r, y = place[0], place[2]
    g = r % groups
    for key in sorted(keys, key=lambda key: key[0]):
        for col in range(plan.cols):

            @pl.when(place[1] == col)
            def _(key=key, col=col):
                for t in range(groups):
                    row = key[0] * groups + (g ^ t)

                    def start(row=row, t=t):
                        for k, (q, first, height) in enumerate(plan.chunks):
                            index, begin = sources[key, col, k, t]
                            at = pl.ds(pl.multiple_of((y ^ q) * half + first, 16), height)
                            for p in range(2):
                                lane = pl.ds((2 * key[1] + p) * side, side)
                                pltpu.make_async_copy(
                                    sig_in[index].at[p, pl.ds(begin, height), :],
                                    sig.at[row, at, lane],
                                    sems.at[key[0]],
                                ).start()

                    if key[0] * groups > key[1]:
                        start()
                    else:
                        pl.when(row > key[1])(start)

    for s in range(rows):
        right_at[r ^ s] = right[s][...]
    for n in range(rows):
        diag_at[n // groups * groups + (g ^ (n % groups))] = diag[n][...]

    weight = 1.0 / math.sqrt(side * rows)

    def turn(value):
        return jnp.concatenate([-value[:, width:], value[:, :width]], axis=1)

    for row in range(rows):
        if row == max(1, row // groups * groups):
            for key in keys:
                if key[0] == row // groups:
                    for _ in range(2 * sum(key[0] * groups + t > key[1] for t in range(groups))):
                        tile = sig.at[0, :, pl.ds(0, side)]
                        pltpu.make_async_copy(tile, tile, sems.at[key[0]]).wait()
        pending = right_at[row].astype(jnp.float32)
        if row > 0:
            depth = 2 * side * row
            pending = pending + weight * jnp.dot(
                sig[row, :, :depth], solved[:depth, :], preferred_element_type=jnp.float32
            )
        both = jnp.concatenate([pending, turn(pending)], axis=0).astype(jnp.bfloat16)
        value = jnp.dot(
            diag_at[row],
            both,
            preferred_element_type=jnp.float32,
        )
        solved[pl.ds(2 * row * side, side), :] = value.astype(jnp.bfloat16)
        solved[pl.ds((2 * row + 1) * side, side), :] = turn(value).astype(jnp.bfloat16)
        for s in range(rows):

            @pl.when((r ^ s) == row)
            def _(s=s, row=row):
                at = pl.ds(2 * row * side, side)
                pltpu.make_async_copy(solved.at[at, :], outs[s], out_sems.at[s]).start()

    for s in range(rows):
        pltpu.make_async_copy(solved.at[pl.ds(0, side), :], outs[s], out_sems.at[s]).wait()


def after(value, *others):
    return lax.optimization_barrier((value, others))[0]


def pick(held, number):
    value = held[0][...]
    for n in range(1, len(held)):
        value = jnp.where(number == n, held[n][...], value)
    return value


def spread_kernel(plan, block, place, *refs):
    groups, width = plan.groups, plan.width
    ins, out, held, sem = refs[:groups], refs[-3], refs[-2], refs[-1]
    parts = [pick(ins, (place[0] % groups) ^ g) for g in range(groups)]
    for p in range(2):
        held[:, p, :] = jnp.concatenate(
            [part[:, p * width : (p + 1) * width] for part in parts], axis=1
        )
    run_copies([pltpu.make_async_copy(held, out.at[(place[0] // groups) ^ block], sem.at[0])])


def on_device(mesh, lesser, greater, triples, diag_inverse, right_side):
    moments, _, side, _ = lesser.shape
    plan = Plan(mesh, moments, side)
    rows, cols, moms, groups = plan.rows, plan.cols, plan.moms, plan.groups
    half, width = plan.half, plan.width
    pair_count = triples.shape[1]
    count = moms * moments
    r, z, y = (lax.axis_index(axis) for axis in AXES)
    x = r // groups
    place = jnp.stack([r, z, y]).astype(jnp.int32)
    bf16, f32 = jnp.bfloat16, jnp.float32
    params = pltpu.CompilerParams(vmem_limit_bytes=VMEM_BYTES)
    dma = lambda *shape: pltpu.SemaphoreType.DMA(shape)

    def exchange_mom(value, q):
        return plan.send(value, lambda a, b, c: (a, b, c ^ q))

    def exchange_row(value, s):
        return plan.send(value, lambda a, b, c: (a ^ s, b, c))

    def by_block(came):
        return [lax.select_n(x ^ b, *came) for b in range(moments)]

    def part_of(value, q, u):
        return lax.dynamic_slice_in_dim(value, (y ^ q) * half + u * plan.sub, plan.sub, 2)

    parts = [part_of(lesser, q, 0) for q in range(1, moms)]
    greater, diag_inverse, right_side = after((greater, diag_inverse, right_side), parts)
    lesser_came = [[exchange_mom(parts[q - 1], q) for q in range(1, moms)]]
    partner = jnp.swapaxes(greater, 2, 3)
    parts = [part_of(partner, q, 0) for q in range(1, moms)]
    diag_inverse, right_side = after((diag_inverse, right_side), parts)
    partner_came = [[exchange_mom(parts[q - 1], q) for q in range(1, moms)]]
    for u in range(1, plan.subs):
        parts = [(part_of(lesser, q, u), part_of(partner, q, u)) for q in range(1, moms)]
        parts = after(parts, lesser_came[-1])
        lesser_came.append([exchange_mom(parts[q - 1][0], q) for q in range(1, moms)])
        partner_came.append([exchange_mom(parts[q - 1][1], q) for q in range(1, moms)])

    mine = [lax.dynamic_index_in_dim(diag_inverse, x ^ b, 0, keepdims=False) for b in range(moments)]
    diag = mine[:1] + [exchange_row(mine[b], b * groups) for b in range(1, moments)]

    right = right_side.reshape(moments, side, 2, groups, width).transpose(0, 3, 1, 2, 4)
    right = right.reshape(rows, side, 2 * width)
    right_all = [lax.dynamic_index_in_dim(right, r ^ s, 0, keepdims=False) for s in range(rows)]
    high = jnp.maximum(triples[..., 0], triples[..., 1])
    low = jnp.minimum(triples[..., 0], triples[..., 1])
    quads, thirds = high * (high + 1) // 2 + low, triples[..., 2]
    copies = 2 if plan.sub % 32 == 0 else 1
    came = []
    whole = []
    so_far = []

    def self_energy(u, *behind):
        height = (u + 1) * plan.sub
        shapes = [(2, height, side)] * count
        return pl.pallas_call(
            functools.partial(sigma_kernel, plan, pair_count, u, copies),
            out_shape=[jax.ShapeDtypeStruct(shape, bf16) for shape in shapes],
            in_specs=[smem()] * 3 + hbm(2 * moms + len(so_far)),
            out_specs=hbm(count),
            scratch_shapes=[
                pltpu.VMEM((count, 2, plan.sub, side), bf16),
                pltpu.VMEM((count, 2, plan.sub, side), bf16),
                pltpu.VMEM((count * (count + 1) // 2, 2, 16, side), f32),
                pltpu.VMEM((count, 2, 16, side), f32),
                pltpu.VMEM((count, 2, height, side), bf16),
                dma(copies * 2 * moms),
                dma(copies * count),
                dma(count),
            ],
            compiler_params=params,
            name="self_energy",
        )(
            *after((place, quads, thirds), behind),
            *([lesser] + lesser_came[u]),
            *([partner] + partner_came[u]),
            *so_far,
        )

    def to_row(value, b, q):
        goal = lambda a, c, m: (a ^ (b * groups), c, m ^ q) if a > c else None
        return plan.send(value, goal)

    for u in range(plan.subs):
        so_far = list(self_energy(u, right_all, diag))
    came.append(so_far[:1] + [to_row(so_far[b], b, 0) for b in range(1, moments)])
    whole += so_far[:moments]
    late = []
    for q in range(1, moms):
        mine = so_far[q * moments : (q + 1) * moments]
        came.append(
            [exchange_mom(mine[0], q)] + [to_row(mine[b], b, q) for b in range(1, moments)]
        )
        late += [(came[-1][0], None)] + [(mine[b], q) for b in range(1, moments)]
    right_all = after(right_all, came[-1])
    right_all = right_all[:1] + [exchange_row(right_all[s], s) for s in range(1, rows)]
    diag = after(by_block(diag), came[-1])
    diag = [jnp.concatenate([value[0], value[1]], axis=1) for value in diag]
    diag_all = [
        diag[b] if t == 0 else exchange_row(diag[b], t) for b in range(moments) for t in range(groups)
    ]

    def valid(key, a):
        return key[0] * groups + a % groups > key[1]

    found = {}
    own = [by_block(tiles) for tiles in came]
    both = [jnp.concatenate([tiles[b] for tiles in own], axis=1) for b in range(moments)]
    for key in plan.keys:
        for k in range(len(plan.chunks)):
            found[key, key[1], k] = (both[key[0]], plan.starts[k])

    def choose(values, behind):
        distinct = list({id(value): value for value in values.values()}.values())
        number = {id(value): n for n, value in enumerate(distinct)}
        distinct = after(distinct, behind)
        chosen = distinct[0]
        for col, value in values.items():
            if number[id(value)]:
                chosen = jnp.where(z == col, distinct[number[id(value)]], chosen)
        return chosen

    def shift(values, goals, behind):
        goal = lambda a, c, m: (a, goals[c][1], m) if c in goals and valid(goals[c][0], a) else None
        return plan.send(choose(values, behind), goal)

    top, ring, rest = moments - 1, plan.ring(), plan.rest()
    got = [[] for _ in plan.chunks]

    def ring_step(q, number, *behind):
        sends = {col: item for (n, col), item in ring.items() if n == number}
        values = {
            col: own[q][key[0]] if step is None else got[q][step]
            for col, (key, _, step) in sends.items()
        }
        value = shift(values, {col: item[:2] for col, item in sends.items()}, behind)
        got[q].append(value)
        for key, to, _ in sends.values():
            found[key, to, q] = (value, 0)

    def left_step(k):
        value = shift({col: own[k][top] for col in plan.left()}, plan.left(), ())
        for key, to in plan.left().values():
            found[key, to, k] = (value, 0)
        return value

    def rest_step(number, *behind):
        step = rest[number]
        value = shift({col: both[key[0]] for col, (key, _) in step.items()}, step, behind)
        for key, to in step.values():
            for k in range(len(plan.chunks)):
                found[key, to, k] = (value, plan.starts[k])

    lefts = [left_step(k) for k in range(len(plan.chunks))]
    for number in range(cols - 1):
        for k in range(len(plan.chunks)):
            behind = [got[k - 1][number]] if k and number else []
            if number == 1 and k + 1 < len(plan.chunks):
                behind += [came[k + 1], lefts[k]]
            ring_step(k, number, *behind)
    for number in range(len(rest)):
        low = any(key[0] < top for key, _ in rest[number].values())
        rest_step(number, *([got[0][1], got[-1][0], right_all] if low else [got[0][0]]))

    buffers = []

    def number_of(value):
        for index, held in enumerate(buffers):
            if held is value:
                return index
        buffers.append(value)
        return len(buffers) - 1

    sources = {name + (0,): (number_of(value), part) for name, (value, part) in found.items()}
    sig_all = list(buffers)
    for t in range(1, groups):
        for name, (value, part) in found.items():
            sources[name + (t,)] = (len(sig_all) + number_of(value), part)
        sig_all += [exchange_row(value, t) for value in buffers]

    lanes = -(-2 * width // 128) * 128
    held = 2 * rows * side * (2 * side * (cols + 1) + 4 * lanes)
    solved = pl.pallas_call(
        functools.partial(solve_kernel, plan, sources),
        out_shape=[jax.ShapeDtypeStruct((side, 2 * width), bf16)] * rows,
        in_specs=[smem()] + [pl.BlockSpec(memory_space=pltpu.VMEM)] * (2 * rows) + hbm(len(sig_all)),
        out_specs=hbm(rows),
        scratch_shapes=[
            pltpu.VMEM((rows, side, 2 * side * (cols - 1)), bf16),
            pltpu.VMEM((rows * 2 * side, 2 * width), bf16),
            pltpu.VMEM((rows, side, 2 * side), bf16),
            pltpu.VMEM((rows, side, 2 * width), bf16),
            dma(moments),
            dma(rows),
        ],
        compiler_params=pltpu.CompilerParams(vmem_limit_bytes=held + 12 * 1024 * 1024),
        name="substitution",
    )(place, *diag_all, *right_all, *sig_all)

    for value, q in late:
        whole.append(value if q is None else exchange_mom(after(value, solved), q))
    sigma = pl.pallas_call(
        functools.partial(place_kernel, plan),
        out_shape=jax.ShapeDtypeStruct(lesser.shape, bf16),
        in_specs=[smem()] + hbm(len(whole)),
        scratch_shapes=[dma(len(whole))],
        compiler_params=params,
        name="place_sigma",
    )(place, *whole)

    back = [solved[0]] + [exchange_row(solved[s], s) for s in range(1, rows)]
    spread = None
    for block in range(moments):
        pieces = back[block * groups : (block + 1) * groups]
        before = []
        if block:
            pieces = after(pieces, spread, sigma)
            before = [spread]
        spread = pl.pallas_call(
            functools.partial(spread_kernel, plan, block),
            out_shape=jax.ShapeDtypeStruct(right_side.shape, bf16),
            in_specs=[smem()]
            + [pl.BlockSpec(memory_space=pltpu.VMEM)] * groups
            + hbm(len(before)),
            out_specs=hbm(1)[0],
            scratch_shapes=[pltpu.VMEM((side, 2, side), bf16), dma(1)],
            input_output_aliases={1 + groups: 0} if block else {},
            compiler_params=params,
            name="place_solution",
        )(place, *pieces, *before)
    return sigma, spread


def solution(mesh):
    placed = (
        P("mom", None, "row", "col"),
        P("mom", None, "col", "row"),
        P(),
        P("mom", None, "row", None),
        P("mom", "row", None, "col"),
    )
    return jax.shard_map(
        functools.partial(on_device, mesh),
        mesh=mesh,
        in_specs=placed,
        out_specs=(P("mom", None, "row", "col"), P("mom", "row", None, "col")),
        check_vma=False,
    )
```
